32 devices in a mesh: band: 16 (over z, x, core), fft: 2 (over y).
Axes of the slice: x: 2, y: 2, z: 4, core: 2. Of those that a mesh axis runs over, the one named last changes fastest.
Arguments:
- orbitals: float32 [32, 64, 4096], P('band', 'fft'), may hold values from -5 to 5
Outputs:
- exchange: float32 [32, 64, 4096], P('band', 'fft')
The draws below stay inside these ranges and needn't reach their ends.
All inputs are finite; a program needn't handle non-finite values.
Results may differ from the reference program's by a relative error of at most 0.00018.
Values sent between devices are 32-bit elements; how exact they have to be, the bound alone decides.
A program may use at most 64 MiB of HBM per device.

```python
import math
import jax
import jax.numpy as jnp
from jax import lax

GRID = 64
ORB_DEV = 2
ROUNDS = 2
NORB = 32


def draw_orbitals(key, part):
    rough_key = jax.random.fold_in(key, 0)
    shape = (NORB, GRID, GRID * GRID)
    rough = jax.random.normal(rough_key, shape, jnp.float32)
    return jnp.clip(rough, -5.0, 5.0)


def setup_inputs(seed: int = 0) -> dict:
    arg_keys = jax.random.split(jax.random.key(seed), 2)
    return {
        "orbitals": draw_orbitals(jax.random.fold_in(arg_keys[1], 71), 0),
    }


EXX_FRACTION = 0.25
SCREEN = 0.05


def kernel_table(length):
    indices = jnp.arange(length, dtype=jnp.int32)
    signed = jnp.where(indices < length // 2, indices, indices - length).astype(jnp.float32)
    wavenum = signed * (2.0 * math.pi / length)
    squares = wavenum[:, None, None] ** 2 + wavenum[None, :, None] ** 2 + wavenum[None, None, :] ** 2
    guarded = jnp.where(squares > 0, squares, 1.0)
    return jnp.where(squares > 0, (1.0 - jnp.exp(-guarded / (4.0 * SCREEN * SCREEN))) / guarded, 0.0)


def reference(orbitals):
    fields = orbitals.reshape(NORB, GRID, GRID, GRID)
    sources = fields[: ROUNDS * ORB_DEV]
    kernel = kernel_table(GRID)

    def apply_one(orbital):
        density = orbital[None] * sources
        spectrum = jnp.fft.fftn(density, axes=(1, 2, 3))
        potential = jnp.real(jnp.fft.ifftn(spectrum * kernel, axes=(1, 2, 3)))
        return -EXX_FRACTION * jnp.sum(sources * potential, axis=0)

    result = lax.map(apply_one, fields)
    return result.reshape(NORB, GRID, GRID * GRID)
```

```python
import functools
import math

import jax
import jax.numpy as jnp
import numpy as np
from jax import lax
from jax.experimental import pallas as pl
from jax.experimental.pallas import tpu as pltpu
from jax.sharding import PartitionSpec as P

GRID = 64
ROUNDS = 2
EXX_FRACTION = 0.25
SCREEN = 0.05
MESH = pl.DeviceIdType.MESH
MIB = 1024 * 1024


def real_modes(length):
    n = np.arange(length)
    rows = [np.cos(2 * np.pi * q * n / length) for q in range(length // 2 + 1)]
    rows += [np.sin(2 * np.pi * q * n / length) for q in range(1, length // 2)]
    matrix = np.array(rows)
    return matrix / np.sqrt((matrix**2).sum(1, keepdims=True))


def split(matrix):
    high = matrix.astype(jnp.bfloat16)
    return high, (matrix - high.astype(np.float64)).astype(jnp.bfloat16)


def matrices():
    modes = real_modes(GRID)
    z_forward = np.kron(np.array([[1.0, 1.0], [1.0, -1.0]]) / np.sqrt(2.0), modes.T)
    out = []
    for matrix in (z_forward, z_forward.T):
        high, low = split(matrix)
        out += [np.concatenate([high, high], 0), low]
    for matrix in (modes, modes.T):
        high, low = split(matrix)
        out.append(np.concatenate([high, high, low], 1))
    return out


def mode_numbers():
    half = GRID // 2
    return np.concatenate([np.arange(half + 1), np.arange(1, half)])


def filter_table():
    k = jnp.asarray(mode_numbers(), jnp.float32)
    quarter = GRID // 4
    q = np.concatenate([np.arange(quarter + 1), np.arange(1, quarter)])
    weight = np.where((q == 0) | (q == quarter), 1.0, 2.0) / (GRID // 2)
    ky = jnp.asarray(np.stack([q, GRID // 2 - q], 1), jnp.float32)
    unit = 2.0 * math.pi / GRID
    squares = (
        (k * unit)[:, None, None, None] ** 2
        + (ky * unit)[None, :, :, None] ** 2
        + (k * unit)[None, None, None, :] ** 2
    )
    guarded = jnp.where(squares > 0, squares, 1.0)
    table = jnp.where(
        squares > 0, (1.0 - jnp.exp(-guarded / (4.0 * SCREEN * SCREEN))) / guarded, 0.0
    )
    table = table * jnp.asarray(weight, jnp.float32)[None, :, None, None]
    return table.reshape(GRID, GRID * GRID)


def rotate(c, s, cos, sin):
    return cos * c - sin * s, sin * c + cos * s


def forward(x):
    n = len(x)
    if n == 2:
        return [x[0] + x[1], x[0] - x[1]], {}
    ce, se = forward(x[0::2])
    co, so = forward(x[1::2])
    half, quarter = n // 2, n // 4
    c, s = [None] * (half + 1), {}
    c[0], c[half] = ce[0] + co[0], ce[0] - co[0]
    c[quarter], s[quarter] = ce[quarter], co[quarter]
    for q in range(1, quarter):
        if 8 * q == n:
            r = math.sqrt(0.5)
            a, b = (co[q] - so[q]) * r, (co[q] + so[q]) * r
        else:
            a, b = rotate(co[q], so[q], math.cos(2 * math.pi * q / n), math.sin(2 * math.pi * q / n))
        c[q], c[half - q] = ce[q] + a, ce[q] - a
        s[q], s[half - q] = b + se[q], b - se[q]
    return c, s


def backward(c, s):
    n = 2 * (len(c) - 1)
    if n == 2:
        return [c[0] + c[1], c[0] - c[1]]
    half, quarter = n // 2, n // 4
    ce, co, se, so = [None] * (quarter + 1), [None] * (quarter + 1), {}, {}
    ce[0], co[0] = c[0] + c[half], c[0] - c[half]
    ce[quarter], co[quarter] = c[quarter], s[quarter]
    for q in range(1, quarter):
        ce[q], a = c[q] + c[half - q], c[q] - c[half - q]
        b, se[q] = s[q] + s[half - q], s[q] - s[half - q]
        if 8 * q == n:
            r = math.sqrt(0.5)
            co[q], so[q] = (a + b) * r, (b - a) * r
        else:
            co[q], so[q] = rotate(a, b, math.cos(2 * math.pi * q / n), -math.sin(2 * math.pi * q / n))
    out = [None] * n
    out[0::2], out[1::2] = backward(ce, se), backward(co, so)
    return out


def twiddles(shape, q):
    odd = lax.broadcasted_iota(jnp.int32, shape, 1) >= shape[1] // 2
    angle = 2 * math.pi * q / GRID
    return jnp.where(odd, math.cos(angle), 1.0), jnp.where(odd, math.sin(angle), 0.0)


def halves(value):
    high = value.astype(jnp.bfloat16)
    return high, (value - high.astype(jnp.float32)).astype(jnp.bfloat16)


def along_z(tiles, double, low):
    rows = jnp.concatenate(tiles, 0)
    high, rest = halves(rows)
    out = jnp.dot(jnp.concatenate([high, rest], 1), double, preferred_element_type=jnp.float32)
    out = out + jnp.dot(high, low, preferred_element_type=jnp.float32)
    step = tiles[0].shape[0]
    return [out[i * step : (i + 1) * step] for i in range(len(tiles))]


def along_x(value, triple):
    high, rest = halves(value)
    stacked = jnp.concatenate([high, rest, high], 0)
    return jnp.dot(triple, stacked, preferred_element_type=jnp.float32)


LANES = 128
PART = 512


def exchange_kernel(
    orbital_ref, source_ref, filter_ref, zf2_ref, zfl_ref, zb2_ref, zbl_ref, xf_ref, xb_ref, out_ref, work
):
    length, cells = work.shape
    count = cells // LANES
    quarter = count // 2
    shape = (8, LANES)

    @pl.loop(0, length // 8)
    def _(block):
        rows = pl.ds(pl.multiple_of(block * 8, 8), 8)
        cells_in = [
            orbital_ref[rows, i * LANES : (i + 1) * LANES]
            * source_ref[0, rows, i * LANES : (i + 1) * LANES]
            for i in range(count)
        ]
        c, s = forward(cells_in)
        for q in range(1, quarter):
            cos, sin = twiddles(shape, q)
            c[q], s[q] = rotate(c[q], s[q], cos, sin)
        for i, value in enumerate(c + [s[q] for q in range(1, quarter)]):
            work[rows, i * LANES : (i + 1) * LANES] = value

    for part in range(cells // PART):
        base = part * PART
        tiles = [work[:, base + i : base + i + LANES] for i in range(0, PART, LANES)]
        tiles = along_z(tiles, zf2_ref[...], zfl_ref[...])
        value = along_x(jnp.concatenate(tiles, 1), xf_ref[...])
        value = along_x(value * filter_ref[:, base : base + PART], xb_ref[...])
        tiles = [value[:, i : i + LANES] for i in range(0, PART, LANES)]
        tiles = along_z(tiles, zb2_ref[...], zbl_ref[...])
        for i, tile in enumerate(tiles):
            work[:, base + i * LANES : base + (i + 1) * LANES] = tile

    first = pl.program_id(0) == 0

    @pl.loop(0, length // 8)
    def _(block):
        rows = pl.ds(pl.multiple_of(block * 8, 8), 8)
        values = [work[rows, i * LANES : (i + 1) * LANES] for i in range(count)]
        c, s = values[: quarter + 1], dict(enumerate(values[quarter + 1 :], 1))
        for q in range(1, quarter):
            cos, sin = twiddles(shape, q)
            c[q], s[q] = rotate(c[q], s[q], cos, -sin)
        for i, value in enumerate(backward(c, s)):
            lanes = slice(i * LANES, (i + 1) * LANES)
            term = value * source_ref[0, rows, lanes] * -EXX_FRACTION
            out_ref[rows, lanes] = jnp.where(first, 0.0, out_ref[rows, lanes]) + term


def apply_exchange(orbital, sources):
    count, length, cells = sources.shape
    constants = [jnp.asarray(m) for m in matrices()]
    whole = lambda shape: pl.BlockSpec(shape, lambda j: (0, 0))
    return pl.pallas_call(
        exchange_kernel,
        grid=(count,),
        out_shape=jax.ShapeDtypeStruct((length, cells), jnp.float32),
        in_specs=[
            whole((length, cells)),
            pl.BlockSpec((1, length, cells), lambda j: (j, 0, 0)),
            whole((length, cells)),
        ]
        + [whole(m.shape) for m in constants],
        out_specs=whole((length, cells)),
        scratch_shapes=[pltpu.VMEM((length, cells), jnp.float32)],
        compiler_params=pltpu.CompilerParams(vmem_limit_bytes=32 * MIB),
        name="exchange",
    )(orbital, sources, filter_table(), *constants)


GROUP = 8


def gather_kernel(chips, row, x_ref, s_ref, p_ref, copy_sem, swap_send, swap_recv, z_send, x_send, tree_recv,
                  y_send, y_recv, c_send, c_recv):
    band, half = lax.axis_index("band"), lax.axis_index("fft")
    chip, core = band // 2, band % 2
    owned, planes, _ = x_ref.shape
    other_half, other_band = 1 - half, chip * 2 + 1 - core
    up, side, parent = band + 2 * row, band + 2, lax.select(chip < row, band - 2 * chip, band - 2 * row)
    root, inner = chip == 0, chip < row
    has_up = chip + row < chips
    to_y = {"band": band, "fft": other_half}
    to_core = {"band": other_band, "fft": half}

    barrier = pltpu.get_barrier_semaphore()

    def greet(target):
        pl.semaphore_signal(barrier, inc=1, device_id=target, device_id_type=MESH)

    greet(to_y)
    greet(to_core)

    @pl.when(has_up)
    def _():
        greet({"band": up, "fft": half})

    @pl.when(root)
    def _():
        greet({"band": side, "fft": half})

    @pl.when(jnp.logical_not(root))
    def _():
        greet({"band": parent, "fft": half})

    pl.semaphore_wait(barrier, 3 + has_up.astype(jnp.int32))

    def remote(src, dst, send, recv, target):
        return pltpu.make_async_remote_copy(
            src_ref=src, dst_ref=dst, send_sem=send, recv_sem=recv, device_id=target, device_id_type=MESH
        )

    swap = remote(x_ref.at[other_half], p_ref.at[half], swap_send, swap_recv, to_y)
    swap.start()
    keep = pltpu.make_async_copy(x_ref.at[half], p_ref.at[half], copy_sem.at[0])
    keep.start()
    own = pltpu.make_async_copy(x_ref, s_ref.at[core, :, half], copy_sem.at[1])

    @pl.when(root)
    def _():
        own.start()

    pieces = [(o, g) for o in range(owned) for g in range(0, planes, GROUP)]

    def piece(index, source_core, source_half):
        o, g = pieces[index]
        return s_ref.at[source_core, o, source_half, pl.ds(g, GROUP)]

    def sends(index, src):
        dst = piece(index, core, half)
        return (
            remote(src, dst, z_send.at[index], tree_recv.at[index], {"band": up, "fft": half}),
            remote(src, dst, x_send.at[index], tree_recv.at[index], {"band": side, "fft": half}),
            remote(src, dst, y_send.at[index], y_recv.at[index], to_y),
            remote(src, dst, c_send.at[0, index], c_recv.at[0, index], to_core),
        )

    def pass_on(index):
        block = piece(index, core, other_half)
        return remote(block, block, c_send.at[1, index], c_recv.at[1, index], to_core)

    def arrived(block, recv, target):
        remote(block, block, swap_send, recv, target).wait_recv()

    def finish_y(index):
        arrived(piece(index, core, other_half), y_recv.at[index], to_y)
        pass_on(index).start()

    for index, (o, g) in enumerate(pieces):
        @pl.when(root)
        def _():
            to_up, to_side, across, beside = sends(index, x_ref.at[o, pl.ds(g, GROUP)])
            to_up.start()
            to_side.start()
            across.start()
            beside.start()

        @pl.when(jnp.logical_not(root))
        def _():
            block = piece(index, core, half)
            arrived(block, tree_recv.at[index], to_y)
            to_up, _, across, beside = sends(index, block)

            @pl.when(has_up)
            def _():
                to_up.start()

            across.start()
            beside.start()

        if index > 0:
            finish_y(index - 1)
    finish_y(len(pieces) - 1)

    for index in range(len(pieces)):
        arrived(piece(index, 1 - core, half), c_recv.at[0, index], to_core)
        arrived(piece(index, 1 - core, other_half), c_recv.at[1, index], to_core)
        to_up, to_side, across, beside = sends(index, piece(index, core, half))

        @pl.when(has_up)
        def _():
            to_up.wait_send()

        @pl.when(root)
        def _():
            to_side.wait_send()

        across.wait_send()
        beside.wait_send()
        pass_on(index).wait_send()

    @pl.when(root)
    def _():
        own.wait()

    keep.wait()
    arrived(p_ref.at[other_half], swap_recv, to_y)
    swap.wait_send()


def gather(orbitals, bands, row):
    owned, planes, cells = orbitals.shape
    count = owned * planes // GROUP
    dma = pltpu.SemaphoreType.DMA
    sources, orbital = pl.pallas_call(
        functools.partial(gather_kernel, bands // 2, row),
        out_shape=(
            jax.ShapeDtypeStruct((ROUNDS, owned, 2, planes, cells), jnp.float32),
            jax.ShapeDtypeStruct((2, planes, cells), jnp.float32),
        ),
        in_specs=[pl.BlockSpec(memory_space=pl.ANY)],
        out_specs=(pl.BlockSpec(memory_space=pl.ANY), pl.BlockSpec(memory_space=pl.ANY)),
        scratch_shapes=[dma((2,)), dma, dma]
        + [dma((count,))] * 5
        + [dma((2, count))] * 2,
        compiler_params=pltpu.CompilerParams(collective_id=0, has_side_effects=True),
        name="gather",
    )(orbitals)
    return sources.reshape(ROUNDS * owned, 2 * planes, cells), orbital.reshape(2 * planes, cells)


def two_halves(bands, orbitals):
    planes = orbitals.shape[1]
    sources, orbital = gather(orbitals, bands, 2)
    result = apply_exchange(orbital, sources)
    half = lax.axis_index("fft")
    mine = lax.dynamic_slice_in_dim(result, half * planes, planes, 0)
    theirs = lax.dynamic_slice_in_dim(result, (1 - half) * planes, planes, 0)
    back = lax.ppermute(theirs, "fft", [(0, 1), (1, 0)])
    return jnp.where(half == 0, jnp.stack([mine, back]), jnp.stack([back, mine]))


def many_parts(parts, orbitals):
    owned = orbitals.shape[0]
    place, band = lax.axis_index("fft"), lax.axis_index("band")
    fields = lax.all_gather(orbitals, "fft", axis=1, tiled=True)
    held = jnp.concatenate([jnp.where(band == r, fields, 0.0) for r in range(ROUNDS)], 0)
    sources = lax.psum(held, "band")
    groups = max(parts // owned, 1)
    share = sources.shape[0] // groups
    mine = lax.dynamic_slice_in_dim(sources, (place // owned) * share, share, 0)
    which = place % owned
    result = apply_exchange(lax.dynamic_index_in_dim(fields, which, 0, False), mine)
    placed = jnp.where(jnp.arange(owned)[:, None, None] == which, result[None], 0.0)
    return lax.psum_scatter(placed, "fft", scatter_dimension=1, tiled=True)


def solution(mesh):
    parts = mesh.shape["fft"]
    if parts == 2:
        body = functools.partial(two_halves, mesh.shape["band"])
    else:
        body = functools.partial(many_parts, parts)
    return jax.shard_map(
        body, mesh=mesh, in_specs=(P("band", "fft", None),), out_specs=P("band", "fft", None), check_vma=False
    )
```

```python
import functools
import math

import jax
import jax.numpy as jnp
import numpy as np
from jax import lax
from jax.experimental import pallas as pl
from jax.experimental.pallas import tpu as pltpu
from jax.sharding import PartitionSpec as P

GRID = 64
ROUNDS = 2
EXX_FRACTION = 0.25
SCREEN = 0.05
MESH = pl.DeviceIdType.MESH
MIB = 1024 * 1024


def real_modes(length):
    n = np.arange(length)
    rows = [np.cos(2 * np.pi * q * n / length) for q in range(length // 2 + 1)]
    rows += [np.sin(2 * np.pi * q * n / length) for q in range(1, length // 2)]
    matrix = np.array(rows)
    return matrix / np.sqrt((matrix**2).sum(1, keepdims=True))


def split(matrix):
    high = matrix.astype(jnp.bfloat16)
    return high, (matrix - high.astype(np.float64)).astype(jnp.bfloat16)


def matrices():
    modes = real_modes(GRID)
    z_forward = np.kron(np.array([[1.0, 1.0], [1.0, -1.0]]) / np.sqrt(2.0), modes.T)
    out = []
    for matrix in (z_forward, z_forward.T):
        high, low = split(matrix)
        out += [np.concatenate([high, high], 0), low]
    for matrix in (modes, modes.T):
        high, low = split(matrix)
        out.append(
            np.concatenate(
                [np.concatenate([high, high], 1), np.concatenate([low, np.zeros_like(low)], 1)], 0
            )
        )
    return out


def mode_numbers():
    half = GRID // 2
    return np.concatenate([np.arange(half + 1), np.arange(1, half)])


def filter_table():
    k = jnp.asarray(mode_numbers(), jnp.float32)
    quarter = GRID // 4
    q = np.concatenate([np.arange(quarter + 1), np.arange(1, quarter)])
    weight = np.where((q == 0) | (q == quarter), 1.0, 2.0) / (GRID // 2)
    ky = jnp.asarray(np.stack([q, GRID // 2 - q], 1), jnp.float32)
    unit = 2.0 * math.pi / GRID
    squares = (
        (k * unit)[:, None, None, None] ** 2
        + (ky * unit)[None, :, :, None] ** 2
        + (k * unit)[None, None, None, :] ** 2
    )
    guarded = jnp.where(squares > 0, squares, 1.0)
    table = jnp.where(
        squares > 0, (1.0 - jnp.exp(-guarded / (4.0 * SCREEN * SCREEN))) / guarded, 0.0
    )
    table = table * jnp.asarray(weight, jnp.float32)[None, :, None, None]
    return table.reshape(GRID, GRID * GRID)


def rotate(c, s, cos, sin):
    return cos * c - sin * s, sin * c + cos * s


def forward(x):
    n = len(x)
    if n == 2:
        return [x[0] + x[1], x[0] - x[1]], {}
    ce, se = forward(x[0::2])
    co, so = forward(x[1::2])
    half, quarter = n // 2, n // 4
    c, s = [None] * (half + 1), {}
    c[0], c[half] = ce[0] + co[0], ce[0] - co[0]
    c[quarter], s[quarter] = ce[quarter], co[quarter]
    for q in range(1, quarter):
        if 8 * q == n:
            r = math.sqrt(0.5)
            a, b = (co[q] - so[q]) * r, (co[q] + so[q]) * r
        else:
            a, b = rotate(co[q], so[q], math.cos(2 * math.pi * q / n), math.sin(2 * math.pi * q / n))
        c[q], c[half - q] = ce[q] + a, ce[q] - a
        s[q], s[half - q] = b + se[q], b - se[q]
    return c, s


def backward(c, s):
    n = 2 * (len(c) - 1)
    if n == 2:
        return [c[0] + c[1], c[0] - c[1]]
    half, quarter = n // 2, n // 4
    ce, co, se, so = [None] * (quarter + 1), [None] * (quarter + 1), {}, {}
    ce[0], co[0] = c[0] + c[half], c[0] - c[half]
    ce[quarter], co[quarter] = c[quarter], s[quarter]
    for q in range(1, quarter):
        ce[q], a = c[q] + c[half - q], c[q] - c[half - q]
        b, se[q] = s[q] + s[half - q], s[q] - s[half - q]
        if 8 * q == n:
            r = math.sqrt(0.5)
            co[q], so[q] = (a + b) * r, (b - a) * r
        else:
            co[q], so[q] = rotate(a, b, math.cos(2 * math.pi * q / n), -math.sin(2 * math.pi * q / n))
    out = [None] * n
    out[0::2], out[1::2] = backward(ce, se), backward(co, so)
    return out


def twiddles(shape, q):
    odd = lax.broadcasted_iota(jnp.int32, shape, 1) >= shape[1] // 2
    angle = 2 * math.pi * q / GRID
    return jnp.where(odd, math.cos(angle), 1.0), jnp.where(odd, math.sin(angle), 0.0)


def halves(value):
    high = value.astype(jnp.bfloat16)
    return high, (value - high.astype(jnp.float32)).astype(jnp.bfloat16)


def along_z(tiles, double, low):
    rows = jnp.concatenate(tiles, 0)
    high, rest = halves(rows)
    out = jnp.dot(jnp.concatenate([high, rest], 1), double, preferred_element_type=jnp.float32)
    out = out + jnp.dot(high, low, preferred_element_type=jnp.float32)
    step = tiles[0].shape[0]
    return [out[i * step : (i + 1) * step] for i in range(len(tiles))]


def along_x(value, double):
    length = value.shape[0]
    out = jnp.dot(double, jnp.concatenate(halves(value), 0), preferred_element_type=jnp.float32)
    return out[:length] + out[length:]


LANES = 128
PART = 512


def into_modes(densities):
    count = len(densities)
    quarter = count // 2
    c, s = forward(densities)
    for q in range(1, quarter):
        cos, sin = twiddles(densities[0].shape, q)
        c[q], s[q] = rotate(c[q], s[q], cos, sin)
    return c + [s[q] for q in range(1, quarter)]


def out_of_modes(values):
    quarter = len(values) // 2
    c, s = values[: quarter + 1], dict(enumerate(values[quarter + 1 :], 1))
    for q in range(1, quarter):
        cos, sin = twiddles(values[0].shape, q)
        c[q], s[q] = rotate(c[q], s[q], cos, -sin)
    return backward(c, s)


def filtered(tiles, table, zf2, zfl, zb2, zbl, xf, xb):
    value = along_x(jnp.concatenate(along_z(tiles, zf2, zfl), 1), xf)
    value = along_x(value * table, xb)
    return along_z([value[:, i : i + LANES] for i in range(0, value.shape[1], LANES)], zb2, zbl)


def columns(i):
    return slice(i * LANES, (i + 1) * LANES)


def exchange_kernel(orbital_ref, source_ref, filter_ref, *rest):
    constants, (out_ref, work) = rest[:6], rest[6:]
    length, cells = work.shape
    count = cells // LANES

    @pl.loop(0, length // 8)
    def _(block):
        rows = pl.ds(pl.multiple_of(block * 8, 8), 8)
        values = [
            orbital_ref[rows, columns(i)] * source_ref[0, rows, columns(i)] for i in range(count)
        ]
        for i, value in enumerate(into_modes(values)):
            work[rows, columns(i)] = value

    @pl.loop(0, cells // PART)
    def _(part):
        lanes = [pl.ds(pl.multiple_of(part * PART + i, LANES), LANES) for i in range(0, PART, LANES)]
        table = filter_ref[:, pl.ds(pl.multiple_of(part * PART, PART), PART)]
        tiles = filtered([work[:, lane] for lane in lanes], table, *(r[...] for r in constants))
        for lane, tile in zip(lanes, tiles):
            work[:, lane] = tile

    first = pl.program_id(0) == 0

    @pl.loop(0, length // 8)
    def _(block):
        rows = pl.ds(pl.multiple_of(block * 8, 8), 8)
        values = out_of_modes([work[rows, columns(i)] for i in range(count)])
        for i, value in enumerate(values):
            term = value * source_ref[0, rows, columns(i)] * -EXX_FRACTION
            out_ref[rows, columns(i)] = jnp.where(first, 0.0, out_ref[rows, columns(i)]) + term


def apply_exchange(orbital, sources):
    count, length, cells = sources.shape
    constants = [jnp.asarray(m) for m in matrices()]
    whole = lambda shape: pl.BlockSpec(shape, lambda j: (0, 0))
    return pl.pallas_call(
        exchange_kernel,
        grid=(count,),
        out_shape=jax.ShapeDtypeStruct((length, cells), jnp.float32),
        in_specs=[
            whole((length, cells)),
            pl.BlockSpec((1, length, cells), lambda j: (j, 0, 0)),
            whole((length, cells)),
        ]
        + [whole(m.shape) for m in constants],
        out_specs=whole((length, cells)),
        scratch_shapes=[pltpu.VMEM((length, cells), jnp.float32)],
        compiler_params=pltpu.CompilerParams(vmem_limit_bytes=32 * MIB),
        name="exchange",
    )(orbital, sources, filter_table(), *constants)


GROUP = 8
PIECE = 2048
LAG = 3


def filter_part(part, length):
    shape = (length, PART)
    half, quarter = length // 2, length // 4
    lane = lax.broadcasted_iota(jnp.int32, shape, 1) + part * PART

    def mode(index):
        return jnp.where(index > half, index - half, index)

    row = lane >> 7
    q = jnp.where(row > quarter, row - quarter, row)
    ky = jnp.where((lane & half * 2) == 0, q, half - q)
    edge = jnp.logical_or(q == 0, q == quarter)
    squares = jnp.zeros(shape, jnp.float32)
    for k in (mode(lax.broadcasted_iota(jnp.int32, shape, 0)), ky, mode(lane & (length - 1))):
        squares = squares + (k.astype(jnp.float32) * (2.0 * math.pi / length)) ** 2
    guarded = jnp.where(squares > 0, squares, 1.0)
    table = (1.0 - jnp.exp(-guarded / (4.0 * SCREEN * SCREEN))) / guarded
    return jnp.where(squares > 0, table, 0.0) * jnp.where(edge, 1.0 / half, 2.0 / half)


def fused_kernel(chips, row, x_ref, *rest):
    constants, out_ref = rest[:6], rest[6]
    (source, orbital, table, work, total, copy_sem, swap_send, swap_recv, up_send, side_send, tree_recv,
     y_send, y_recv, share_send, c_send, c_recv, back_send, back_recv) = rest[7:]
    band, half = lax.axis_index("band"), lax.axis_index("fft")
    chip, core = band // 2, band % 2
    column, layer = chip % row, chip // row
    owned, planes, cells = x_ref.shape
    length = 2 * planes
    other = 1 - half
    groups, parts = planes // GROUP, cells // PIECE
    per_orbital = groups * parts
    pieces = owned * per_orbital
    root, has_up, has_down = chip == 0, chip + row < chips, layer > 0
    to_y = {"band": band, "fft": other}
    to_core = {"band": band + 1 - 2 * core, "fft": half}
    to_x = {"band": band + 2 - 4 * column, "fft": half}
    to_up = {"band": band + 2 * row, "fft": half}
    to_down = {"band": band - 2 * row, "fft": half}

    barrier = pltpu.get_barrier_semaphore()

    def greet(target):
        pl.semaphore_signal(barrier, inc=1, device_id=target, device_id_type=MESH)

    greet(to_y)
    greet(to_core)
    greet(to_x)

    @pl.when(has_up)
    def _():
        greet(to_up)

    @pl.when(has_down)
    def _():
        greet(to_down)

    pl.semaphore_wait(barrier, 3 + has_up.astype(jnp.int32) + has_down.astype(jnp.int32))

    def remote(src, dst, send, recv, target):
        return pltpu.make_async_remote_copy(
            src_ref=src, dst_ref=dst, send_sem=send, recv_sem=recv, device_id=target, device_id_type=MESH
        )

    swap = remote(x_ref.at[other], orbital.at[half], swap_send, swap_recv, to_y)
    swap.start()
    keep = pltpu.make_async_copy(x_ref.at[half], orbital.at[half], copy_sem.at[0])
    keep.start()

    @pl.when(root)
    def _():
        pltpu.make_async_copy(x_ref, source.at[core, :, half], copy_sem.at[1]).start()

    def place(k):
        group = (k % per_orbital) // parts
        lanes = pl.ds(pl.multiple_of((k % parts) * PIECE, PIECE), PIECE)
        return k // per_orbital, pl.ds(pl.multiple_of(group * GROUP, GROUP), GROUP), lanes

    def piece(k, source_core, source_half):
        o, rows, lanes = place(k)
        return source.at[source_core, o, source_half, rows, lanes]

    def crosses(k):
        mine = jnp.where(layer == 0, k % 4, k % 2) == 0
        return mine == (column == 0)

    def send_up(k, src):
        return remote(src, piece(k, core, half), up_send.at[k], tree_recv.at[k], to_up)

    def send_side(k, src):
        return remote(src, piece(k, core, half), side_send.at[k], tree_recv.at[k], to_x)

    def send_across(k, src):
        return remote(src, piece(k, core, half), y_send.at[k], y_recv.at[k], to_y)

    def send_beside(k, src, which, source_half):
        return remote(src, piece(k, core, source_half), c_send.at[which, k], c_recv.at[which, k], to_core)

    def send_share(k):
        block = piece(k, core, other)
        return remote(block, block, share_send.at[k], y_recv.at[k], to_x)

    def arrived(block, recv, target):
        remote(block, block, swap_send, recv, target).wait_recv()

    def relay(k, src):
        @pl.when(has_up)
        def _():
            send_up(k, src).start()

        @pl.when(crosses(k))
        def _():
            send_across(k, src).start()

    def event(k):
        @pl.when(k < pieces)
        def _():
            @pl.when(root)
            def _():
                o, rows, lanes = place(k)
                src = x_ref.at[o, rows, lanes]
                send_side(k, src).start()
                relay(k, src)
                send_beside(k, src, 0, half).start()

            @pl.when(jnp.logical_not(root))
            def _():
                src = piece(k, core, half)
                arrived(src, tree_recv.at[k], to_y)
                relay(k, src)
                send_beside(k, src, 0, half).start()

        def across(k, sharing):
            @pl.when(jnp.logical_and(jnp.logical_and(k >= 0, k < pieces), crosses(k) == sharing))
            def _():
                block = piece(k, core, other)
                arrived(block, y_recv.at[k], to_y)
                if sharing:
                    send_share(k).start()
                send_beside(k, block, 1, other).start()

        across(k - 1, True)
        across(k - 2, False)

        @pl.when(k >= LAG)
        def _():
            arrived(piece(k - LAG, 1 - core, half), c_recv.at[0, k - LAG], to_core)
            arrived(piece(k - LAG, 1 - core, other), c_recv.at[1, k - LAG], to_core)

    ahead = per_orbital + LAG
    slots = pieces - per_orbital

    @pl.loop(0, ahead)
    def _(k):
        event(k)

        @pl.when(k < cells // PART)
        def _():
            table[:, pl.ds(pl.multiple_of(k * PART, PART), PART)] = filter_part(k, length)

    arrived(orbital.at[other], swap_recv, to_y)
    keep.wait()

    @pl.when(root)
    def _():
        pltpu.make_async_copy(x_ref, source.at[core, :, half], copy_sem.at[1]).wait()

    def slot(index, block):
        number = index * 6 + block // 4

        @pl.when(jnp.logical_and(block % 4 == 0, number < slots))
        def _():
            event(ahead + number)

    def back(group):
        rows = pl.ds(pl.multiple_of(group * GROUP, GROUP), GROUP)
        return remote(
            total.at[other, rows], out_ref.at[half, rows], back_send.at[group], back_recv.at[group], to_y
        )

    count = cells // LANES
    last = ROUNDS * owned - 1

    @pl.loop(0, ROUNDS * owned)
    def _(index):
        b, o = index % ROUNDS, index // ROUNDS

        @pl.loop(0, 2 * groups)
        def _(block):
            slot(index, block)
            h, rows = block // groups, pl.ds(pl.multiple_of((block % groups) * GROUP, GROUP), GROUP)
            to = pl.ds(pl.multiple_of(block * GROUP, GROUP), GROUP)
            values = [
                orbital[h, rows, columns(i)] * source[b, o, h, rows, columns(i)] for i in range(count)
            ]
            for i, value in enumerate(into_modes(values)):
                work[to, columns(i)] = value

        @pl.loop(0, cells // PART)
        def _(part):
            slot(index, part + 8)
            lanes = [pl.ds(pl.multiple_of(part * PART + i, LANES), LANES) for i in range(0, PART, LANES)]
            whole = table[:, pl.ds(pl.multiple_of(part * PART, PART), PART)]
            tiles = filtered([work[:, lane] for lane in lanes], whole, *(r[...] for r in constants))
            for lane, tile in zip(lanes, tiles):
                work[:, lane] = tile

        @pl.loop(0, 2 * groups)
        def _(step):
            slot(index, step + 16)
            block = (step + groups * other) % (2 * groups)
            h, rows = block // groups, pl.ds(pl.multiple_of((block % groups) * GROUP, GROUP), GROUP)
            to = pl.ds(pl.multiple_of(block * GROUP, GROUP), GROUP)
            values = out_of_modes([work[to, columns(i)] for i in range(count)])
            for i, value in enumerate(values):
                term = value * source[b, o, h, rows, columns(i)] * -EXX_FRACTION
                total[h, rows, columns(i)] = jnp.where(index == 0, 0.0, total[h, rows, columns(i)]) + term

            @pl.when(jnp.logical_and(index == last, step < groups))
            def _():
                back(step).start()

    mine = pltpu.make_async_copy(total.at[half], out_ref.at[half], copy_sem.at[2])
    mine.start()

    @pl.loop(0, pieces)
    def _(k):
        src = piece(k, core, half)

        @pl.when(has_up)
        def _():
            send_up(k, src).wait_send()

        @pl.when(root)
        def _():
            send_side(k, src).wait_send()

        @pl.when(crosses(k))
        def _():
            send_across(k, src).wait_send()
            send_share(k).wait_send()

        send_beside(k, src, 0, half).wait_send()
        send_beside(k, src, 1, half).wait_send()

    swap.wait_send()

    @pl.loop(0, groups)
    def _(group):
        back(group).wait_send()
        rows = pl.ds(pl.multiple_of(group * GROUP, GROUP), GROUP)
        arrived(out_ref.at[other, rows], back_recv.at[group], to_y)

    mine.wait()


def two_halves(bands, row, orbitals):
    owned, planes, cells = orbitals.shape
    count = owned * (planes // GROUP) * (cells // PIECE)
    dma = pltpu.SemaphoreType.DMA
    constants = [jnp.asarray(m) for m in matrices()]
    grid = lambda *lead: pltpu.VMEM((*lead, planes, cells), jnp.float32)
    flat = pltpu.VMEM((2 * planes, cells), jnp.float32)
    return pl.pallas_call(
        functools.partial(fused_kernel, bands // 2, row),
        out_shape=jax.ShapeDtypeStruct(orbitals.shape, jnp.float32),
        in_specs=[pl.BlockSpec(memory_space=pl.ANY)]
        + [pl.BlockSpec(memory_space=pltpu.VMEM)] * len(constants),
        out_specs=pl.BlockSpec(memory_space=pl.ANY),
        scratch_shapes=[grid(ROUNDS, owned, 2), grid(2), flat, flat, grid(2)]
        + [dma((3,)), dma, dma]
        + [dma((count,))] * 6
        + [dma((2, count))] * 2
        + [dma((planes // GROUP,))] * 2,
        compiler_params=pltpu.CompilerParams(
            collective_id=0, has_side_effects=True, vmem_limit_bytes=32 * MIB
        ),
        name="exchange",
    )(orbitals, *constants)


def many_parts(parts, orbitals):
    owned = orbitals.shape[0]
    place, band = lax.axis_index("fft"), lax.axis_index("band")
    fields = lax.all_gather(orbitals, "fft", axis=1, tiled=True)
    held = jnp.concatenate([jnp.where(band == r, fields, 0.0) for r in range(ROUNDS)], 0)
    sources = lax.psum(held, "band")
    groups = max(parts // owned, 1)
    share = sources.shape[0] // groups
    mine = lax.dynamic_slice_in_dim(sources, (place // owned) * share, share, 0)
    which = place % owned
    result = apply_exchange(lax.dynamic_index_in_dim(fields, which, 0, False), mine)
    placed = jnp.where(jnp.arange(owned)[:, None, None] == which, result[None], 0.0)
    return lax.psum_scatter(placed, "fft", scatter_dimension=1, tiled=True)


def solution(mesh):
    parts = mesh.shape["fft"]
    if parts == 2:
        body = functools.partial(two_halves, mesh.shape["band"], 2)
    else:
        body = functools.partial(many_parts, parts)
    return jax.shard_map(
        body, mesh=mesh, in_specs=(P("band", "fft", None),), out_specs=P("band", "fft", None), check_vma=False
    )
```

```python
import functools
import math

import jax
import jax.numpy as jnp
import numpy as np
from jax import lax
from jax.experimental import pallas as pl
from jax.experimental.pallas import tpu as pltpu
from jax.sharding import PartitionSpec as P

GRID = 64
ROUNDS = 2
EXX_FRACTION = 0.25
SCREEN = 0.05
MESH = pl.DeviceIdType.MESH
MIB = 1024 * 1024


def real_modes(length):
    n = np.arange(length)
    rows = [np.cos(2 * np.pi * q * n / length) for q in range(length // 2 + 1)]
    rows += [np.sin(2 * np.pi * q * n / length) for q in range(1, length // 2)]
    matrix = np.array(rows)
    return matrix / np.sqrt((matrix**2).sum(1, keepdims=True))


def split(matrix):
    high = matrix.astype(jnp.bfloat16)
    return high, (matrix - high.astype(np.float64)).astype(jnp.bfloat16)


def matrices():
    modes = real_modes(GRID)
    z_forward = np.kron(np.array([[1.0, 1.0], [1.0, -1.0]]) / np.sqrt(2.0), modes.T)
    out = []
    for matrix in (z_forward, z_forward.T):
        high, low = split(matrix)
        out += [np.concatenate([high, high], 0), low]
    for matrix in (modes, modes.T):
        high, low = split(matrix)
        out.append(
            np.concatenate(
                [np.concatenate([high, high], 1), np.concatenate([low, np.zeros_like(low)], 1)], 0
            )
        )
    return np.concatenate(out, 0)


def unpack(ref):
    out, start = [], 0
    for rows in (256, 128, 256, 128, 128, 128):
        out.append(ref[start : start + rows, :])
        start += rows
    return out


def mode_numbers():
    half = GRID // 2
    return np.concatenate([np.arange(half + 1), np.arange(1, half)])


def filter_table():
    k = jnp.asarray(mode_numbers(), jnp.float32)
    quarter = GRID // 4
    q = np.concatenate([np.arange(quarter + 1), np.arange(1, quarter)])
    weight = np.where((q == 0) | (q == quarter), 1.0, 2.0) / (GRID // 2)
    ky = jnp.asarray(np.stack([q, GRID // 2 - q], 1), jnp.float32)
    unit = 2.0 * math.pi / GRID
    squares = (
        (k * unit)[:, None, None, None] ** 2
        + (ky * unit)[None, :, :, None] ** 2
        + (k * unit)[None, None, None, :] ** 2
    )
    guarded = jnp.where(squares > 0, squares, 1.0)
    table = jnp.where(
        squares > 0, (1.0 - jnp.exp(-guarded / (4.0 * SCREEN * SCREEN))) / guarded, 0.0
    )
    table = table * jnp.asarray(weight, jnp.float32)[None, :, None, None]
    return table.reshape(GRID, GRID * GRID)


def rotate(c, s, cos, sin):
    return cos * c - sin * s, sin * c + cos * s


def forward(x):
    n = len(x)
    if n == 2:
        return [x[0] + x[1], x[0] - x[1]], {}
    ce, se = forward(x[0::2])
    co, so = forward(x[1::2])
    half, quarter = n // 2, n // 4
    c, s = [None] * (half + 1), {}
    c[0], c[half] = ce[0] + co[0], ce[0] - co[0]
    c[quarter], s[quarter] = ce[quarter], co[quarter]
    for q in range(1, quarter):
        if 8 * q == n:
            r = math.sqrt(0.5)
            a, b = (co[q] - so[q]) * r, (co[q] + so[q]) * r
        else:
            a, b = rotate(co[q], so[q], math.cos(2 * math.pi * q / n), math.sin(2 * math.pi * q / n))
        c[q], c[half - q] = ce[q] + a, ce[q] - a
        s[q], s[half - q] = b + se[q], b - se[q]
    return c, s


def backward(c, s):
    n = 2 * (len(c) - 1)
    if n == 2:
        return [c[0] + c[1], c[0] - c[1]]
    half, quarter = n // 2, n // 4
    ce, co, se, so = [None] * (quarter + 1), [None] * (quarter + 1), {}, {}
    ce[0], co[0] = c[0] + c[half], c[0] - c[half]
    ce[quarter], co[quarter] = c[quarter], s[quarter]
    for q in range(1, quarter):
        ce[q], a = c[q] + c[half - q], c[q] - c[half - q]
        b, se[q] = s[q] + s[half - q], s[q] - s[half - q]
        if 8 * q == n:
            r = math.sqrt(0.5)
            co[q], so[q] = (a + b) * r, (b - a) * r
        else:
            co[q], so[q] = rotate(a, b, math.cos(2 * math.pi * q / n), -math.sin(2 * math.pi * q / n))
    out = [None] * n
    out[0::2], out[1::2] = backward(ce, se), backward(co, so)
    return out


def twiddles(shape, q):
    odd = lax.broadcasted_iota(jnp.int32, shape, 1) >= shape[1] // 2
    angle = 2 * math.pi * q / GRID
    return jnp.where(odd, math.cos(angle), 1.0), jnp.where(odd, math.sin(angle), 0.0)


def halves(value):
    high = value.astype(jnp.bfloat16)
    return high, (value - high.astype(jnp.float32)).astype(jnp.bfloat16)


def along_z(tiles, double, low):
    rows = jnp.concatenate(tiles, 0)
    high, rest = halves(rows)
    out = jnp.dot(jnp.concatenate([high, rest], 1), double, preferred_element_type=jnp.float32)
    out = out + jnp.dot(high, low, preferred_element_type=jnp.float32)
    step = tiles[0].shape[0]
    return [out[i * step : (i + 1) * step] for i in range(len(tiles))]


def along_x(value, double):
    length = value.shape[0]
    out = jnp.dot(double, jnp.concatenate(halves(value), 0), preferred_element_type=jnp.float32)
    return out[:length] + out[length:]


LANES = 128
PART = 2048
TABLE_PART = 512


def into_modes(densities):
    count = len(densities)
    quarter = count // 2
    c, s = forward(densities)
    for q in range(1, quarter):
        cos, sin = twiddles(densities[0].shape, q)
        c[q], s[q] = rotate(c[q], s[q], cos, sin)
    return c + [s[q] for q in range(1, quarter)]


def out_of_modes(values):
    quarter = len(values) // 2
    c, s = values[: quarter + 1], dict(enumerate(values[quarter + 1 :], 1))
    for q in range(1, quarter):
        cos, sin = twiddles(values[0].shape, q)
        c[q], s[q] = rotate(c[q], s[q], cos, -sin)
    return backward(c, s)


def filtered(tiles, table, zf2, zfl, zb2, zbl, xf, xb):
    value = along_x(jnp.concatenate(along_z(tiles, zf2, zfl), 1), xf)
    value = along_x(value * table, xb)
    return along_z([value[:, i : i + LANES] for i in range(0, value.shape[1], LANES)], zb2, zbl)


def columns(i):
    return slice(i * LANES, (i + 1) * LANES)


def exchange_kernel(orbital_ref, source_ref, filter_ref, *rest):
    constants, out_ref, work = rest
    length, cells = work.shape
    count = cells // LANES

    @pl.loop(0, length // 8)
    def _(block):
        rows = pl.ds(pl.multiple_of(block * 8, 8), 8)
        values = [
            orbital_ref[rows, columns(i)] * source_ref[0, rows, columns(i)] for i in range(count)
        ]
        for i, value in enumerate(into_modes(values)):
            work[rows, columns(i)] = value

    @pl.loop(0, cells // PART)
    def _(part):
        lanes = [pl.ds(pl.multiple_of(part * PART + i, LANES), LANES) for i in range(0, PART, LANES)]
        table = filter_ref[:, pl.ds(pl.multiple_of(part * PART, PART), PART)]
        tiles = filtered([work[:, lane] for lane in lanes], table, *unpack(constants))
        for lane, tile in zip(lanes, tiles):
            work[:, lane] = tile

    first = pl.program_id(0) == 0

    @pl.loop(0, length // 8)
    def _(block):
        rows = pl.ds(pl.multiple_of(block * 8, 8), 8)
        values = out_of_modes([work[rows, columns(i)] for i in range(count)])
        for i, value in enumerate(values):
            term = value * source_ref[0, rows, columns(i)] * -EXX_FRACTION
            out_ref[rows, columns(i)] = jnp.where(first, 0.0, out_ref[rows, columns(i)]) + term


def apply_exchange(orbital, sources):
    count, length, cells = sources.shape
    constants = jnp.asarray(matrices())
    whole = lambda shape: pl.BlockSpec(shape, lambda j: (0, 0))
    return pl.pallas_call(
        exchange_kernel,
        grid=(count,),
        out_shape=jax.ShapeDtypeStruct((length, cells), jnp.float32),
        in_specs=[
            whole((length, cells)),
            pl.BlockSpec((1, length, cells), lambda j: (j, 0, 0)),
            whole((length, cells)),
            whole(constants.shape),
        ],
        out_specs=whole((length, cells)),
        scratch_shapes=[pltpu.VMEM((length, cells), jnp.float32)],
        compiler_params=pltpu.CompilerParams(vmem_limit_bytes=32 * MIB),
        name="exchange",
    )(orbital, sources, filter_table(), constants)


GROUP = 8
PIECE = 2048
LAG = 3


def filter_part(part, length):
    shape = (length, TABLE_PART)
    half, quarter = length // 2, length // 4
    lane = lax.broadcasted_iota(jnp.int32, shape, 1) + part * TABLE_PART

    def mode(index):
        return jnp.where(index > half, index - half, index)

    row = lane >> 7
    q = jnp.where(row > quarter, row - quarter, row)
    ky = jnp.where((lane & half * 2) == 0, q, half - q)
    edge = jnp.logical_or(q == 0, q == quarter)
    squares = jnp.zeros(shape, jnp.float32)
    for k in (mode(lax.broadcasted_iota(jnp.int32, shape, 0)), ky, mode(lane & (length - 1))):
        squares = squares + (k.astype(jnp.float32) * (2.0 * math.pi / length)) ** 2
    guarded = jnp.where(squares > 0, squares, 1.0)
    table = (1.0 - jnp.exp(-guarded / (4.0 * SCREEN * SCREEN))) / guarded
    return jnp.where(squares > 0, table, 0.0) * jnp.where(edge, 1.0 / half, 2.0 / half)


def fused_kernel(chips, row, x_ref, matrix_ref, out_ref, *rest):
    (constants, source, orbital, table, work, total, copy_sem, swap_send, swap_recv, up_send, side_send, tree_recv,
     y_send, y_recv, share_send, c_send, c_recv, back_send, back_recv) = rest
    band, half = lax.axis_index("band"), lax.axis_index("fft")
    chip, core = band // 2, band % 2
    column, layer = chip % row, chip // row
    owned, planes, cells = x_ref.shape
    length = 2 * planes
    other = 1 - half
    groups, parts = planes // GROUP, cells // PIECE
    per_orbital = groups * parts
    pieces = owned * per_orbital
    root, has_up, has_down = chip == 0, chip + row < chips, layer > 0
    to_y = {"band": band, "fft": other}
    to_core = {"band": band + 1 - 2 * core, "fft": half}
    to_x = {"band": band + 2 - 4 * column, "fft": half}
    to_up = {"band": band + 2 * row, "fft": half}
    to_down = {"band": band - 2 * row, "fft": half}

    barrier = pltpu.get_barrier_semaphore()

    def greet(target):
        pl.semaphore_signal(barrier, inc=1, device_id=target, device_id_type=MESH)

    greet(to_y)
    greet(to_core)
    greet(to_x)

    @pl.when(has_up)
    def _():
        greet(to_up)

    @pl.when(has_down)
    def _():
        greet(to_down)

    pl.semaphore_wait(barrier, 3 + has_up.astype(jnp.int32) + has_down.astype(jnp.int32))

    def remote(src, dst, send, recv, target):
        return pltpu.make_async_remote_copy(
            src_ref=src, dst_ref=dst, send_sem=send, recv_sem=recv, device_id=target, device_id_type=MESH
        )

    swap = remote(x_ref.at[other], orbital.at[half], swap_send, swap_recv, to_y)
    swap.start()
    keep = pltpu.make_async_copy(x_ref.at[half], orbital.at[half], copy_sem.at[0])
    keep.start()
    fetch = pltpu.make_async_copy(matrix_ref, constants, copy_sem.at[3])
    fetch.start()

    @pl.when(root)
    def _():
        pltpu.make_async_copy(x_ref, source.at[core, :, half], copy_sem.at[1]).start()

    def place(k):
        group = (k % per_orbital) // parts
        lanes = pl.ds(pl.multiple_of((k % parts) * PIECE, PIECE), PIECE)
        return k // per_orbital, pl.ds(pl.multiple_of(group * GROUP, GROUP), GROUP), lanes

    def piece(k, source_core, source_half):
        o, rows, lanes = place(k)
        return source.at[source_core, o, source_half, rows, lanes]

    def crosses(k):
        mine = jnp.where(layer == 0, k % 4, k % 2) == 0
        return mine == (column == 0)

    def send_up(k, src):
        return remote(src, piece(k, core, half), up_send.at[k], tree_recv.at[k], to_up)

    def send_side(k, src):
        return remote(src, piece(k, core, half), side_send.at[k], tree_recv.at[k], to_x)

    def send_across(k, src):
        return remote(src, piece(k, core, half), y_send.at[k], y_recv.at[k], to_y)

    def send_beside(k, src, which, source_half):
        return remote(src, piece(k, core, source_half), c_send.at[which, k], c_recv.at[which, k], to_core)

    def send_share(k):
        block = piece(k, core, other)
        return remote(block, block, share_send.at[k], y_recv.at[k], to_x)

    def arrived(block, recv, target):
        remote(block, block, swap_send, recv, target).wait_recv()

    def relay(k, src):
        @pl.when(has_up)
        def _():
            send_up(k, src).start()

        @pl.when(crosses(k))
        def _():
            send_across(k, src).start()

    def event(k):
        @pl.when(k < pieces)
        def _():
            @pl.when(root)
            def _():
                o, rows, lanes = place(k)
                src = x_ref.at[o, rows, lanes]
                send_side(k, src).start()
                relay(k, src)
                send_beside(k, src, 0, half).start()

            @pl.when(jnp.logical_not(root))
            def _():
                src = piece(k, core, half)
                arrived(src, tree_recv.at[k], to_y)
                relay(k, src)
                send_beside(k, src, 0, half).start()

        def across(k, sharing):
            @pl.when(jnp.logical_and(jnp.logical_and(k >= 0, k < pieces), crosses(k) == sharing))
            def _():
                block = piece(k, core, other)
                arrived(block, y_recv.at[k], to_y)
                if sharing:
                    send_share(k).start()
                send_beside(k, block, 1, other).start()

        across(k - 1, True)
        across(k - 2, False)

        @pl.when(k >= LAG)
        def _():
            arrived(piece(k - LAG, 1 - core, half), c_recv.at[0, k - LAG], to_core)
            arrived(piece(k - LAG, 1 - core, other), c_recv.at[1, k - LAG], to_core)

    ahead = per_orbital + LAG
    slots = pieces - per_orbital

    @pl.loop(0, ahead)
    def _(k):
        event(k)

        @pl.when(k < cells // TABLE_PART)
        def _():
            lanes = pl.ds(pl.multiple_of(k * TABLE_PART, TABLE_PART), TABLE_PART)
            table[:, lanes] = filter_part(k, length)

    arrived(orbital.at[other], swap_recv, to_y)
    keep.wait()
    fetch.wait()

    @pl.when(root)
    def _():
        pltpu.make_async_copy(x_ref, source.at[core, :, half], copy_sem.at[1]).wait()

    def slot(index, block):
        number = index * 6 + block // 4

        @pl.when(jnp.logical_and(block % 4 == 0, number < slots))
        def _():
            event(ahead + number)

    def back(group):
        rows = pl.ds(pl.multiple_of(group * GROUP, GROUP), GROUP)
        return remote(
            total.at[other, rows], out_ref.at[half, rows], back_send.at[group], back_recv.at[group], to_y
        )

    count = cells // LANES
    last = ROUNDS * owned - 1

    @pl.loop(0, ROUNDS * owned)
    def _(index):
        b, o = index % ROUNDS, index // ROUNDS

        @pl.loop(0, 2 * groups)
        def _(block):
            slot(index, block)
            h, rows = block // groups, pl.ds(pl.multiple_of((block % groups) * GROUP, GROUP), GROUP)
            to = pl.ds(pl.multiple_of(block * GROUP, GROUP), GROUP)
            values = [
                orbital[h, rows, columns(i)] * source[b, o, h, rows, columns(i)] for i in range(count)
            ]
            for i, value in enumerate(into_modes(values)):
                work[to, columns(i)] = value

        @pl.loop(0, cells // PART)
        def _(part):
            slot(index, part * 4 + 8)
            lanes = [pl.ds(pl.multiple_of(part * PART + i, LANES), LANES) for i in range(0, PART, LANES)]
            whole = table[:, pl.ds(pl.multiple_of(part * PART, PART), PART)]
            tiles = filtered([work[:, lane] for lane in lanes], whole, *unpack(constants))
            for lane, tile in zip(lanes, tiles):
                work[:, lane] = tile

        @pl.loop(0, 2 * groups)
        def _(step):
            slot(index, step + 16)
            block = (step + groups * other) % (2 * groups)
            h, rows = block // groups, pl.ds(pl.multiple_of((block % groups) * GROUP, GROUP), GROUP)
            to = pl.ds(pl.multiple_of(block * GROUP, GROUP), GROUP)
            values = out_of_modes([work[to, columns(i)] for i in range(count)])
            for i, value in enumerate(values):
                term = value * source[b, o, h, rows, columns(i)] * -EXX_FRACTION
                total[h, rows, columns(i)] = jnp.where(index == 0, 0.0, total[h, rows, columns(i)]) + term

            @pl.when(jnp.logical_and(index == last, step < groups))
            def _():
                back(step).start()

    mine = pltpu.make_async_copy(total.at[half], out_ref.at[half], copy_sem.at[2])
    mine.start()

    @pl.loop(0, pieces)
    def _(k):
        src = piece(k, core, half)

        @pl.when(has_up)
        def _():
            send_up(k, src).wait_send()

        @pl.when(root)
        def _():
            send_side(k, src).wait_send()

        @pl.when(crosses(k))
        def _():
            send_across(k, src).wait_send()
            send_share(k).wait_send()

        send_beside(k, src, 0, half).wait_send()
        send_beside(k, src, 1, half).wait_send()

    swap.wait_send()

    @pl.loop(0, groups)
    def _(group):
        back(group).wait_send()
        rows = pl.ds(pl.multiple_of(group * GROUP, GROUP), GROUP)
        arrived(out_ref.at[other, rows], back_recv.at[group], to_y)

    mine.wait()


def two_halves(bands, row, orbitals):
    owned, planes, cells = orbitals.shape
    count = owned * (planes // GROUP) * (cells // PIECE)
    dma = pltpu.SemaphoreType.DMA
    constants = jnp.asarray(matrices())
    grid = lambda *lead: pltpu.VMEM((*lead, planes, cells), jnp.float32)
    flat = pltpu.VMEM((2 * planes, cells), jnp.float32)
    return pl.pallas_call(
        functools.partial(fused_kernel, bands // 2, row),
        out_shape=jax.ShapeDtypeStruct(orbitals.shape, jnp.float32),
        in_specs=[pl.BlockSpec(memory_space=pl.ANY)] * 2,
        out_specs=pl.BlockSpec(memory_space=pl.ANY),
        scratch_shapes=[pltpu.VMEM(constants.shape, jnp.bfloat16), grid(ROUNDS, owned, 2), grid(2), flat, flat, grid(2)]
        + [dma((4,)), dma, dma]
        + [dma((count,))] * 6
        + [dma((2, count))] * 2
        + [dma((planes // GROUP,))] * 2,
        compiler_params=pltpu.CompilerParams(
            collective_id=0, has_side_effects=True, vmem_limit_bytes=60 * MIB
        ),
        name="exchange",
    )(orbitals, constants)


def many_parts(parts, orbitals):
    owned = orbitals.shape[0]
    place, band = lax.axis_index("fft"), lax.axis_index("band")
    fields = lax.all_gather(orbitals, "fft", axis=1, tiled=True)
    held = jnp.concatenate([jnp.where(band == r, fields, 0.0) for r in range(ROUNDS)], 0)
    sources = lax.psum(held, "band")
    groups = max(parts // owned, 1)
    share = sources.shape[0] // groups
    mine = lax.dynamic_slice_in_dim(sources, (place // owned) * share, share, 0)
    which = place % owned
    result = apply_exchange(lax.dynamic_index_in_dim(fields, which, 0, False), mine)
    placed = jnp.where(jnp.arange(owned)[:, None, None] == which, result[None], 0.0)
    return lax.psum_scatter(placed, "fft", scatter_dimension=1, tiled=True)


def solution(mesh):
    parts = mesh.shape["fft"]
    if parts == 2:
        body = functools.partial(two_halves, mesh.shape["band"], 2)
    else:
        body = functools.partial(many_parts, parts)
    return jax.shard_map(
        body, mesh=mesh, in_specs=(P("band", "fft", None),), out_specs=P("band", "fft", None), check_vma=False
    )
```

```python
import functools
import math

import jax
import jax.numpy as jnp
import numpy as np
from jax import lax
from jax.experimental import pallas as pl
from jax.experimental.pallas import tpu as pltpu
from jax.sharding import PartitionSpec as P

GRID = 64
ROUNDS = 2
EXX_FRACTION = 0.25
SCREEN = 0.05
MESH = pl.DeviceIdType.MESH
MIB = 1024 * 1024


def real_modes(length):
    n = np.arange(length)
    rows = [np.cos(2 * np.pi * q * n / length) for q in range(length // 2 + 1)]
    rows += [np.sin(2 * np.pi * q * n / length) for q in range(1, length // 2)]
    matrix = np.array(rows)
    return matrix / np.sqrt((matrix**2).sum(1, keepdims=True))


def split(matrix):
    high = matrix.astype(jnp.bfloat16)
    return high, (matrix - high.astype(np.float64)).astype(jnp.bfloat16)


def matrices():
    modes = real_modes(GRID)
    z_forward = np.kron(np.array([[1.0, 1.0], [1.0, -1.0]]) / np.sqrt(2.0), modes.T)
    out = []
    for matrix in (z_forward, z_forward.T):
        high, low = split(matrix)
        out += [np.concatenate([high, high], 0), low]
    for matrix in (modes, modes.T):
        high, low = split(matrix)
        out.append(
            np.concatenate(
                [np.concatenate([high, high], 1), np.concatenate([low, np.zeros_like(low)], 1)], 0
            )
        )
    return np.concatenate(out, 0)


def unpack(ref):
    out, start = [], 0
    for rows in (256, 128, 256, 128, 128, 128):
        out.append(ref[start : start + rows, :])
        start += rows
    return out


def mode_numbers():
    half = GRID // 2
    return np.concatenate([np.arange(half + 1), np.arange(1, half)])


def filter_table():
    k = jnp.asarray(mode_numbers(), jnp.float32)
    quarter = GRID // 4
    q = np.concatenate([np.arange(quarter + 1), np.arange(1, quarter)])
    weight = np.where((q == 0) | (q == quarter), 1.0, 2.0) / (GRID // 2)
    ky = jnp.asarray(np.stack([q, GRID // 2 - q], 1), jnp.float32)
    unit = 2.0 * math.pi / GRID
    squares = (
        (k * unit)[:, None, None, None] ** 2
        + (ky * unit)[None, :, :, None] ** 2
        + (k * unit)[None, None, None, :] ** 2
    )
    guarded = jnp.where(squares > 0, squares, 1.0)
    table = jnp.where(
        squares > 0, (1.0 - jnp.exp(-guarded / (4.0 * SCREEN * SCREEN))) / guarded, 0.0
    )
    table = table * jnp.asarray(weight, jnp.float32)[None, :, None, None]
    return table.reshape(GRID, GRID * GRID)


def rotate(c, s, cos, sin):
    return cos * c - sin * s, sin * c + cos * s


def forward(x):
    n = len(x)
    if n == 2:
        return [x[0] + x[1], x[0] - x[1]], {}
    ce, se = forward(x[0::2])
    co, so = forward(x[1::2])
    half, quarter = n // 2, n // 4
    c, s = [None] * (half + 1), {}
    c[0], c[half] = ce[0] + co[0], ce[0] - co[0]
    c[quarter], s[quarter] = ce[quarter], co[quarter]
    for q in range(1, quarter):
        if 8 * q == n:
            r = math.sqrt(0.5)
            a, b = (co[q] - so[q]) * r, (co[q] + so[q]) * r
        else:
            a, b = rotate(co[q], so[q], math.cos(2 * math.pi * q / n), math.sin(2 * math.pi * q / n))
        c[q], c[half - q] = ce[q] + a, ce[q] - a
        s[q], s[half - q] = b + se[q], b - se[q]
    return c, s


def backward(c, s):
    n = 2 * (len(c) - 1)
    if n == 2:
        return [c[0] + c[1], c[0] - c[1]]
    half, quarter = n // 2, n // 4
    ce, co, se, so = [None] * (quarter + 1), [None] * (quarter + 1), {}, {}
    ce[0], co[0] = c[0] + c[half], c[0] - c[half]
    ce[quarter], co[quarter] = c[quarter], s[quarter]
    for q in range(1, quarter):
        ce[q], a = c[q] + c[half - q], c[q] - c[half - q]
        b, se[q] = s[q] + s[half - q], s[q] - s[half - q]
        if 8 * q == n:
            r = math.sqrt(0.5)
            co[q], so[q] = (a + b) * r, (b - a) * r
        else:
            co[q], so[q] = rotate(a, b, math.cos(2 * math.pi * q / n), -math.sin(2 * math.pi * q / n))
    out = [None] * n
    out[0::2], out[1::2] = backward(ce, se), backward(co, so)
    return out


def twiddles(shape, q):
    odd = lax.broadcasted_iota(jnp.int32, shape, 1) >= shape[1] // 2
    angle = 2 * math.pi * q / GRID
    return jnp.where(odd, math.cos(angle), 1.0), jnp.where(odd, math.sin(angle), 0.0)


def halves(value):
    high = value.astype(jnp.bfloat16)
    return high, (value - high.astype(jnp.float32)).astype(jnp.bfloat16)


def along_z(tiles, double, low):
    rows = jnp.concatenate(tiles, 0)
    high, rest = halves(rows)
    out = jnp.dot(jnp.concatenate([high, rest], 1), double, preferred_element_type=jnp.float32)
    out = out + jnp.dot(high, low, preferred_element_type=jnp.float32)
    step = tiles[0].shape[0]
    return [out[i * step : (i + 1) * step] for i in range(len(tiles))]


def along_x(value, double):
    length = value.shape[0]
    out = jnp.dot(double, jnp.concatenate(halves(value), 0), preferred_element_type=jnp.float32)
    return out[:length] + out[length:]


LANES = 128
PART = 2048
TABLE_PART = 512


def into_modes(densities):
    count = len(densities)
    quarter = count // 2
    c, s = forward(densities)
    for q in range(1, quarter):
        cos, sin = twiddles(densities[0].shape, q)
        c[q], s[q] = rotate(c[q], s[q], cos, sin)
    return c + [s[q] for q in range(1, quarter)]


def out_of_modes(values):
    quarter = len(values) // 2
    c, s = values[: quarter + 1], dict(enumerate(values[quarter + 1 :], 1))
    for q in range(1, quarter):
        cos, sin = twiddles(values[0].shape, q)
        c[q], s[q] = rotate(c[q], s[q], cos, -sin)
    return backward(c, s)


def filtered(tiles, table, zf2, zfl, zb2, zbl, xf, xb):
    value = along_x(jnp.concatenate(along_z(tiles, zf2, zfl), 1), xf)
    value = along_x(value * table, xb)
    return along_z([value[:, i : i + LANES] for i in range(0, value.shape[1], LANES)], zb2, zbl)


def columns(i):
    return slice(i * LANES, (i + 1) * LANES)


def exchange_kernel(orbital_ref, source_ref, filter_ref, *rest):
    constants, out_ref, work = rest
    length, cells = work.shape
    count = cells // LANES

    @pl.loop(0, length // 8)
    def _(block):
        rows = pl.ds(pl.multiple_of(block * 8, 8), 8)
        values = [
            orbital_ref[rows, columns(i)] * source_ref[0, rows, columns(i)] for i in range(count)
        ]
        for i, value in enumerate(into_modes(values)):
            work[rows, columns(i)] = value

    @pl.loop(0, cells // PART)
    def _(part):
        lanes = [pl.ds(pl.multiple_of(part * PART + i, LANES), LANES) for i in range(0, PART, LANES)]
        table = filter_ref[:, pl.ds(pl.multiple_of(part * PART, PART), PART)]
        tiles = filtered([work[:, lane] for lane in lanes], table, *unpack(constants))
        for lane, tile in zip(lanes, tiles):
            work[:, lane] = tile

    first = pl.program_id(0) == 0

    @pl.loop(0, length // 8)
    def _(block):
        rows = pl.ds(pl.multiple_of(block * 8, 8), 8)
        values = out_of_modes([work[rows, columns(i)] for i in range(count)])
        for i, value in enumerate(values):
            term = value * source_ref[0, rows, columns(i)] * -EXX_FRACTION
            out_ref[rows, columns(i)] = jnp.where(first, 0.0, out_ref[rows, columns(i)]) + term


def apply_exchange(orbital, sources):
    count, length, cells = sources.shape
    constants = jnp.asarray(matrices())
    whole = lambda shape: pl.BlockSpec(shape, lambda j: (0, 0))
    return pl.pallas_call(
        exchange_kernel,
        grid=(count,),
        out_shape=jax.ShapeDtypeStruct((length, cells), jnp.float32),
        in_specs=[
            whole((length, cells)),
            pl.BlockSpec((1, length, cells), lambda j: (j, 0, 0)),
            whole((length, cells)),
            whole(constants.shape),
        ],
        out_specs=whole((length, cells)),
        scratch_shapes=[pltpu.VMEM((length, cells), jnp.float32)],
        compiler_params=pltpu.CompilerParams(vmem_limit_bytes=32 * MIB),
        name="exchange",
    )(orbital, sources, filter_table(), constants)


GROUP = 8
PIECE = 2048
LAG = 6


def filter_part(part, length):
    shape = (length, TABLE_PART)
    half, quarter = length // 2, length // 4
    lane = lax.broadcasted_iota(jnp.int32, shape, 1) + part * TABLE_PART

    def mode(index):
        return jnp.where(index > half, index - half, index)

    row = lane >> 7
    q = jnp.where(row > quarter, row - quarter, row)
    ky = jnp.where((lane & half * 2) == 0, q, half - q)
    edge = jnp.logical_or(q == 0, q == quarter)
    squares = jnp.zeros(shape, jnp.float32)
    for k in (mode(lax.broadcasted_iota(jnp.int32, shape, 0)), ky, mode(lane & (length - 1))):
        squares = squares + (k.astype(jnp.float32) * (2.0 * math.pi / length)) ** 2
    guarded = jnp.where(squares > 0, squares, 1.0)
    table = (1.0 - jnp.exp(-guarded / (4.0 * SCREEN * SCREEN))) / guarded
    return jnp.where(squares > 0, table, 0.0) * jnp.where(edge, 1.0 / half, 2.0 / half)


def fused_kernel(chips, row, x_ref, matrix_ref, out_ref, *rest):
    (constants, source, orbital, table, work, total, copy_sem, swap_send, swap_recv, up_send, side_send, tree_recv,
     y_send, y_recv, share_send, c_send, c_recv, back_send, back_recv) = rest
    band, half = lax.axis_index("band"), lax.axis_index("fft")
    chip, core = band // 2, band % 2
    column, layer = chip % row, chip // row
    owned, planes, cells = x_ref.shape
    length = 2 * planes
    other = 1 - half
    groups, parts = planes // GROUP, cells // PIECE
    per_orbital = groups * parts
    pieces = owned * per_orbital
    root, has_up, has_down = chip == 0, chip + row < chips, layer > 0
    to_y = {"band": band, "fft": other}
    to_core = {"band": band + 1 - 2 * core, "fft": half}
    to_x = {"band": band + 2 - 4 * column, "fft": half}
    to_up = {"band": band + 2 * row, "fft": half}
    to_down = {"band": band - 2 * row, "fft": half}

    barrier = pltpu.get_barrier_semaphore()

    def greet(target):
        pl.semaphore_signal(barrier, inc=1, device_id=target, device_id_type=MESH)

    greet(to_y)
    greet(to_core)
    greet(to_x)

    @pl.when(has_up)
    def _():
        greet(to_up)

    @pl.when(has_down)
    def _():
        greet(to_down)

    pl.semaphore_wait(barrier, 3 + has_up.astype(jnp.int32) + has_down.astype(jnp.int32))

    def remote(src, dst, send, recv, target):
        return pltpu.make_async_remote_copy(
            src_ref=src, dst_ref=dst, send_sem=send, recv_sem=recv, device_id=target, device_id_type=MESH
        )

    swap = remote(x_ref.at[other], orbital.at[half], swap_send, swap_recv, to_y)
    swap.start()
    keep = pltpu.make_async_copy(x_ref.at[half], orbital.at[half], copy_sem.at[0])
    keep.start()
    fetch = pltpu.make_async_copy(matrix_ref, constants, copy_sem.at[3])
    fetch.start()

    @pl.when(root)
    def _():
        pltpu.make_async_copy(x_ref, source.at[core, :, half], copy_sem.at[1]).start()

    def place(k):
        group = (k % per_orbital) // parts
        lanes = pl.ds(pl.multiple_of((k % parts) * PIECE, PIECE), PIECE)
        return k // per_orbital, pl.ds(pl.multiple_of(group * GROUP, GROUP), GROUP), lanes

    def piece(k, source_core, source_half):
        o, rows, lanes = place(k)
        return source.at[source_core, o, source_half, rows, lanes]

    def crosses(k):
        mine = jnp.where(layer == 0, k % 4, k % 2) == 0
        return mine == (column == 0)

    def send_up(k, src):
        return remote(src, piece(k, core, half), up_send.at[k], tree_recv.at[k], to_up)

    def send_side(k, src):
        return remote(src, piece(k, core, half), side_send.at[k], tree_recv.at[k], to_x)

    def send_across(k, src):
        return remote(src, piece(k, core, half), y_send.at[k], y_recv.at[k], to_y)

    def send_beside(k, src, which, source_half):
        return remote(src, piece(k, core, source_half), c_send.at[which, k], c_recv.at[which, k], to_core)

    def send_share(k):
        block = piece(k, core, other)
        return remote(block, block, share_send.at[k], y_recv.at[k], to_x)

    def arrived(block, recv, target):
        remote(block, block, swap_send, recv, target).wait_recv()

    def relay(k, src):
        @pl.when(has_up)
        def _():
            send_up(k, src).start()

        @pl.when(crosses(k))
        def _():
            send_across(k, src).start()

    def event(k):
        @pl.when(k < pieces)
        def _():
            @pl.when(root)
            def _():
                o, rows, lanes = place(k)
                src = x_ref.at[o, rows, lanes]
                send_side(k, src).start()
                relay(k, src)
                send_beside(k, src, 0, half).start()

            @pl.when(jnp.logical_not(root))
            def _():
                src = piece(k, core, half)
                arrived(src, tree_recv.at[k], to_y)
                relay(k, src)
                send_beside(k, src, 0, half).start()

        def across(k, sharing):
            @pl.when(jnp.logical_and(jnp.logical_and(k >= 0, k < pieces), crosses(k) == sharing))
            def _():
                block = piece(k, core, other)
                arrived(block, y_recv.at[k], to_y)
                if sharing:
                    send_share(k).start()
                send_beside(k, block, 1, other).start()

        across(k - LAG // 3, True)
        across(k - 2 * LAG // 3, False)

        @pl.when(k >= LAG)
        def _():
            arrived(piece(k - LAG, 1 - core, half), c_recv.at[0, k - LAG], to_core)
            arrived(piece(k - LAG, 1 - core, other), c_recv.at[1, k - LAG], to_core)

    ahead = per_orbital + LAG
    slots = pieces - per_orbital

    @pl.loop(0, ahead)
    def _(k):
        event(k)

        @pl.when(k < cells // TABLE_PART)
        def _():
            lanes = pl.ds(pl.multiple_of(k * TABLE_PART, TABLE_PART), TABLE_PART)
            table[:, lanes] = filter_part(k, length)

    arrived(orbital.at[other], swap_recv, to_y)
    keep.wait()
    fetch.wait()

    @pl.when(root)
    def _():
        pltpu.make_async_copy(x_ref, source.at[core, :, half], copy_sem.at[1]).wait()

    def slot(index, block):
        number = index * 6 + block // 4

        @pl.when(jnp.logical_and(block % 4 == 0, number < slots))
        def _():
            event(ahead + number)

    def back(group):
        rows = pl.ds(pl.multiple_of(group * GROUP, GROUP), GROUP)
        return remote(
            total.at[other, rows], out_ref.at[half, rows], back_send.at[group], back_recv.at[group], to_y
        )

    count = cells // LANES
    last = ROUNDS * owned - 1

    @pl.loop(0, ROUNDS * owned)
    def _(index):
        b, o = index % ROUNDS, index // ROUNDS

        @pl.loop(0, 2 * groups)
        def _(block):
            slot(index, block)
            h, rows = block // groups, pl.ds(pl.multiple_of((block % groups) * GROUP, GROUP), GROUP)
            to = pl.ds(pl.multiple_of(block * GROUP, GROUP), GROUP)
            values = [
                orbital[h, rows, columns(i)] * source[b, o, h, rows, columns(i)] for i in range(count)
            ]
            for i, value in enumerate(into_modes(values)):
                work[to, columns(i)] = value

        @pl.loop(0, cells // PART)
        def _(part):
            slot(index, part * 4 + 8)
            lanes = [pl.ds(pl.multiple_of(part * PART + i, LANES), LANES) for i in range(0, PART, LANES)]
            whole = table[:, pl.ds(pl.multiple_of(part * PART, PART), PART)]
            tiles = filtered([work[:, lane] for lane in lanes], whole, *unpack(constants))
            for lane, tile in zip(lanes, tiles):
                work[:, lane] = tile

        @pl.loop(0, 2 * groups)
        def _(step):
            slot(index, step + 16)
            block = (step + groups * other) % (2 * groups)
            h, rows = block // groups, pl.ds(pl.multiple_of((block % groups) * GROUP, GROUP), GROUP)
            to = pl.ds(pl.multiple_of(block * GROUP, GROUP), GROUP)
            values = out_of_modes([work[to, columns(i)] for i in range(count)])
            for i, value in enumerate(values):
                term = value * source[b, o, h, rows, columns(i)] * -EXX_FRACTION
                total[h, rows, columns(i)] = jnp.where(index == 0, 0.0, total[h, rows, columns(i)]) + term

            @pl.when(jnp.logical_and(index == last, step < groups))
            def _():
                back(step).start()

    mine = pltpu.make_async_copy(total.at[half], out_ref.at[half], copy_sem.at[2])
    mine.start()

    @pl.loop(0, pieces)
    def _(k):
        src = piece(k, core, half)

        @pl.when(has_up)
        def _():
            send_up(k, src).wait_send()

        @pl.when(root)
        def _():
            send_side(k, src).wait_send()

        @pl.when(crosses(k))
        def _():
            send_across(k, src).wait_send()
            send_share(k).wait_send()

        send_beside(k, src, 0, half).wait_send()
        send_beside(k, src, 1, half).wait_send()

    swap.wait_send()

    @pl.loop(0, groups)
    def _(group):
        back(group).wait_send()
        rows = pl.ds(pl.multiple_of(group * GROUP, GROUP), GROUP)
        arrived(out_ref.at[other, rows], back_recv.at[group], to_y)

    mine.wait()


def two_halves(bands, row, orbitals):
    owned, planes, cells = orbitals.shape
    count = owned * (planes // GROUP) * (cells // PIECE)
    dma = pltpu.SemaphoreType.DMA
    constants = jnp.asarray(matrices())
    grid = lambda *lead: pltpu.VMEM((*lead, planes, cells), jnp.float32)
    flat = pltpu.VMEM((2 * planes, cells), jnp.float32)
    return pl.pallas_call(
        functools.partial(fused_kernel, bands // 2, row),
        out_shape=jax.ShapeDtypeStruct(orbitals.shape, jnp.float32),
        in_specs=[pl.BlockSpec(memory_space=pl.ANY)] * 2,
        out_specs=pl.BlockSpec(memory_space=pl.ANY),
        scratch_shapes=[pltpu.VMEM(constants.shape, jnp.bfloat16), grid(ROUNDS, owned, 2), grid(2), flat, flat, grid(2)]
        + [dma((4,)), dma, dma]
        + [dma((count,))] * 6
        + [dma((2, count))] * 2
        + [dma((planes // GROUP,))] * 2,
        compiler_params=pltpu.CompilerParams(
            collective_id=0, has_side_effects=True, vmem_limit_bytes=60 * MIB
        ),
        name="exchange",
    )(orbitals, constants)


def many_parts(parts, orbitals):
    owned = orbitals.shape[0]
    place, band = lax.axis_index("fft"), lax.axis_index("band")
    fields = lax.all_gather(orbitals, "fft", axis=1, tiled=True)
    held = jnp.concatenate([jnp.where(band == r, fields, 0.0) for r in range(ROUNDS)], 0)
    sources = lax.psum(held, "band")
    groups = max(parts // owned, 1)
    share = sources.shape[0] // groups
    mine = lax.dynamic_slice_in_dim(sources, (place // owned) * share, share, 0)
    which = place % owned
    result = apply_exchange(lax.dynamic_index_in_dim(fields, which, 0, False), mine)
    placed = jnp.where(jnp.arange(owned)[:, None, None] == which, result[None], 0.0)
    return lax.psum_scatter(placed, "fft", scatter_dimension=1, tiled=True)


def solution(mesh):
    parts = mesh.shape["fft"]
    if parts == 2:
        body = functools.partial(two_halves, mesh.shape["band"], 2)
    else:
        body = functools.partial(many_parts, parts)
    return jax.shard_map(
        body, mesh=mesh, in_specs=(P("band", "fft", None),), out_specs=P("band", "fft", None), check_vma=False
    )
```

```python
import functools
import math

import jax
import jax.numpy as jnp
import numpy as np
from jax import lax
from jax.experimental import pallas as pl
from jax.experimental.pallas import tpu as pltpu
from jax.sharding import PartitionSpec as P

GRID = 64
ROUNDS = 2
EXX_FRACTION = 0.25
SCREEN = 0.05
MESH = pl.DeviceIdType.MESH
MIB = 1024 * 1024


def real_modes(length):
    n = np.arange(length)
    rows = [np.cos(2 * np.pi * q * n / length) for q in range(length // 2 + 1)]
    rows += [np.sin(2 * np.pi * q * n / length) for q in range(1, length // 2)]
    matrix = np.array(rows)
    return matrix / np.sqrt((matrix**2).sum(1, keepdims=True))


def split(matrix):
    high = matrix.astype(jnp.bfloat16)
    return high, (matrix - high.astype(np.float64)).astype(jnp.bfloat16)


def matrices():
    modes = real_modes(GRID)
    z_forward = np.kron(np.array([[1.0, 1.0], [1.0, -1.0]]) / np.sqrt(2.0), modes.T)
    out = []
    for matrix in (z_forward, z_forward.T):
        high, low = split(matrix)
        out += [np.concatenate([high, high], 0), low]
    for matrix in (modes, modes.T):
        high, low = split(matrix)
        out.append(
            np.concatenate(
                [np.concatenate([high, high], 1), np.concatenate([low, np.zeros_like(low)], 1)], 0
            )
        )
    return np.concatenate(out, 0)


def unpack(ref):
    out, start = [], 0
    for rows in (256, 128, 256, 128, 128, 128):
        out.append(ref[start : start + rows, :])
        start += rows
    return out


def mode_numbers():
    half = GRID // 2
    return np.concatenate([np.arange(half + 1), np.arange(1, half)])


def filter_table():
    k = jnp.asarray(mode_numbers(), jnp.float32)
    quarter = GRID // 4
    q = np.concatenate([np.arange(quarter + 1), np.arange(1, quarter)])
    weight = np.where((q == 0) | (q == quarter), 1.0, 2.0) / (GRID // 2)
    ky = jnp.asarray(np.stack([q, GRID // 2 - q], 1), jnp.float32)
    unit = 2.0 * math.pi / GRID
    squares = (
        (k * unit)[:, None, None, None] ** 2
        + (ky * unit)[None, :, :, None] ** 2
        + (k * unit)[None, None, None, :] ** 2
    )
    guarded = jnp.where(squares > 0, squares, 1.0)
    table = jnp.where(
        squares > 0, (1.0 - jnp.exp(-guarded / (4.0 * SCREEN * SCREEN))) / guarded, 0.0
    )
    table = table * jnp.asarray(weight, jnp.float32)[None, :, None, None]
    return table.reshape(GRID, GRID * GRID)


def rotate(c, s, cos, sin):
    return cos * c - sin * s, sin * c + cos * s


def forward(x):
    n = len(x)
    if n == 2:
        return [x[0] + x[1], x[0] - x[1]], {}
    ce, se = forward(x[0::2])
    co, so = forward(x[1::2])
    half, quarter = n // 2, n // 4
    c, s = [None] * (half + 1), {}
    c[0], c[half] = ce[0] + co[0], ce[0] - co[0]
    c[quarter], s[quarter] = ce[quarter], co[quarter]
    for q in range(1, quarter):
        if 8 * q == n:
            r = math.sqrt(0.5)
            a, b = (co[q] - so[q]) * r, (co[q] + so[q]) * r
        else:
            a, b = rotate(co[q], so[q], math.cos(2 * math.pi * q / n), math.sin(2 * math.pi * q / n))
        c[q], c[half - q] = ce[q] + a, ce[q] - a
        s[q], s[half - q] = b + se[q], b - se[q]
    return c, s


def backward(c, s):
    n = 2 * (len(c) - 1)
    if n == 2:
        return [c[0] + c[1], c[0] - c[1]]
    half, quarter = n // 2, n // 4
    ce, co, se, so = [None] * (quarter + 1), [None] * (quarter + 1), {}, {}
    ce[0], co[0] = c[0] + c[half], c[0] - c[half]
    ce[quarter], co[quarter] = c[quarter], s[quarter]
    for q in range(1, quarter):
        ce[q], a = c[q] + c[half - q], c[q] - c[half - q]
        b, se[q] = s[q] + s[half - q], s[q] - s[half - q]
        if 8 * q == n:
            r = math.sqrt(0.5)
            co[q], so[q] = (a + b) * r, (b - a) * r
        else:
            co[q], so[q] = rotate(a, b, math.cos(2 * math.pi * q / n), -math.sin(2 * math.pi * q / n))
    out = [None] * n
    out[0::2], out[1::2] = backward(ce, se), backward(co, so)
    return out


def twiddles(shape, q):
    odd = lax.broadcasted_iota(jnp.int32, shape, 1) >= shape[1] // 2
    angle = 2 * math.pi * q / GRID
    return jnp.where(odd, math.cos(angle), 1.0), jnp.where(odd, math.sin(angle), 0.0)


def halves(value):
    high = value.astype(jnp.bfloat16)
    return high, (value - high.astype(jnp.float32)).astype(jnp.bfloat16)


def along_z(tiles, double, low):
    rows = jnp.concatenate(tiles, 0)
    high, rest = halves(rows)
    out = jnp.dot(jnp.concatenate([high, rest], 1), double, preferred_element_type=jnp.float32)
    out = out + jnp.dot(high, low, preferred_element_type=jnp.float32)
    step = tiles[0].shape[0]
    return [out[i * step : (i + 1) * step] for i in range(len(tiles))]


def along_x(value, double):
    length = value.shape[0]
    out = jnp.dot(double, jnp.concatenate(halves(value), 0), preferred_element_type=jnp.float32)
    return out[:length] + out[length:]


LANES = 128
PART = 2048
TABLE_PART = 512


def into_modes(densities):
    count = len(densities)
    quarter = count // 2
    c, s = forward(densities)
    for q in range(1, quarter):
        cos, sin = twiddles(densities[0].shape, q)
        c[q], s[q] = rotate(c[q], s[q], cos, sin)
    return c + [s[q] for q in range(1, quarter)]


def out_of_modes(values):
    quarter = len(values) // 2
    c, s = values[: quarter + 1], dict(enumerate(values[quarter + 1 :], 1))
    for q in range(1, quarter):
        cos, sin = twiddles(values[0].shape, q)
        c[q], s[q] = rotate(c[q], s[q], cos, -sin)
    return backward(c, s)


def filtered(tiles, table, zf2, zfl, zb2, zbl, xf, xb):
    value = along_x(jnp.concatenate(along_z(tiles, zf2, zfl), 1), xf)
    value = along_x(value * table, xb)
    return along_z([value[:, i : i + LANES] for i in range(0, value.shape[1], LANES)], zb2, zbl)


def columns(i):
    return slice(i * LANES, (i + 1) * LANES)


def exchange_kernel(orbital_ref, source_ref, filter_ref, *rest):
    constants, out_ref, work = rest
    length, cells = work.shape
    count = cells // LANES

    @pl.loop(0, length // 8)
    def _(block):
        rows = pl.ds(pl.multiple_of(block * 8, 8), 8)
        values = [
            orbital_ref[rows, columns(i)] * source_ref[0, rows, columns(i)] for i in range(count)
        ]
        for i, value in enumerate(into_modes(values)):
            work[rows, columns(i)] = value

    @pl.loop(0, cells // PART)
    def _(part):
        lanes = [pl.ds(pl.multiple_of(part * PART + i, LANES), LANES) for i in range(0, PART, LANES)]
        table = filter_ref[:, pl.ds(pl.multiple_of(part * PART, PART), PART)]
        tiles = filtered([work[:, lane] for lane in lanes], table, *unpack(constants))
        for lane, tile in zip(lanes, tiles):
            work[:, lane] = tile

    first = pl.program_id(0) == 0

    @pl.loop(0, length // 8)
    def _(block):
        rows = pl.ds(pl.multiple_of(block * 8, 8), 8)
        values = out_of_modes([work[rows, columns(i)] for i in range(count)])
        for i, value in enumerate(values):
            term = value * source_ref[0, rows, columns(i)] * -EXX_FRACTION
            out_ref[rows, columns(i)] = jnp.where(first, 0.0, out_ref[rows, columns(i)]) + term


def apply_exchange(orbital, sources):
    count, length, cells = sources.shape
    constants = jnp.asarray(matrices())
    whole = lambda shape: pl.BlockSpec(shape, lambda j: (0, 0))
    return pl.pallas_call(
        exchange_kernel,
        grid=(count,),
        out_shape=jax.ShapeDtypeStruct((length, cells), jnp.float32),
        in_specs=[
            whole((length, cells)),
            pl.BlockSpec((1, length, cells), lambda j: (j, 0, 0)),
            whole((length, cells)),
            whole(constants.shape),
        ],
        out_specs=whole((length, cells)),
        scratch_shapes=[pltpu.VMEM((length, cells), jnp.float32)],
        compiler_params=pltpu.CompilerParams(vmem_limit_bytes=32 * MIB),
        name="exchange",
    )(orbital, sources, filter_table(), constants)


GROUP = 8
COLUMNS = 4
LAG = 2
TABLE_PART = 512


def filter_part(part, length):
    shape = (length, TABLE_PART)
    half, quarter = length // 2, length // 4
    lane = lax.broadcasted_iota(jnp.int32, shape, 1) + part * TABLE_PART

    def mode(index):
        return jnp.where(index > half, index - half, index)

    row = lane >> 7
    q = jnp.where(row > quarter, row - quarter, row)
    ky = jnp.where((lane & half * 2) == 0, q, half - q)
    edge = jnp.logical_or(q == 0, q == quarter)
    squares = jnp.zeros(shape, jnp.float32)
    for k in (mode(lax.broadcasted_iota(jnp.int32, shape, 0)), ky, mode(lane & (length - 1))):
        squares = squares + (k.astype(jnp.float32) * (2.0 * math.pi / length)) ** 2
    guarded = jnp.where(squares > 0, squares, 1.0)
    table = (1.0 - jnp.exp(-guarded / (4.0 * SCREEN * SCREEN))) / guarded
    return jnp.where(squares > 0, table, 0.0) * jnp.where(edge, 1.0 / half, 2.0 / half)


def fused_kernel(chips, row, x_ref, matrix_ref, out_ref, *rest):
    (constants, source, orbital, table, work, total, copy_sem, swap_send, swap_recv, local_sem, scatter_send,
     up_send, y_send, x_send, c_send, own_recv, y_recv, x_recv, d_recv, c_recv, back_send, back_recv) = rest
    band, half = lax.axis_index("band"), lax.axis_index("fft")
    chip, core = band // 2, band % 2
    side, layer = chip % row, chip // row
    owned, planes, cells = x_ref.shape
    length = 2 * planes
    other = 1 - half
    groups, width = planes // GROUP, cells // COLUMNS
    per_orbital = 2 * groups
    pieces = owned * per_orbital
    root, has_up, has_down = chip == 0, chip + row < chips, layer > 0
    across_band = band + 2 - 4 * side
    to_y = {"band": band, "fft": other}
    to_core = {"band": band + 1 - 2 * core, "fft": half}
    to_x = {"band": across_band, "fft": half}
    to_diagonal = {"band": across_band, "fft": other}
    to_up = {"band": band + 2 * row, "fft": half}
    to_down = {"band": band - 2 * row, "fft": half}
    own = 2 * side + half
    over_y, over_x, over_both = own + 1 - 2 * half, own + 2 - 4 * side, 3 - own

    barrier = pltpu.get_barrier_semaphore()

    def greet(target):
        pl.semaphore_signal(barrier, inc=1, device_id=target, device_id_type=MESH)

    greet(to_y)
    greet(to_core)
    greet(to_x)

    @pl.when(has_up)
    def _():
        greet(to_up)

    @pl.when(has_down)
    def _():
        greet(to_down)

    @pl.when(layer == 0)
    def _():
        greet(to_diagonal)

    pl.semaphore_wait(barrier, 4 + has_up.astype(jnp.int32))

    def remote(src, dst, send, recv, target):
        return pltpu.make_async_remote_copy(
            src_ref=src, dst_ref=dst, send_sem=send, recv_sem=recv, device_id=target, device_id_type=MESH
        )

    def arrived(block, recv):
        remote(block, block, swap_send, recv, to_y).wait_recv()

    def sent(block, send):
        remote(block, block, send, swap_recv, to_y).wait_send()

    def place(q, column):
        rows = pl.ds(pl.multiple_of((q % per_orbital) // 2 * GROUP, GROUP), GROUP)
        return q // per_orbital, q % 2, rows, pl.ds(pl.multiple_of(column * width, width), width)

    def piece(q, column, source_core=core):
        o, h, rows, lanes = place(q, column)
        return source.at[source_core, o, h, rows, lanes]

    def outer(q, column):
        o, _, rows, lanes = place(q, column)
        return x_ref.at[o, rows, lanes]

    def local(q):
        return pltpu.make_async_copy(outer(q, own), piece(q, own), local_sem.at[q])

    swap = remote(x_ref.at[other], orbital.at[half], swap_send, swap_recv, to_y)
    swap.start()

    @pl.when(root)
    def _():
        @pl.loop(0, pieces)
        def _(q):
            @pl.when(q % 2 == half)
            def _():
                for i, (column, target) in enumerate(
                    ((over_x, to_x), (over_both, to_diagonal), (over_y, to_y))
                ):
                    remote(
                        outer(q, column), piece(q, column), scatter_send.at[i], own_recv.at[q], target
                    ).start()
                local(q).start()

    keep = pltpu.make_async_copy(x_ref.at[half], orbital.at[half], copy_sem.at[0])
    keep.start()
    fetch = pltpu.make_async_copy(matrix_ref, constants, copy_sem.at[1])
    fetch.start()

    def send(block, send_sem, recv_sem, target):
        remote(block, block, send_sem, recv_sem, target).start()

    def within(q):
        return jnp.logical_and(q >= 0, q < pieces)

    def beside(q, block):
        send(block, c_send, c_recv.at[q // per_orbital], to_core)

    def event(k):
        @pl.when(k < pieces)
        def _():
            block = piece(k, own)
            at_home = jnp.logical_and(root, k % 2 == half)

            @pl.when(at_home)
            def _():
                local(k).wait()

            @pl.when(jnp.logical_not(at_home))
            def _():
                arrived(block, own_recv.at[k])

            @pl.when(has_up)
            def _():
                send(block, up_send, own_recv.at[k], to_up)

            send(block, y_send, y_recv.at[k], to_y)
            send(block, x_send, x_recv.at[k], to_x)
            beside(k, block)

        q = k - LAG

        @pl.when(within(q))
        def _():
            block = piece(q, over_y)
            arrived(block, y_recv.at[q])
            send(block, x_send, d_recv.at[q], to_x)
            beside(q, block)
            block = piece(q, over_x)
            arrived(block, x_recv.at[q])
            beside(q, block)

        r = k - 2 * LAG

        @pl.when(within(r))
        def _():
            block = piece(r, over_both)
            arrived(block, d_recv.at[r])
            beside(r, block)

    ahead = per_orbital + 2 * LAG
    slots = pieces - per_orbital

    @pl.loop(0, ahead)
    def _(k):
        event(k)

        @pl.when(k < cells // TABLE_PART)
        def _():
            lanes = pl.ds(pl.multiple_of(k * TABLE_PART, TABLE_PART), TABLE_PART)
            table[:, lanes] = filter_part(k, length)

    arrived(orbital.at[other], swap_recv)
    keep.wait()
    fetch.wait()

    def slot(index, block):
        number = index * 6 + block // 4

        @pl.when(jnp.logical_and(block % 4 == 0, number < slots))
        def _():
            event(ahead + number)

    def back(group):
        rows = pl.ds(pl.multiple_of(group * GROUP, GROUP), GROUP)
        return remote(total.at[other, rows], out_ref.at[half, rows], back_send, back_recv, to_y)

    count = cells // LANES
    last = ROUNDS * owned - 1

    @pl.loop(0, ROUNDS * owned)
    def _(index):
        b, o = index % ROUNDS, index // ROUNDS

        @pl.when(b == 0)
        def _():
            arrived(source.at[1 - core, o], c_recv.at[o])

        @pl.loop(0, 2 * groups)
        def _(block):
            slot(index, block)
            h, rows = block // groups, pl.ds(pl.multiple_of((block % groups) * GROUP, GROUP), GROUP)
            to = pl.ds(pl.multiple_of(block * GROUP, GROUP), GROUP)
            values = [
                orbital[h, rows, columns(i)] * source[b, o, h, rows, columns(i)] for i in range(count)
            ]
            for i, value in enumerate(into_modes(values)):
                work[to, columns(i)] = value

        @pl.loop(0, cells // PART)
        def _(part):
            slot(index, part * 4 + 8)
            lanes = [pl.ds(pl.multiple_of(part * PART + i, LANES), LANES) for i in range(0, PART, LANES)]
            whole = table[:, pl.ds(pl.multiple_of(part * PART, PART), PART)]
            tiles = filtered([work[:, lane] for lane in lanes], whole, *unpack(constants))
            for lane, tile in zip(lanes, tiles):
                work[:, lane] = tile

        @pl.loop(0, 2 * groups)
        def _(step):
            slot(index, step + 16)
            block = (step + groups * other) % (2 * groups)
            h, rows = block // groups, pl.ds(pl.multiple_of((block % groups) * GROUP, GROUP), GROUP)
            to = pl.ds(pl.multiple_of(block * GROUP, GROUP), GROUP)
            values = out_of_modes([work[to, columns(i)] for i in range(count)])
            for i, value in enumerate(values):
                term = value * source[b, o, h, rows, columns(i)] * -EXX_FRACTION
                total[h, rows, columns(i)] = jnp.where(index == 0, 0.0, total[h, rows, columns(i)]) + term

            @pl.when(jnp.logical_and(index == last, step < groups))
            def _():
                back(step).start()

    mine = pltpu.make_async_copy(total.at[half], out_ref.at[half], copy_sem.at[2])
    mine.start()

    @pl.when(has_up)
    def _():
        sent(orbital.at[0], up_send)

    @pl.when(root)
    def _():
        for i in range(3):
            sent(orbital.at[0, : planes // 2], scatter_send.at[i])

    sent(orbital.at[0], y_send)
    sent(orbital, x_send)
    sent(source.at[core], c_send)
    swap.wait_send()
    sent(total.at[other], back_send)
    mine.wait()
    arrived(out_ref.at[other], back_recv)


def two_halves(bands, row, orbitals):
    owned, planes, cells = orbitals.shape
    count = owned * 2 * (planes // GROUP)
    dma = pltpu.SemaphoreType.DMA
    constants = jnp.asarray(matrices())
    grid = lambda *lead: pltpu.VMEM((*lead, planes, cells), jnp.float32)
    flat = pltpu.VMEM((2 * planes, cells), jnp.float32)
    return pl.pallas_call(
        functools.partial(fused_kernel, bands // 2, row),
        out_shape=jax.ShapeDtypeStruct(orbitals.shape, jnp.float32),
        in_specs=[pl.BlockSpec(memory_space=pl.ANY)] * 2,
        out_specs=pl.BlockSpec(memory_space=pl.ANY),
        scratch_shapes=[pltpu.VMEM(constants.shape, jnp.bfloat16), grid(ROUNDS, owned, 2), grid(2), flat, flat, grid(2)]
        + [dma((3,)), dma, dma, dma((count,)), dma((3,))]
        + [dma] * 4
        + [dma((count,))] * 4
        + [dma((owned,)), dma, dma],
        compiler_params=pltpu.CompilerParams(
            collective_id=0, has_side_effects=True, vmem_limit_bytes=60 * MIB
        ),
        name="exchange",
    )(orbitals, constants)


def many_parts(parts, orbitals):
    owned = orbitals.shape[0]
    place, band = lax.axis_index("fft"), lax.axis_index("band")
    fields = lax.all_gather(orbitals, "fft", axis=1, tiled=True)
    held = jnp.concatenate([jnp.where(band == r, fields, 0.0) for r in range(ROUNDS)], 0)
    sources = lax.psum(held, "band")
    groups = max(parts // owned, 1)
    share = sources.shape[0] // groups
    mine = lax.dynamic_slice_in_dim(sources, (place // owned) * share, share, 0)
    which = place % owned
    result = apply_exchange(lax.dynamic_index_in_dim(fields, which, 0, False), mine)
    placed = jnp.where(jnp.arange(owned)[:, None, None] == which, result[None], 0.0)
    return lax.psum_scatter(placed, "fft", scatter_dimension=1, tiled=True)


def solution(mesh):
    parts = mesh.shape["fft"]
    if parts == 2:
        body = functools.partial(two_halves, mesh.shape["band"], 2)
    else:
        body = functools.partial(many_parts, parts)
    return jax.shard_map(
        body, mesh=mesh, in_specs=(P("band", "fft", None),), out_specs=P("band", "fft", None), check_vma=False
    )
```

```python
import functools
import math

import jax
import jax.numpy as jnp
import numpy as np
from jax import lax
from jax.experimental import pallas as pl
from jax.experimental.pallas import tpu as pltpu
from jax.sharding import PartitionSpec as P

GRID = 64
ROUNDS = 2
EXX_FRACTION = 0.25
SCREEN = 0.05
MESH = pl.DeviceIdType.MESH
MIB = 1024 * 1024


def real_modes(length):
    n = np.arange(length)
    rows = [np.cos(2 * np.pi * q * n / length) for q in range(length // 2 + 1)]
    rows += [np.sin(2 * np.pi * q * n / length) for q in range(1, length // 2)]
    matrix = np.array(rows)
    return matrix / np.sqrt((matrix**2).sum(1, keepdims=True))


def split(matrix):
    high = matrix.astype(jnp.bfloat16)
    return high, (matrix - high.astype(np.float64)).astype(jnp.bfloat16)


def matrices():
    modes = real_modes(GRID)
    z_forward = np.kron(np.array([[1.0, 1.0], [1.0, -1.0]]) / np.sqrt(2.0), modes.T)
    out = []
    for matrix in (z_forward, z_forward.T):
        high, low = split(matrix)
        out += [np.concatenate([high, high], 0), np.concatenate([low, np.zeros_like(low)], 0)]
    for matrix in (modes, modes.T):
        high, low = split(matrix)
        out.append(
            np.concatenate(
                [np.concatenate([high, high], 1), np.concatenate([low, np.zeros_like(low)], 1)], 0
            )
        )
    return np.concatenate(out, 0)


def unpack(ref):
    sides = [ref[i * 256 : (i + 1) * 256, :] for i in range(4)]
    across = [ref[1024 + i * 128 : 1152 + i * 128, :] for i in range(2)]
    return [jnp.concatenate(sides[:2], 1), jnp.concatenate(sides[2:], 1)] + across


def mode_numbers():
    half = GRID // 2
    return np.concatenate([np.arange(half + 1), np.arange(1, half)])


def filter_table():
    k = jnp.asarray(mode_numbers(), jnp.float32)
    quarter = GRID // 4
    q = np.concatenate([np.arange(quarter + 1), np.arange(1, quarter)])
    weight = np.where((q == 0) | (q == quarter), 1.0, 2.0) / (GRID // 2)
    ky = jnp.asarray(np.stack([q, GRID // 2 - q], 1), jnp.float32)
    unit = 2.0 * math.pi / GRID
    squares = (
        (k * unit)[:, None, None, None] ** 2
        + (ky * unit)[None, :, :, None] ** 2
        + (k * unit)[None, None, None, :] ** 2
    )
    guarded = jnp.where(squares > 0, squares, 1.0)
    table = jnp.where(
        squares > 0, (1.0 - jnp.exp(-guarded / (4.0 * SCREEN * SCREEN))) / guarded, 0.0
    )
    table = table * jnp.asarray(weight, jnp.float32)[None, :, None, None]
    return table.reshape(GRID, GRID * GRID)


def rotate(c, s, cos, sin):
    return cos * c - sin * s, sin * c + cos * s


def forward(x):
    n = len(x)
    if n == 2:
        return [x[0] + x[1], x[0] - x[1]], {}
    ce, se = forward(x[0::2])
    co, so = forward(x[1::2])
    half, quarter = n // 2, n // 4
    c, s = [None] * (half + 1), {}
    c[0], c[half] = ce[0] + co[0], ce[0] - co[0]
    c[quarter], s[quarter] = ce[quarter], co[quarter]
    for q in range(1, quarter):
        if 8 * q == n:
            r = math.sqrt(0.5)
            a, b = (co[q] - so[q]) * r, (co[q] + so[q]) * r
        else:
            a, b = rotate(co[q], so[q], math.cos(2 * math.pi * q / n), math.sin(2 * math.pi * q / n))
        c[q], c[half - q] = ce[q] + a, ce[q] - a
        s[q], s[half - q] = b + se[q], b - se[q]
    return c, s


def backward(c, s):
    n = 2 * (len(c) - 1)
    if n == 2:
        return [c[0] + c[1], c[0] - c[1]]
    half, quarter = n // 2, n // 4
    ce, co, se, so = [None] * (quarter + 1), [None] * (quarter + 1), {}, {}
    ce[0], co[0] = c[0] + c[half], c[0] - c[half]
    ce[quarter], co[quarter] = c[quarter], s[quarter]
    for q in range(1, quarter):
        ce[q], a = c[q] + c[half - q], c[q] - c[half - q]
        b, se[q] = s[q] + s[half - q], s[q] - s[half - q]
        if 8 * q == n:
            r = math.sqrt(0.5)
            co[q], so[q] = (a + b) * r, (b - a) * r
        else:
            co[q], so[q] = rotate(a, b, math.cos(2 * math.pi * q / n), -math.sin(2 * math.pi * q / n))
    out = [None] * n
    out[0::2], out[1::2] = backward(ce, se), backward(co, so)
    return out


def twiddles(shape, q):
    odd = lax.broadcasted_iota(jnp.int32, shape, 1) >= shape[1] // 2
    angle = 2 * math.pi * q / GRID
    return jnp.where(odd, math.cos(angle), 1.0), jnp.where(odd, math.sin(angle), 0.0)


def halves(value):
    high = value.astype(jnp.bfloat16)
    return high, (value - high.astype(jnp.float32)).astype(jnp.bfloat16)


def along_z(tiles, double):
    high, rest = halves(jnp.concatenate(tiles, 0))
    out = jnp.dot(jnp.concatenate([high, rest], 1), double, preferred_element_type=jnp.float32)
    out = out[:, :LANES] + out[:, LANES:]
    step = tiles[0].shape[0]
    return [out[i * step : (i + 1) * step] for i in range(len(tiles))]


def along_x(value, double):
    length = value.shape[0]
    out = jnp.dot(double, jnp.concatenate(halves(value), 0), preferred_element_type=jnp.float32)
    return out[:length] + out[length:]


LANES = 128
PART = 2048
TABLE_PART = 512


def into_modes(densities):
    count = len(densities)
    quarter = count // 2
    c, s = forward(densities)
    for q in range(1, quarter):
        cos, sin = twiddles(densities[0].shape, q)
        c[q], s[q] = rotate(c[q], s[q], cos, sin)
    return c + [s[q] for q in range(1, quarter)]


def out_of_modes(values):
    quarter = len(values) // 2
    c, s = values[: quarter + 1], dict(enumerate(values[quarter + 1 :], 1))
    for q in range(1, quarter):
        cos, sin = twiddles(values[0].shape, q)
        c[q], s[q] = rotate(c[q], s[q], cos, -sin)
    return backward(c, s)


def filtered(tiles, table, z_forward, z_backward, x_forward, x_backward):
    value = along_x(jnp.concatenate(along_z(tiles, z_forward), 1), x_forward)
    value = along_x(value * table, x_backward)
    return along_z([value[:, i : i + LANES] for i in range(0, value.shape[1], LANES)], z_backward)


def columns(i):
    return slice(i * LANES, (i + 1) * LANES)


def exchange_kernel(orbital_ref, source_ref, filter_ref, *rest):
    constants, out_ref, work = rest
    length, cells = work.shape
    count = cells // LANES

    @pl.loop(0, length // 8)
    def _(block):
        rows = pl.ds(pl.multiple_of(block * 8, 8), 8)
        values = [
            orbital_ref[rows, columns(i)] * source_ref[0, rows, columns(i)] for i in range(count)
        ]
        for i, value in enumerate(into_modes(values)):
            work[rows, columns(i)] = value

    @pl.loop(0, cells // PART)
    def _(part):
        lanes = [pl.ds(pl.multiple_of(part * PART + i, LANES), LANES) for i in range(0, PART, LANES)]
        table = filter_ref[:, pl.ds(pl.multiple_of(part * PART, PART), PART)]
        tiles = filtered([work[:, lane] for lane in lanes], table, *unpack(constants))
        for lane, tile in zip(lanes, tiles):
            work[:, lane] = tile

    first = pl.program_id(0) == 0

    @pl.loop(0, length // 8)
    def _(block):
        rows = pl.ds(pl.multiple_of(block * 8, 8), 8)
        values = out_of_modes([work[rows, columns(i)] for i in range(count)])
        for i, value in enumerate(values):
            term = value * source_ref[0, rows, columns(i)] * -EXX_FRACTION
            out_ref[rows, columns(i)] = jnp.where(first, 0.0, out_ref[rows, columns(i)]) + term


def apply_exchange(orbital, sources):
    count, length, cells = sources.shape
    constants = jnp.asarray(matrices())
    whole = lambda shape: pl.BlockSpec(shape, lambda j: (0, 0))
    return pl.pallas_call(
        exchange_kernel,
        grid=(count,),
        out_shape=jax.ShapeDtypeStruct((length, cells), jnp.float32),
        in_specs=[
            whole((length, cells)),
            pl.BlockSpec((1, length, cells), lambda j: (j, 0, 0)),
            whole((length, cells)),
            whole(constants.shape),
        ],
        out_specs=whole((length, cells)),
        scratch_shapes=[pltpu.VMEM((length, cells), jnp.float32)],
        compiler_params=pltpu.CompilerParams(vmem_limit_bytes=32 * MIB),
        name="exchange",
    )(orbital, sources, filter_table(), constants)


GROUP = 8
COLUMNS = 4
LAG = 2
START = 8
TABLE_PART = 512


def filter_part(part, length):
    shape = (length, TABLE_PART)
    half, quarter = length // 2, length // 4
    lane = lax.broadcasted_iota(jnp.int32, shape, 1) + part * TABLE_PART

    def mode(index):
        return jnp.where(index > half, index - half, index)

    row = lane >> 7
    q = jnp.where(row > quarter, row - quarter, row)
    ky = jnp.where((lane & half * 2) == 0, q, half - q)
    edge = jnp.logical_or(q == 0, q == quarter)
    squares = jnp.zeros(shape, jnp.float32)
    for k in (mode(lax.broadcasted_iota(jnp.int32, shape, 0)), ky, mode(lane & (length - 1))):
        squares = squares + (k.astype(jnp.float32) * (2.0 * math.pi / length)) ** 2
    guarded = jnp.where(squares > 0, squares, 1.0)
    table = (1.0 - jnp.exp(-guarded / (4.0 * SCREEN * SCREEN))) / guarded
    return jnp.where(squares > 0, table, 0.0) * jnp.where(edge, 1.0 / half, 2.0 / half)


def fused_kernel(chips, row, x_ref, matrix_ref, out_ref, *rest):
    (constants, source, orbital, table, work, total, partial, copy_sem, swap_send, swap_recv, beside_send,
     beside_recv, local_sem, scatter_send, up_send, y_send, x_send, own_recv, y_recv, x_recv, d_recv,
     part_send, part_recv, back_send, back_recv, done_send, done_recv) = rest
    band, half = lax.axis_index("band"), lax.axis_index("fft")
    chip, core = band // 2, band % 2
    side, layer = chip % row, chip // row
    owned, planes, cells = x_ref.shape
    length = 2 * planes
    other = 1 - half
    groups, width = planes // GROUP, cells // COLUMNS
    share = groups // 2
    per_orbital = 2 * groups
    pieces = owned * per_orbital
    root, has_up, has_down = chip == 0, chip + row < chips, layer > 0
    across_band, beside_band = band + 2 - 4 * side, band + 1 - 2 * core
    to_y = {"band": band, "fft": other}
    to_core = {"band": beside_band, "fft": half}
    to_cross = {"band": beside_band, "fft": other}
    to_x = {"band": across_band, "fft": half}
    to_diagonal = {"band": across_band, "fft": other}
    to_up = {"band": band + 2 * row, "fft": half}
    to_down = {"band": band - 2 * row, "fft": half}
    own = 2 * side + half
    over_y, over_x, over_both = own + 1 - 2 * half, own + 2 - 4 * side, 3 - own

    barrier = pltpu.get_barrier_semaphore()

    def greet(target):
        pl.semaphore_signal(barrier, inc=1, device_id=target, device_id_type=MESH)

    greet(to_y)
    greet(to_core)
    greet(to_cross)
    greet(to_x)

    @pl.when(has_up)
    def _():
        greet(to_up)

    @pl.when(has_down)
    def _():
        greet(to_down)

    @pl.when(layer == 0)
    def _():
        greet(to_diagonal)

    pl.semaphore_wait(barrier, 5 + has_up.astype(jnp.int32))

    def remote(src, dst, send, recv, target):
        return pltpu.make_async_remote_copy(
            src_ref=src, dst_ref=dst, send_sem=send, recv_sem=recv, device_id=target, device_id_type=MESH
        )

    def send(block, send_sem, recv_sem, target):
        remote(block, block, send_sem, recv_sem, target).start()

    def arrived(block, recv):
        remote(block, block, swap_send, recv, to_y).wait_recv()

    def sent(block, send_sem):
        remote(block, block, send_sem, swap_recv, to_y).wait_send()

    def group_rows(group):
        return pl.ds(pl.multiple_of(group * GROUP, GROUP), GROUP)

    def place(q, column):
        rows = group_rows((q % per_orbital) // 2)
        return q // per_orbital, q % 2, rows, pl.ds(pl.multiple_of(column * width, width), width)

    def piece(q, column):
        return source.at[place(q, column)]

    def outer(q, column):
        o, _, rows, lanes = place(q, column)
        return x_ref.at[o, rows, lanes]

    def local(q):
        return pltpu.make_async_copy(outer(q, own), piece(q, own), local_sem.at[q])

    swap = remote(x_ref.at[other], orbital.at[core, half], swap_send, swap_recv, to_y)
    swap.start()

    @pl.when(root)
    def _():
        @pl.loop(0, pieces)
        def _(q):
            @pl.when(q % 2 == half)
            def _():
                for i, (column, target) in enumerate(
                    ((over_x, to_x), (over_both, to_diagonal), (over_y, to_y))
                ):
                    remote(
                        outer(q, column), piece(q, column), scatter_send.at[i], own_recv.at[q], target
                    ).start()
                local(q).start()

    remote(x_ref.at[half], orbital.at[core, half], beside_send.at[0], beside_recv.at[0], to_core).start()
    keep = pltpu.make_async_copy(x_ref.at[half], orbital.at[core, half], copy_sem.at[0])
    keep.start()
    fetch = pltpu.make_async_copy(matrix_ref, constants, copy_sem.at[1])
    fetch.start()

    def within(q):
        return jnp.logical_and(q >= 0, q < pieces)

    def event(k):
        @pl.when(k < pieces)
        def _():
            block = piece(k, own)
            at_home = jnp.logical_and(root, k % 2 == half)

            @pl.when(at_home)
            def _():
                local(k).wait()

            @pl.when(jnp.logical_not(at_home))
            def _():
                arrived(block, own_recv.at[k])

            @pl.when(has_up)
            def _():
                send(block, up_send, own_recv.at[k], to_up)

            send(block, y_send, y_recv.at[k], to_y)
            send(block, x_send, x_recv.at[k], to_x)

        q = k - LAG

        @pl.when(within(q))
        def _():
            block = piece(q, over_y)
            arrived(block, y_recv.at[q])
            send(block, x_send, d_recv.at[q], to_x)
            arrived(piece(q, over_x), x_recv.at[q])

        r = k - 2 * LAG

        @pl.when(within(r))
        def _():
            arrived(piece(r, over_both), d_recv.at[r])

        @pl.when(k == START - 1)
        def _():
            arrived(orbital.at[core, other], swap_recv)
            send(orbital.at[core, other], beside_send.at[1], beside_recv.at[1], to_core)

        @pl.when(k == START)
        def _():
            keep.wait()
            arrived(orbital.at[1 - core, half], beside_recv.at[0])
            arrived(orbital.at[1 - core, other], beside_recv.at[1])

        t = k - START

        @pl.when(within(t))
        def _():
            o, h, rows = t // per_orbital, t % 2, group_rows((t % per_orbital) // 2)
            to = group_rows(h * groups + (t % per_orbital) // 2)

            @pl.loop(0, 2)
            def _(which):
                values = [
                    orbital[which, h, rows, columns(i)] * source[o, h, rows, columns(i)]
                    for i in range(count)
                ]
                for i, value in enumerate(into_modes(values)):
                    work[2 * o + which, to, columns(i)] = value

    count = cells // LANES
    ahead = per_orbital + START

    @pl.loop(0, ahead)
    def _(k):
        event(k)

        @pl.when(k < cells // TABLE_PART)
        def _():
            lanes = pl.ds(pl.multiple_of(k * TABLE_PART, TABLE_PART), TABLE_PART)
            table[:, lanes] = filter_part(k, length)

    fetch.wait()

    def slot(index, number):
        @pl.when(index < 2)
        def _():
            event(ahead + index * 4 + number)

    @pl.loop(0, 2 * owned)
    def _(index):
        which, o = index % 2, index // 2

        @pl.loop(0, cells // PART)
        def _(part):
            slot(index, part)
            lanes = [pl.ds(pl.multiple_of(part * PART + i, LANES), LANES) for i in range(0, PART, LANES)]
            whole = table[:, pl.ds(pl.multiple_of(part * PART, PART), PART)]
            tiles = filtered([work[index, :, lane] for lane in lanes], whole, *unpack(constants))
            for lane, tile in zip(lanes, tiles):
                work[index, :, lane] = tile

        @pl.loop(0, per_orbital)
        def _(step):
            @pl.when(step % 4 == 0)
            def _():
                slot(index, 2 + step // 4)

            mine = step // groups
            n = step % groups
            h = jnp.where(n < share, other, half)
            holder = jnp.where(mine == 1, core, 1 - core)
            group = holder * share + n % share
            rows, to = group_rows(group), group_rows(h * groups + group)
            values = out_of_modes([work[index, to, columns(i)] for i in range(count)])
            for i, value in enumerate(values):
                term = value * source[o, h, rows, columns(i)] * -EXX_FRACTION
                earlier = jnp.where(o == 0, 0.0, total[which, h, rows, columns(i)])
                total[which, h, rows, columns(i)] = earlier + term

            block = total.at[which, h, rows]
            last = o == owned - 1

            @pl.when(jnp.logical_and(last, mine == 0))
            def _():
                remote(block, partial.at[which, n], part_send, part_recv.at[which, n], to_core).start()

            @pl.when(jnp.logical_and(last, mine == 1))
            def _():
                arrived(partial.at[which, n], part_recv.at[which, n])
                for i in range(count):
                    total[which, h, rows, columns(i)] += partial[which, n, :, columns(i)]
                goal = out_ref.at[half, rows]

                @pl.when(n < share)
                def _():
                    remote(
                        block, goal, back_send, back_recv.at[core], {"band": 2 * chip + which, "fft": other}
                    ).start()

                @pl.when(jnp.logical_and(n >= share, which == core))
                def _():
                    pltpu.make_async_copy(block, goal, copy_sem.at[2]).start()

                @pl.when(jnp.logical_and(n >= share, which != core))
                def _():
                    remote(block, goal, done_send, done_recv, to_core).start()

    @pl.when(has_up)
    def _():
        sent(orbital.at[0, 0], up_send)

    @pl.when(root)
    def _():
        for i in range(3):
            sent(orbital.at[0, 0, : planes // 2], scatter_send.at[i])

    sent(orbital.at[0, 0], y_send)
    sent(orbital.at[0], x_send)
    sent(orbital.at[0, 0], beside_send.at[0])
    sent(orbital.at[0, 0], beside_send.at[1])
    swap.wait_send()
    sent(total.at[0], part_send)
    sent(total.at[0, 0], back_send)
    first, second = out_ref.at[other, : planes // 2], out_ref.at[other, planes // 2 :]
    sent(total.at[0, 0, : planes // 2], done_send)
    arrived(first, done_recv)
    pltpu.make_async_copy(total.at[0, 0, : planes // 2], first, copy_sem.at[2]).wait()
    arrived(first, back_recv.at[0])
    arrived(second, back_recv.at[1])


def two_halves(bands, row, orbitals):
    owned, planes, cells = orbitals.shape
    groups = planes // GROUP
    count = owned * 2 * groups
    dma = pltpu.SemaphoreType.DMA
    constants = jnp.asarray(matrices())
    grid = lambda *lead: pltpu.VMEM((*lead, planes, cells), jnp.float32)
    return pl.pallas_call(
        functools.partial(fused_kernel, bands // 2, row),
        out_shape=jax.ShapeDtypeStruct(orbitals.shape, jnp.float32),
        in_specs=[pl.BlockSpec(memory_space=pl.ANY)] * 2,
        out_specs=pl.BlockSpec(memory_space=pl.ANY),
        scratch_shapes=[
            pltpu.VMEM(constants.shape, jnp.bfloat16),
            grid(owned, 2),
            grid(2, 2),
            pltpu.VMEM((2 * planes, cells), jnp.float32),
            pltpu.VMEM((2 * owned, 2 * planes, cells), jnp.float32),
            grid(2, 2),
            pltpu.VMEM((2, groups, GROUP, cells), jnp.float32),
        ]
        + [dma((3,)), dma, dma, dma((2,)), dma((2,)), dma((count,)), dma((3,))]
        + [dma] * 3
        + [dma((count,))] * 4
        + [dma, dma((2, groups)), dma, dma((2,)), dma, dma],
        compiler_params=pltpu.CompilerParams(
            collective_id=0, has_side_effects=True, vmem_limit_bytes=60 * MIB
        ),
        name="exchange",
    )(orbitals, constants)


def many_parts(parts, orbitals):
    owned = orbitals.shape[0]
    place, band = lax.axis_index("fft"), lax.axis_index("band")
    fields = lax.all_gather(orbitals, "fft", axis=1, tiled=True)
    held = jnp.concatenate([jnp.where(band == r, fields, 0.0) for r in range(ROUNDS)], 0)
    sources = lax.psum(held, "band")
    groups = max(parts // owned, 1)
    share = sources.shape[0] // groups
    mine = lax.dynamic_slice_in_dim(sources, (place // owned) * share, share, 0)
    which = place % owned
    result = apply_exchange(lax.dynamic_index_in_dim(fields, which, 0, False), mine)
    placed = jnp.where(jnp.arange(owned)[:, None, None] == which, result[None], 0.0)
    return lax.psum_scatter(placed, "fft", scatter_dimension=1, tiled=True)


def solution(mesh):
    parts = mesh.shape["fft"]
    if parts == 2:
        body = functools.partial(two_halves, mesh.shape["band"], 2)
    else:
        body = functools.partial(many_parts, parts)
    return jax.shard_map(
        body, mesh=mesh, in_specs=(P("band", "fft", None),), out_specs=P("band", "fft", None), check_vma=False
    )
```

```python
import functools
import math

import jax
import jax.numpy as jnp
import numpy as np
from jax import lax
from jax.experimental import pallas as pl
from jax.experimental.pallas import tpu as pltpu
from jax.sharding import PartitionSpec as P

GRID = 64
ROUNDS = 2
EXX_FRACTION = 0.25
SCREEN = 0.05
MESH = pl.DeviceIdType.MESH
MIB = 1024 * 1024


def real_modes(length):
    n = np.arange(length)
    rows = [np.cos(2 * np.pi * q * n / length) for q in range(length // 2 + 1)]
    rows += [np.sin(2 * np.pi * q * n / length) for q in range(1, length // 2)]
    matrix = np.array(rows)
    return matrix / np.sqrt((matrix**2).sum(1, keepdims=True))


def split(matrix):
    high = matrix.astype(jnp.bfloat16)
    return high, (matrix - high.astype(np.float64)).astype(jnp.bfloat16)


def matrices():
    modes = real_modes(GRID)
    z_forward = np.kron(np.array([[1.0, 1.0], [1.0, -1.0]]) / np.sqrt(2.0), modes.T)
    out = []
    for matrix in (z_forward, z_forward.T):
        high, low = split(matrix)
        out += [np.concatenate([high, high], 0), np.concatenate([low, np.zeros_like(low)], 0)]
    for matrix in (modes, modes.T):
        high, low = split(matrix)
        out.append(
            np.concatenate(
                [np.concatenate([high, high], 1), np.concatenate([low, np.zeros_like(low)], 1)], 0
            )
        )
    return np.concatenate(out, 0)


def unpack(ref):
    sides = [ref[i * 256 : (i + 1) * 256, :] for i in range(4)]
    across = [ref[1024 + i * 128 : 1152 + i * 128, :] for i in range(2)]
    return [jnp.concatenate(sides[:2], 1), jnp.concatenate(sides[2:], 1)] + across


def mode_numbers():
    half = GRID // 2
    return np.concatenate([np.arange(half + 1), np.arange(1, half)])


def filter_table():
    k = jnp.asarray(mode_numbers(), jnp.float32)
    quarter = GRID // 4
    q = np.concatenate([np.arange(quarter + 1), np.arange(1, quarter)])
    weight = np.where((q == 0) | (q == quarter), 1.0, 2.0) / (GRID // 2)
    ky = jnp.asarray(np.stack([q, GRID // 2 - q], 1), jnp.float32)
    unit = 2.0 * math.pi / GRID
    squares = (
        (k * unit)[:, None, None, None] ** 2
        + (ky * unit)[None, :, :, None] ** 2
        + (k * unit)[None, None, None, :] ** 2
    )
    guarded = jnp.where(squares > 0, squares, 1.0)
    table = jnp.where(
        squares > 0, (1.0 - jnp.exp(-guarded / (4.0 * SCREEN * SCREEN))) / guarded, 0.0
    )
    table = table * jnp.asarray(weight, jnp.float32)[None, :, None, None]
    return table.reshape(GRID, GRID * GRID)


def rotate(c, s, cos, sin):
    return cos * c - sin * s, sin * c + cos * s


def forward(x):
    n = len(x)
    if n == 2:
        return [x[0] + x[1], x[0] - x[1]], {}
    ce, se = forward(x[0::2])
    co, so = forward(x[1::2])
    half, quarter = n // 2, n // 4
    c, s = [None] * (half + 1), {}
    c[0], c[half] = ce[0] + co[0], ce[0] - co[0]
    c[quarter], s[quarter] = ce[quarter], co[quarter]
    for q in range(1, quarter):
        if 8 * q == n:
            r = math.sqrt(0.5)
            a, b = (co[q] - so[q]) * r, (co[q] + so[q]) * r
        else:
            a, b = rotate(co[q], so[q], math.cos(2 * math.pi * q / n), math.sin(2 * math.pi * q / n))
        c[q], c[half - q] = ce[q] + a, ce[q] - a
        s[q], s[half - q] = b + se[q], b - se[q]
    return c, s


def backward(c, s):
    n = 2 * (len(c) - 1)
    if n == 2:
        return [c[0] + c[1], c[0] - c[1]]
    half, quarter = n // 2, n // 4
    ce, co, se, so = [None] * (quarter + 1), [None] * (quarter + 1), {}, {}
    ce[0], co[0] = c[0] + c[half], c[0] - c[half]
    ce[quarter], co[quarter] = c[quarter], s[quarter]
    for q in range(1, quarter):
        ce[q], a = c[q] + c[half - q], c[q] - c[half - q]
        b, se[q] = s[q] + s[half - q], s[q] - s[half - q]
        if 8 * q == n:
            r = math.sqrt(0.5)
            co[q], so[q] = (a + b) * r, (b - a) * r
        else:
            co[q], so[q] = rotate(a, b, math.cos(2 * math.pi * q / n), -math.sin(2 * math.pi * q / n))
    out = [None] * n
    out[0::2], out[1::2] = backward(ce, se), backward(co, so)
    return out


def twiddles(shape, q):
    odd = lax.broadcasted_iota(jnp.int32, shape, 1) >= shape[1] // 2
    angle = 2 * math.pi * q / GRID
    return jnp.where(odd, math.cos(angle), 1.0), jnp.where(odd, math.sin(angle), 0.0)


def halves(value):
    high = value.astype(jnp.bfloat16)
    return high, (value - high.astype(jnp.float32)).astype(jnp.bfloat16)


def along_z(tiles, double):
    high, rest = halves(jnp.concatenate(tiles, 0))
    out = jnp.dot(jnp.concatenate([high, rest], 1), double, preferred_element_type=jnp.float32)
    out = out[:, :LANES] + out[:, LANES:]
    step = tiles[0].shape[0]
    return [out[i * step : (i + 1) * step] for i in range(len(tiles))]


def along_x(value, double):
    length = value.shape[0]
    out = jnp.dot(double, jnp.concatenate(halves(value), 0), preferred_element_type=jnp.float32)
    return out[:length] + out[length:]


LANES = 128
PART = 2048
TABLE_PART = 512


def into_modes(densities):
    count = len(densities)
    quarter = count // 2
    c, s = forward(densities)
    for q in range(1, quarter):
        cos, sin = twiddles(densities[0].shape, q)
        c[q], s[q] = rotate(c[q], s[q], cos, sin)
    return c + [s[q] for q in range(1, quarter)]


def out_of_modes(values):
    quarter = len(values) // 2
    c, s = values[: quarter + 1], dict(enumerate(values[quarter + 1 :], 1))
    for q in range(1, quarter):
        cos, sin = twiddles(values[0].shape, q)
        c[q], s[q] = rotate(c[q], s[q], cos, -sin)
    return backward(c, s)


def filtered(tiles, table, z_forward, z_backward, x_forward, x_backward):
    value = along_x(jnp.concatenate(along_z(tiles, z_forward), 1), x_forward)
    value = along_x(value * table, x_backward)
    return along_z([value[:, i : i + LANES] for i in range(0, value.shape[1], LANES)], z_backward)


def columns(i):
    return slice(i * LANES, (i + 1) * LANES)


def exchange_kernel(orbital_ref, source_ref, filter_ref, *rest):
    constants, out_ref, work = rest
    length, cells = work.shape
    count = cells // LANES

    @pl.loop(0, length // 8)
    def _(block):
        rows = pl.ds(pl.multiple_of(block * 8, 8), 8)
        values = [
            orbital_ref[rows, columns(i)] * source_ref[0, rows, columns(i)] for i in range(count)
        ]
        for i, value in enumerate(into_modes(values)):
            work[rows, columns(i)] = value

    @pl.loop(0, cells // PART)
    def _(part):
        lanes = [pl.ds(pl.multiple_of(part * PART + i, LANES), LANES) for i in range(0, PART, LANES)]
        table = filter_ref[:, pl.ds(pl.multiple_of(part * PART, PART), PART)]
        tiles = filtered([work[:, lane] for lane in lanes], table, *unpack(constants))
        for lane, tile in zip(lanes, tiles):
            work[:, lane] = tile

    first = pl.program_id(0) == 0

    @pl.loop(0, length // 8)
    def _(block):
        rows = pl.ds(pl.multiple_of(block * 8, 8), 8)
        values = out_of_modes([work[rows, columns(i)] for i in range(count)])
        for i, value in enumerate(values):
            term = value * source_ref[0, rows, columns(i)] * -EXX_FRACTION
            out_ref[rows, columns(i)] = jnp.where(first, 0.0, out_ref[rows, columns(i)]) + term


def apply_exchange(orbital, sources):
    count, length, cells = sources.shape
    constants = jnp.asarray(matrices())
    whole = lambda shape: pl.BlockSpec(shape, lambda j: (0, 0))
    return pl.pallas_call(
        exchange_kernel,
        grid=(count,),
        out_shape=jax.ShapeDtypeStruct((length, cells), jnp.float32),
        in_specs=[
            whole((length, cells)),
            pl.BlockSpec((1, length, cells), lambda j: (j, 0, 0)),
            whole((length, cells)),
            whole(constants.shape),
        ],
        out_specs=whole((length, cells)),
        scratch_shapes=[pltpu.VMEM((length, cells), jnp.float32)],
        compiler_params=pltpu.CompilerParams(vmem_limit_bytes=32 * MIB),
        name="exchange",
    )(orbital, sources, filter_table(), constants)


GROUP = 8
COLUMNS = 4
LAG = 2
TABLE_PART = 512


def filter_part(part, length):
    shape = (length, TABLE_PART)
    half, quarter = length // 2, length // 4
    lane = lax.broadcasted_iota(jnp.int32, shape, 1) + part * TABLE_PART

    def mode(index):
        return jnp.where(index > half, index - half, index)

    row = lane >> 7
    q = jnp.where(row > quarter, row - quarter, row)
    ky = jnp.where((lane & half * 2) == 0, q, half - q)
    edge = jnp.logical_or(q == 0, q == quarter)
    squares = jnp.zeros(shape, jnp.float32)
    for k in (mode(lax.broadcasted_iota(jnp.int32, shape, 0)), ky, mode(lane & (length - 1))):
        squares = squares + (k.astype(jnp.float32) * (2.0 * math.pi / length)) ** 2
    guarded = jnp.where(squares > 0, squares, 1.0)
    table = (1.0 - jnp.exp(-guarded / (4.0 * SCREEN * SCREEN))) / guarded
    return jnp.where(squares > 0, table, 0.0) * jnp.where(edge, 1.0 / half, 2.0 / half)


def fused_kernel(chips, row, x_ref, matrix_ref, out_ref, *rest):
    (constants, source, orbital, table, work, total, partial, copy_sem, swap_send, swap_recv, beside_send,
     beside_recv, local_sem, scatter_send, up_send, far_send, y_send, x_send, own_recv, y_recv, x_recv, d_recv,
     part_send, part_recv, back_send, back_recv, done_send, done_recv) = rest
    band, half = lax.axis_index("band"), lax.axis_index("fft")
    chip, core = band // 2, band % 2
    side, layer = chip % row, chip // row
    owned, planes, cells = x_ref.shape
    length = 2 * planes
    other = 1 - half
    groups, width = planes // GROUP, cells // COLUMNS
    share = groups // 2
    per_orbital = 2 * groups
    pieces = owned * per_orbital
    root, has_up, bottom = chip == 0, layer % 2 == 0, layer == 0
    across_band, beside_band = band + 2 - 4 * side, band + 1 - 2 * core
    to_y = {"band": band, "fft": other}
    to_core = {"band": beside_band, "fft": half}
    to_cross = {"band": beside_band, "fft": other}
    to_x = {"band": across_band, "fft": half}
    to_diagonal = {"band": across_band, "fft": other}
    to_up = {"band": band + 2 * row, "fft": half}
    to_far = {"band": band + 4 * row, "fft": half}
    to_down = {"band": band - 2 * row * jnp.where(layer == 2, 2, 1), "fft": half}
    own = 2 * side + half
    over_y, over_x, over_both = own + 1 - 2 * half, own + 2 - 4 * side, 3 - own

    barrier = pltpu.get_barrier_semaphore()

    def greet(target):
        pl.semaphore_signal(barrier, inc=1, device_id=target, device_id_type=MESH)

    greet(to_y)
    greet(to_core)
    greet(to_cross)
    greet(to_x)

    @pl.when(has_up)
    def _():
        greet(to_up)

    @pl.when(jnp.logical_not(bottom))
    def _():
        greet(to_down)

    @pl.when(bottom)
    def _():
        greet(to_diagonal)
        greet(to_far)

    pl.semaphore_wait(barrier, 5 + has_up.astype(jnp.int32) + bottom.astype(jnp.int32))

    def remote(src, dst, send, recv, target):
        return pltpu.make_async_remote_copy(
            src_ref=src, dst_ref=dst, send_sem=send, recv_sem=recv, device_id=target, device_id_type=MESH
        )

    def send(block, send_sem, recv_sem, target):
        remote(block, block, send_sem, recv_sem, target).start()

    def arrived(block, recv):
        remote(block, block, swap_send, recv, to_y).wait_recv()

    def sent(block, send_sem):
        remote(block, block, send_sem, swap_recv, to_y).wait_send()

    def group_rows(group):
        return pl.ds(pl.multiple_of(group * GROUP, GROUP), GROUP)

    def place(q, column):
        rows = group_rows((q % per_orbital) // 2)
        return q // per_orbital, q % 2, rows, pl.ds(pl.multiple_of(column * width, width), width)

    def piece(q, column):
        return source.at[place(q, column)]

    def outer(q, column):
        o, _, rows, lanes = place(q, column)
        return x_ref.at[o, rows, lanes]

    def local(q):
        return pltpu.make_async_copy(outer(q, own), piece(q, own), local_sem.at[q])

    swap = remote(x_ref.at[other], orbital.at[core, half], swap_send, swap_recv, to_y)
    swap.start()

    @pl.when(root)
    def _():
        @pl.loop(0, pieces)
        def _(q):
            @pl.when(q % 2 == half)
            def _():
                for i, (column, target) in enumerate(
                    ((over_x, to_x), (over_both, to_diagonal), (over_y, to_y))
                ):
                    remote(
                        outer(q, column), piece(q, column), scatter_send.at[i], own_recv.at[q], target
                    ).start()
                local(q).start()

    remote(x_ref.at[half], orbital.at[core, half], beside_send.at[0], beside_recv.at[0], to_core).start()
    keep = pltpu.make_async_copy(x_ref.at[half], orbital.at[core, half], copy_sem.at[0])
    keep.start()
    fetch = pltpu.make_async_copy(matrix_ref, constants, copy_sem.at[1])
    fetch.start()

    def within(q):
        return jnp.logical_and(q >= 0, q < pieces)

    def event(k):
        @pl.when(k < pieces)
        def _():
            block = piece(k, own)
            at_home = jnp.logical_and(root, k % 2 == half)

            @pl.when(at_home)
            def _():
                local(k).wait()

            @pl.when(jnp.logical_not(at_home))
            def _():
                arrived(block, own_recv.at[k])

            @pl.when(bottom)
            def _():
                send(block, far_send, own_recv.at[k], to_far)

            @pl.when(has_up)
            def _():
                send(block, up_send, own_recv.at[k], to_up)

            send(block, y_send, y_recv.at[k], to_y)
            send(block, x_send, x_recv.at[k], to_x)

        q = k - LAG

        @pl.when(within(q))
        def _():
            block = piece(q, over_y)
            arrived(block, y_recv.at[q])
            send(block, x_send, d_recv.at[q], to_x)
            arrived(piece(q, over_x), x_recv.at[q])

        r = k - 2 * LAG

        @pl.when(within(r))
        def _():
            arrived(piece(r, over_both), d_recv.at[r])

    count = cells // LANES
    ahead = per_orbital + 2 * LAG

    @pl.loop(0, ahead)
    def _(k):
        event(k)

        @pl.when(k < cells // TABLE_PART)
        def _():
            lanes = pl.ds(pl.multiple_of(k * TABLE_PART, TABLE_PART), TABLE_PART)
            table[:, lanes] = filter_part(k, length)

        @pl.when(k == ahead - 2)
        def _():
            arrived(orbital.at[core, other], swap_recv)
            send(orbital.at[core, other], beside_send.at[1], beside_recv.at[1], to_core)

    keep.wait()
    arrived(orbital.at[1 - core, half], beside_recv.at[0])
    arrived(orbital.at[1 - core, other], beside_recv.at[1])
    fetch.wait()

    def slot(index, number):
        @pl.when(index == 0)
        def _():
            event(ahead + number)

    @pl.loop(0, 2 * owned)
    def _(index):
        which, o = index % 2, index // 2

        @pl.when(which == 0)
        def _():
            @pl.loop(0, per_orbital)
            def _(block):
                @pl.when(block % 2 == 0)
                def _():
                    slot(index, block // 2)

                h, rows, to = block // groups, group_rows(block % groups), group_rows(block)

                @pl.loop(0, 2)
                def _(field):
                    values = [
                        orbital[field, h, rows, columns(i)] * source[o, h, rows, columns(i)]
                        for i in range(count)
                    ]
                    for i, value in enumerate(into_modes(values)):
                        work[2 * o + field, to, columns(i)] = value

        @pl.loop(0, cells // PART)
        def _(part):
            slot(index, 4 + part)
            lanes = [pl.ds(pl.multiple_of(part * PART + i, LANES), LANES) for i in range(0, PART, LANES)]
            whole = table[:, pl.ds(pl.multiple_of(part * PART, PART), PART)]
            tiles = filtered([work[index, :, lane] for lane in lanes], whole, *unpack(constants))
            for lane, tile in zip(lanes, tiles):
                work[index, :, lane] = tile

        @pl.loop(0, per_orbital)
        def _(step):
            @pl.when(step % 4 == 0)
            def _():
                slot(index, 6 + step // 4)

            mine = step // groups
            n = step % groups
            h = jnp.where(n < share, other, half)
            holder = jnp.where(mine == 1, core, 1 - core)
            group = holder * share + n % share
            rows, to = group_rows(group), group_rows(h * groups + group)
            values = out_of_modes([work[index, to, columns(i)] for i in range(count)])
            for i, value in enumerate(values):
                term = value * source[o, h, rows, columns(i)] * -EXX_FRACTION
                earlier = jnp.where(o == 0, 0.0, total[which, h, rows, columns(i)])
                total[which, h, rows, columns(i)] = earlier + term

            block = total.at[which, h, rows]
            last = o == owned - 1

            @pl.when(jnp.logical_and(last, mine == 0))
            def _():
                remote(block, partial.at[which, n], part_send, part_recv.at[which, n], to_core).start()

            @pl.when(jnp.logical_and(last, mine == 1))
            def _():
                arrived(partial.at[which, n], part_recv.at[which, n])
                for i in range(count):
                    total[which, h, rows, columns(i)] += partial[which, n, :, columns(i)]
                goal = out_ref.at[half, rows]

                @pl.when(n < share)
                def _():
                    remote(
                        block, goal, back_send, back_recv.at[core], {"band": 2 * chip + which, "fft": other}
                    ).start()

                @pl.when(jnp.logical_and(n >= share, which == core))
                def _():
                    pltpu.make_async_copy(block, goal, copy_sem.at[2]).start()

                @pl.when(jnp.logical_and(n >= share, which != core))
                def _():
                    remote(block, goal, done_send, done_recv, to_core).start()

    @pl.when(has_up)
    def _():
        sent(orbital.at[0, 0], up_send)

    @pl.when(bottom)
    def _():
        sent(orbital.at[0, 0], far_send)

    @pl.when(root)
    def _():
        for i in range(3):
            sent(orbital.at[0, 0, : planes // 2], scatter_send.at[i])

    sent(orbital.at[0, 0], y_send)
    sent(orbital.at[0], x_send)
    sent(orbital.at[0, 0], beside_send.at[0])
    sent(orbital.at[0, 0], beside_send.at[1])
    swap.wait_send()
    sent(total.at[0], part_send)
    sent(total.at[0, 0], back_send)
    first, second = out_ref.at[other, : planes // 2], out_ref.at[other, planes // 2 :]
    sent(total.at[0, 0, : planes // 2], done_send)
    arrived(first, done_recv)
    pltpu.make_async_copy(total.at[0, 0, : planes // 2], first, copy_sem.at[2]).wait()
    arrived(first, back_recv.at[0])
    arrived(second, back_recv.at[1])


def two_halves(bands, row, orbitals):
    owned, planes, cells = orbitals.shape
    groups = planes // GROUP
    count = owned * 2 * groups
    dma = pltpu.SemaphoreType.DMA
    constants = jnp.asarray(matrices())
    grid = lambda *lead: pltpu.VMEM((*lead, planes, cells), jnp.float32)
    return pl.pallas_call(
        functools.partial(fused_kernel, bands // 2, row),
        out_shape=jax.ShapeDtypeStruct(orbitals.shape, jnp.float32),
        in_specs=[pl.BlockSpec(memory_space=pl.ANY)] * 2,
        out_specs=pl.BlockSpec(memory_space=pl.ANY),
        scratch_shapes=[
            pltpu.VMEM(constants.shape, jnp.bfloat16),
            grid(owned, 2),
            grid(2, 2),
            pltpu.VMEM((2 * planes, cells), jnp.float32),
            pltpu.VMEM((2 * owned, 2 * planes, cells), jnp.float32),
            grid(2, 2),
            pltpu.VMEM((2, groups, GROUP, cells), jnp.float32),
        ]
        + [dma((3,)), dma, dma, dma((2,)), dma((2,)), dma((count,)), dma((3,))]
        + [dma] * 4
        + [dma((count,))] * 4
        + [dma, dma((2, groups)), dma, dma((2,)), dma, dma],
        compiler_params=pltpu.CompilerParams(
            collective_id=0, has_side_effects=True, vmem_limit_bytes=60 * MIB
        ),
        name="exchange",
    )(orbitals, constants)


def many_parts(parts, orbitals):
    owned = orbitals.shape[0]
    place, band = lax.axis_index("fft"), lax.axis_index("band")
    fields = lax.all_gather(orbitals, "fft", axis=1, tiled=True)
    held = jnp.concatenate([jnp.where(band == r, fields, 0.0) for r in range(ROUNDS)], 0)
    sources = lax.psum(held, "band")
    groups = max(parts // owned, 1)
    share = sources.shape[0] // groups
    mine = lax.dynamic_slice_in_dim(sources, (place // owned) * share, share, 0)
    which = place % owned
    result = apply_exchange(lax.dynamic_index_in_dim(fields, which, 0, False), mine)
    placed = jnp.where(jnp.arange(owned)[:, None, None] == which, result[None], 0.0)
    return lax.psum_scatter(placed, "fft", scatter_dimension=1, tiled=True)


def solution(mesh):
    parts = mesh.shape["fft"]
    if parts == 2 and mesh.shape["band"] == 16:
        body = functools.partial(two_halves, mesh.shape["band"], 2)
    else:
        body = functools.partial(many_parts, parts)
    return jax.shard_map(
        body, mesh=mesh, in_specs=(P("band", "fft", None),), out_specs=P("band", "fft", None), check_vma=False
    )
```

```python
import functools
import math

import jax
import jax.numpy as jnp
import numpy as np
from jax import lax
from jax.experimental import pallas as pl
from jax.experimental.pallas import tpu as pltpu
from jax.sharding import PartitionSpec as P

GRID = 64
ROUNDS = 2
EXX_FRACTION = 0.25
SCREEN = 0.05
MESH = pl.DeviceIdType.MESH
MIB = 1024 * 1024


def real_modes(length):
    n = np.arange(length)
    rows = [np.cos(2 * np.pi * q * n / length) for q in range(length // 2 + 1)]
    rows += [np.sin(2 * np.pi * q * n / length) for q in range(1, length // 2)]
    matrix = np.array(rows)
    return matrix / np.sqrt((matrix**2).sum(1, keepdims=True))


def split(matrix):
    high = matrix.astype(jnp.bfloat16)
    return high, (matrix - high.astype(np.float64)).astype(jnp.bfloat16)


def matrices():
    modes = real_modes(GRID)
    z_forward = np.kron(np.array([[1.0, 1.0], [1.0, -1.0]]) / np.sqrt(2.0), modes.T)
    out = []
    for matrix in (z_forward, z_forward.T):
        high, low = split(matrix)
        out += [np.concatenate([high, high], 0), np.concatenate([low, np.zeros_like(low)], 0)]
    for matrix in (modes, modes.T):
        high, low = split(matrix)
        out.append(
            np.concatenate(
                [np.concatenate([high, high], 1), np.concatenate([low, np.zeros_like(low)], 1)], 0
            )
        )
    return np.concatenate(out, 0)


def unpack(ref):
    sides = [ref[i * 256 : (i + 1) * 256, :] for i in range(4)]
    across = [ref[1024 + i * 128 : 1152 + i * 128, :] for i in range(2)]
    return [jnp.concatenate(sides[:2], 1), jnp.concatenate(sides[2:], 1)] + across


def mode_numbers():
    half = GRID // 2
    return np.concatenate([np.arange(half + 1), np.arange(1, half)])


def filter_table():
    k = jnp.asarray(mode_numbers(), jnp.float32)
    quarter = GRID // 4
    q = np.concatenate([np.arange(quarter + 1), np.arange(1, quarter)])
    weight = np.where((q == 0) | (q == quarter), 1.0, 2.0) / (GRID // 2)
    ky = jnp.asarray(np.stack([q, GRID // 2 - q], 1), jnp.float32)
    unit = 2.0 * math.pi / GRID
    squares = (
        (k * unit)[:, None, None, None] ** 2
        + (ky * unit)[None, :, :, None] ** 2
        + (k * unit)[None, None, None, :] ** 2
    )
    guarded = jnp.where(squares > 0, squares, 1.0)
    table = jnp.where(
        squares > 0, (1.0 - jnp.exp(-guarded / (4.0 * SCREEN * SCREEN))) / guarded, 0.0
    )
    table = table * jnp.asarray(weight, jnp.float32)[None, :, None, None]
    return table.reshape(GRID, GRID * GRID)


def rotate(c, s, cos, sin):
    return cos * c - sin * s, sin * c + cos * s


def forward(x):
    n = len(x)
    if n == 2:
        return [x[0] + x[1], x[0] - x[1]], {}
    ce, se = forward(x[0::2])
    co, so = forward(x[1::2])
    half, quarter = n // 2, n // 4
    c, s = [None] * (half + 1), {}
    c[0], c[half] = ce[0] + co[0], ce[0] - co[0]
    c[quarter], s[quarter] = ce[quarter], co[quarter]
    for q in range(1, quarter):
        if 8 * q == n:
            r = math.sqrt(0.5)
            a, b = (co[q] - so[q]) * r, (co[q] + so[q]) * r
        else:
            a, b = rotate(co[q], so[q], math.cos(2 * math.pi * q / n), math.sin(2 * math.pi * q / n))
        c[q], c[half - q] = ce[q] + a, ce[q] - a
        s[q], s[half - q] = b + se[q], b - se[q]
    return c, s


def backward(c, s):
    n = 2 * (len(c) - 1)
    if n == 2:
        return [c[0] + c[1], c[0] - c[1]]
    half, quarter = n // 2, n // 4
    ce, co, se, so = [None] * (quarter + 1), [None] * (quarter + 1), {}, {}
    ce[0], co[0] = c[0] + c[half], c[0] - c[half]
    ce[quarter], co[quarter] = c[quarter], s[quarter]
    for q in range(1, quarter):
        ce[q], a = c[q] + c[half - q], c[q] - c[half - q]
        b, se[q] = s[q] + s[half - q], s[q] - s[half - q]
        if 8 * q == n:
            r = math.sqrt(0.5)
            co[q], so[q] = (a + b) * r, (b - a) * r
        else:
            co[q], so[q] = rotate(a, b, math.cos(2 * math.pi * q / n), -math.sin(2 * math.pi * q / n))
    out = [None] * n
    out[0::2], out[1::2] = backward(ce, se), backward(co, so)
    return out


def twiddles(shape, q):
    odd = lax.broadcasted_iota(jnp.int32, shape, 1) >= shape[1] // 2
    angle = 2 * math.pi * q / GRID
    return jnp.where(odd, math.cos(angle), 1.0), jnp.where(odd, math.sin(angle), 0.0)


def halves(value):
    high = value.astype(jnp.bfloat16)
    return high, (value - high.astype(jnp.float32)).astype(jnp.bfloat16)


def along_z(tiles, double):
    high, rest = halves(jnp.concatenate(tiles, 0))
    out = jnp.dot(jnp.concatenate([high, rest], 1), double, preferred_element_type=jnp.float32)
    out = out[:, :LANES] + out[:, LANES:]
    step = tiles[0].shape[0]
    return [out[i * step : (i + 1) * step] for i in range(len(tiles))]


def along_x(value, double):
    length = value.shape[0]
    out = jnp.dot(double, jnp.concatenate(halves(value), 0), preferred_element_type=jnp.float32)
    return out[:length] + out[length:]


LANES = 128
PART = 512
TABLE_PART = 512


def into_modes(densities):
    count = len(densities)
    quarter = count // 2
    c, s = forward(densities)
    for q in range(1, quarter):
        cos, sin = twiddles(densities[0].shape, q)
        c[q], s[q] = rotate(c[q], s[q], cos, sin)
    return c + [s[q] for q in range(1, quarter)]


def out_of_modes(values):
    quarter = len(values) // 2
    c, s = values[: quarter + 1], dict(enumerate(values[quarter + 1 :], 1))
    for q in range(1, quarter):
        cos, sin = twiddles(values[0].shape, q)
        c[q], s[q] = rotate(c[q], s[q], cos, -sin)
    return backward(c, s)


def filtered(tiles, table, z_forward, z_backward, x_forward, x_backward):
    value = along_x(jnp.concatenate(along_z(tiles, z_forward), 1), x_forward)
    value = along_x(value * table, x_backward)
    return along_z([value[:, i : i + LANES] for i in range(0, value.shape[1], LANES)], z_backward)


def columns(i):
    return slice(i * LANES, (i + 1) * LANES)


def exchange_kernel(orbital_ref, source_ref, filter_ref, *rest):
    constants, out_ref, work = rest
    length, cells = work.shape
    count = cells // LANES

    @pl.loop(0, length // 8)
    def _(block):
        rows = pl.ds(pl.multiple_of(block * 8, 8), 8)
        values = [
            orbital_ref[rows, columns(i)] * source_ref[0, rows, columns(i)] for i in range(count)
        ]
        for i, value in enumerate(into_modes(values)):
            work[rows, columns(i)] = value

    @pl.loop(0, cells // PART)
    def _(part):
        lanes = [pl.ds(pl.multiple_of(part * PART + i, LANES), LANES) for i in range(0, PART, LANES)]
        table = filter_ref[:, pl.ds(pl.multiple_of(part * PART, PART), PART)]
        tiles = filtered([work[:, lane] for lane in lanes], table, *unpack(constants))
        for lane, tile in zip(lanes, tiles):
            work[:, lane] = tile

    first = pl.program_id(0) == 0

    @pl.loop(0, length // 8)
    def _(block):
        rows = pl.ds(pl.multiple_of(block * 8, 8), 8)
        values = out_of_modes([work[rows, columns(i)] for i in range(count)])
        for i, value in enumerate(values):
            term = value * source_ref[0, rows, columns(i)] * -EXX_FRACTION
            out_ref[rows, columns(i)] = jnp.where(first, 0.0, out_ref[rows, columns(i)]) + term


def apply_exchange(orbital, sources):
    count, length, cells = sources.shape
    constants = jnp.asarray(matrices())
    whole = lambda shape: pl.BlockSpec(shape, lambda j: (0, 0))
    return pl.pallas_call(
        exchange_kernel,
        grid=(count,),
        out_shape=jax.ShapeDtypeStruct((length, cells), jnp.float32),
        in_specs=[
            whole((length, cells)),
            pl.BlockSpec((1, length, cells), lambda j: (j, 0, 0)),
            whole((length, cells)),
            whole(constants.shape),
        ],
        out_specs=whole((length, cells)),
        scratch_shapes=[pltpu.VMEM((length, cells), jnp.float32)],
        compiler_params=pltpu.CompilerParams(vmem_limit_bytes=32 * MIB),
        name="exchange",
    )(orbital, sources, filter_table(), constants)


GROUP = 8
COLUMNS = 4
LAG = 2
TABLE_PART = 512


def filter_part(part, length):
    shape = (length, TABLE_PART)
    half, quarter = length // 2, length // 4
    lane = lax.broadcasted_iota(jnp.int32, shape, 1) + part * TABLE_PART

    def mode(index):
        return jnp.where(index > half, index - half, index)

    row = lane >> 7
    q = jnp.where(row > quarter, row - quarter, row)
    ky = jnp.where((lane & half * 2) == 0, q, half - q)
    edge = jnp.logical_or(q == 0, q == quarter)
    squares = jnp.zeros(shape, jnp.float32)
    for k in (mode(lax.broadcasted_iota(jnp.int32, shape, 0)), ky, mode(lane & (length - 1))):
        squares = squares + (k.astype(jnp.float32) * (2.0 * math.pi / length)) ** 2
    guarded = jnp.where(squares > 0, squares, 1.0)
    table = (1.0 - jnp.exp(-guarded / (4.0 * SCREEN * SCREEN))) / guarded
    scale = -EXX_FRACTION / half
    return jnp.where(squares > 0, table, 0.0) * jnp.where(edge, scale, 2.0 * scale)


def fused_kernel(chips, row, x_ref, matrix_ref, out_ref, *rest):
    (constants, source, orbital, table, work, total, partial, copy_sem, swap_send, swap_recv, beside_send,
     beside_recv, local_sem, scatter_send, up_send, far_send, y_send, x_send, own_recv, y_recv, x_recv, d_recv,
     part_send, part_recv, back_send, back_recv, done_send, done_recv) = rest
    band, half = lax.axis_index("band"), lax.axis_index("fft")
    chip, core = band // 2, band % 2
    side, layer = chip % row, chip // row
    owned, planes, cells = x_ref.shape
    length = 2 * planes
    other = 1 - half
    groups, width = planes // GROUP, cells // COLUMNS
    share = groups // 2
    per_orbital = 2 * groups
    pieces = owned * per_orbital
    root, has_up, bottom = chip == 0, layer % 2 == 0, layer == 0
    across_band, beside_band = band + 2 - 4 * side, band + 1 - 2 * core
    to_y = {"band": band, "fft": other}
    to_core = {"band": beside_band, "fft": half}
    to_cross = {"band": beside_band, "fft": other}
    to_x = {"band": across_band, "fft": half}
    to_diagonal = {"band": across_band, "fft": other}
    to_up = {"band": band + 2 * row, "fft": half}
    to_far = {"band": band + 4 * row, "fft": half}
    to_down = {"band": band - 2 * row * jnp.where(layer == 2, 2, 1), "fft": half}
    own = 2 * side + half
    over_y, over_x, over_both = own + 1 - 2 * half, own + 2 - 4 * side, 3 - own

    barrier = pltpu.get_barrier_semaphore()

    def greet(target):
        pl.semaphore_signal(barrier, inc=1, device_id=target, device_id_type=MESH)

    greet(to_y)
    greet(to_core)
    greet(to_cross)
    greet(to_x)

    @pl.when(has_up)
    def _():
        greet(to_up)

    @pl.when(jnp.logical_not(bottom))
    def _():
        greet(to_down)

    @pl.when(bottom)
    def _():
        greet(to_diagonal)
        greet(to_far)

    pl.semaphore_wait(barrier, 5 + has_up.astype(jnp.int32) + bottom.astype(jnp.int32))

    def remote(src, dst, send, recv, target):
        return pltpu.make_async_remote_copy(
            src_ref=src, dst_ref=dst, send_sem=send, recv_sem=recv, device_id=target, device_id_type=MESH
        )

    def send(block, send_sem, recv_sem, target):
        remote(block, block, send_sem, recv_sem, target).start()

    def arrived(block, recv):
        remote(block, block, swap_send, recv, to_y).wait_recv()

    def sent(block, send_sem):
        remote(block, block, send_sem, swap_recv, to_y).wait_send()

    def group_rows(group):
        return pl.ds(pl.multiple_of(group * GROUP, GROUP), GROUP)

    def place(q, column):
        rows = group_rows((q % per_orbital) // 2)
        return q // per_orbital, q % 2, rows, pl.ds(pl.multiple_of(column * width, width), width)

    def piece(q, column):
        return source.at[place(q, column)]

    def outer(q, column):
        o, _, rows, lanes = place(q, column)
        return x_ref.at[o, rows, lanes]

    def local(q):
        return pltpu.make_async_copy(outer(q, own), piece(q, own), local_sem.at[q])

    swap = remote(x_ref.at[other], orbital.at[core, half], swap_send, swap_recv, to_y)
    swap.start()

    @pl.when(root)
    def _():
        @pl.loop(0, pieces)
        def _(q):
            @pl.when(q % 2 == half)
            def _():
                for i, (column, target) in enumerate(
                    ((over_x, to_x), (over_both, to_diagonal), (over_y, to_y))
                ):
                    remote(
                        outer(q, column), piece(q, column), scatter_send.at[i], own_recv.at[q], target
                    ).start()
                local(q).start()

    remote(x_ref.at[half], orbital.at[core, half], beside_send.at[0], beside_recv.at[0], to_core).start()
    keep = pltpu.make_async_copy(x_ref.at[half], orbital.at[core, half], copy_sem.at[0])
    keep.start()
    fetch = pltpu.make_async_copy(matrix_ref, constants, copy_sem.at[1])
    fetch.start()

    def within(q):
        return jnp.logical_and(q >= 0, q < pieces)

    def event(k):
        @pl.when(k < pieces)
        def _():
            block = piece(k, own)
            at_home = jnp.logical_and(root, k % 2 == half)

            @pl.when(at_home)
            def _():
                local(k).wait()

            @pl.when(jnp.logical_not(at_home))
            def _():
                arrived(block, own_recv.at[k])

            @pl.when(bottom)
            def _():
                send(block, far_send, own_recv.at[k], to_far)

            @pl.when(has_up)
            def _():
                send(block, up_send, own_recv.at[k], to_up)

            send(block, y_send, y_recv.at[k], to_y)
            send(block, x_send, x_recv.at[k], to_x)

        q = k - LAG

        @pl.when(within(q))
        def _():
            block = piece(q, over_y)
            arrived(block, y_recv.at[q])
            send(block, x_send, d_recv.at[q], to_x)
            arrived(piece(q, over_x), x_recv.at[q])

        r = k - 2 * LAG

        @pl.when(within(r))
        def _():
            arrived(piece(r, over_both), d_recv.at[r])

    count = cells // LANES
    ahead = per_orbital + 2 * LAG

    @pl.loop(0, ahead)
    def _(k):
        event(k)

        @pl.when(k < cells // TABLE_PART)
        def _():
            lanes = pl.ds(pl.multiple_of(k * TABLE_PART, TABLE_PART), TABLE_PART)
            table[:, lanes] = filter_part(k, length)

        @pl.when(k == ahead - 2)
        def _():
            arrived(orbital.at[core, other], swap_recv)
            send(orbital.at[core, other], beside_send.at[1], beside_recv.at[1], to_core)

    keep.wait()
    arrived(orbital.at[1 - core, half], beside_recv.at[0])
    arrived(orbital.at[1 - core, other], beside_recv.at[1])
    fetch.wait()

    def slot(index, number):
        @pl.when(index == 0)
        def _():
            event(ahead + number)

    @pl.loop(0, 2 * owned)
    def _(index):
        which, o = index % 2, index // 2

        @pl.when(which == 0)
        def _():
            @pl.loop(0, per_orbital)
            def _(block):
                @pl.when(block % 2 == 0)
                def _():
                    slot(index, block // 2)

                h, rows, to = block // groups, group_rows(block % groups), group_rows(block)

                @pl.loop(0, 2)
                def _(field):
                    values = [
                        orbital[field, h, rows, columns(i)] * source[o, h, rows, columns(i)]
                        for i in range(count)
                    ]
                    for i, value in enumerate(into_modes(values)):
                        work[2 * o + field, to, columns(i)] = value

        for part in range(cells // PART):
            if part % 4 == 0:
                slot(index, 4 + part // 4)
            lanes = [slice(part * PART + i, part * PART + i + LANES) for i in range(0, PART, LANES)]
            whole = table[:, part * PART : (part + 1) * PART]
            tiles = filtered([work[index, :, lane] for lane in lanes], whole, *unpack(constants))
            for lane, tile in zip(lanes, tiles):
                work[index, :, lane] = tile

        @pl.loop(0, per_orbital)
        def _(step):
            @pl.when(step % 4 == 0)
            def _():
                slot(index, 6 + step // 4)

            mine = step // groups
            n = step % groups
            h = jnp.where(n < share, other, half)
            holder = jnp.where(mine == 1, core, 1 - core)
            group = holder * share + n % share
            rows, to = group_rows(group), group_rows(h * groups + group)
            values = out_of_modes([work[index, to, columns(i)] for i in range(count)])
            for i, value in enumerate(values):
                term = value * source[o, h, rows, columns(i)]
                earlier = jnp.where(o == 0, 0.0, total[which, h, rows, columns(i)])
                total[which, h, rows, columns(i)] = earlier + term

            block = total.at[which, h, rows]
            last = o == owned - 1

            @pl.when(jnp.logical_and(last, mine == 0))
            def _():
                remote(block, partial.at[which, n], part_send, part_recv.at[which, n], to_core).start()

            @pl.when(jnp.logical_and(last, mine == 1))
            def _():
                arrived(partial.at[which, n], part_recv.at[which, n])
                for i in range(count):
                    total[which, h, rows, columns(i)] += partial[which, n, :, columns(i)]
                goal = out_ref.at[half, rows]

                @pl.when(n < share)
                def _():
                    remote(
                        block, goal, back_send, back_recv.at[core], {"band": 2 * chip + which, "fft": other}
                    ).start()

                @pl.when(jnp.logical_and(n >= share, which == core))
                def _():
                    pltpu.make_async_copy(block, goal, copy_sem.at[2]).start()

                @pl.when(jnp.logical_and(n >= share, which != core))
                def _():
                    remote(block, goal, done_send, done_recv, to_core).start()

    @pl.when(has_up)
    def _():
        sent(orbital.at[0, 0], up_send)

    @pl.when(bottom)
    def _():
        sent(orbital.at[0, 0], far_send)

    @pl.when(root)
    def _():
        for i in range(3):
            sent(orbital.at[0, 0, : planes // 2], scatter_send.at[i])

    sent(orbital.at[0, 0], y_send)
    sent(orbital.at[0], x_send)
    sent(orbital.at[0, 0], beside_send.at[0])
    sent(orbital.at[0, 0], beside_send.at[1])
    swap.wait_send()
    sent(total.at[0], part_send)
    sent(total.at[0, 0], back_send)
    first, second = out_ref.at[other, : planes // 2], out_ref.at[other, planes // 2 :]
    sent(total.at[0, 0, : planes // 2], done_send)
    arrived(first, done_recv)
    pltpu.make_async_copy(total.at[0, 0, : planes // 2], first, copy_sem.at[2]).wait()
    arrived(first, back_recv.at[0])
    arrived(second, back_recv.at[1])


def two_halves(bands, row, orbitals):
    owned, planes, cells = orbitals.shape
    groups = planes // GROUP
    count = owned * 2 * groups
    dma = pltpu.SemaphoreType.DMA
    constants = jnp.asarray(matrices())
    grid = lambda *lead: pltpu.VMEM((*lead, planes, cells), jnp.float32)
    return pl.pallas_call(
        functools.partial(fused_kernel, bands // 2, row),
        out_shape=jax.ShapeDtypeStruct(orbitals.shape, jnp.float32),
        in_specs=[pl.BlockSpec(memory_space=pl.ANY)] * 2,
        out_specs=pl.BlockSpec(memory_space=pl.ANY),
        scratch_shapes=[
            pltpu.VMEM(constants.shape, jnp.bfloat16),
            grid(owned, 2),
            grid(2, 2),
            pltpu.VMEM((2 * planes, cells), jnp.float32),
            pltpu.VMEM((2 * owned, 2 * planes, cells), jnp.float32),
            grid(2, 2),
            pltpu.VMEM((2, groups, GROUP, cells), jnp.float32),
        ]
        + [dma((3,)), dma, dma, dma((2,)), dma((2,)), dma((count,)), dma((3,))]
        + [dma] * 4
        + [dma((count,))] * 4
        + [dma, dma((2, groups)), dma, dma((2,)), dma, dma],
        compiler_params=pltpu.CompilerParams(
            collective_id=0, has_side_effects=True, vmem_limit_bytes=60 * MIB
        ),
        name="exchange",
    )(orbitals, constants)


def many_parts(parts, orbitals):
    owned = orbitals.shape[0]
    place, band = lax.axis_index("fft"), lax.axis_index("band")
    fields = lax.all_gather(orbitals, "fft", axis=1, tiled=True)
    held = jnp.concatenate([jnp.where(band == r, fields, 0.0) for r in range(ROUNDS)], 0)
    sources = lax.psum(held, "band")
    groups = max(parts // owned, 1)
    share = sources.shape[0] // groups
    mine = lax.dynamic_slice_in_dim(sources, (place // owned) * share, share, 0)
    which = place % owned
    result = apply_exchange(lax.dynamic_index_in_dim(fields, which, 0, False), mine)
    placed = jnp.where(jnp.arange(owned)[:, None, None] == which, result[None], 0.0)
    return lax.psum_scatter(placed, "fft", scatter_dimension=1, tiled=True)


def solution(mesh):
    parts = mesh.shape["fft"]
    if parts == 2 and mesh.shape["band"] == 16:
        body = functools.partial(two_halves, mesh.shape["band"], 2)
    else:
        body = functools.partial(many_parts, parts)
    return jax.shard_map(
        body, mesh=mesh, in_specs=(P("band", "fft", None),), out_specs=P("band", "fft", None), check_vma=False
    )
```

```python
import functools
import math

import jax
import jax.numpy as jnp
import numpy as np
from jax import lax
from jax.experimental import pallas as pl
from jax.experimental.pallas import tpu as pltpu
from jax.sharding import PartitionSpec as P

GRID = 64
ROUNDS = 2
EXX_FRACTION = 0.25
SCREEN = 0.05
MESH = pl.DeviceIdType.MESH
MIB = 1024 * 1024


def real_modes(length):
    n = np.arange(length)
    rows = [np.cos(2 * np.pi * q * n / length) for q in range(length // 2 + 1)]
    rows += [np.sin(2 * np.pi * q * n / length) for q in range(1, length // 2)]
    matrix = np.array(rows)
    return matrix / np.sqrt((matrix**2).sum(1, keepdims=True))


def split(matrix):
    high = matrix.astype(jnp.bfloat16)
    return high, (matrix - high.astype(np.float64)).astype(jnp.bfloat16)


def matrices():
    modes = real_modes(GRID)
    z_forward = np.kron(np.array([[1.0, 1.0], [1.0, -1.0]]) / np.sqrt(2.0), modes.T)
    out = []
    for matrix in (z_forward, z_forward.T):
        high, low = split(matrix)
        out += [np.concatenate([high, high], 0), np.concatenate([low, np.zeros_like(low)], 0)]
    for matrix in (modes, modes.T):
        high, low = split(matrix)
        out.append(
            np.concatenate(
                [np.concatenate([high, high], 1), np.concatenate([low, np.zeros_like(low)], 1)], 0
            )
        )
    return np.concatenate(out, 0)


def unpack(ref):
    sides = [ref[i * 256 : (i + 1) * 256, :] for i in range(4)]
    across = [ref[1024 + i * 128 : 1152 + i * 128, :] for i in range(2)]
    return [jnp.concatenate(sides[:2], 1), jnp.concatenate(sides[2:], 1)] + across


def mode_numbers():
    half = GRID // 2
    return np.concatenate([np.arange(half + 1), np.arange(1, half)])


def filter_table():
    k = jnp.asarray(mode_numbers(), jnp.float32)
    quarter = GRID // 4
    q = np.concatenate([np.arange(quarter + 1), np.arange(1, quarter)])
    weight = np.where((q == 0) | (q == quarter), 1.0, 2.0) / (GRID // 2)
    ky = jnp.asarray(np.stack([q, GRID // 2 - q], 1), jnp.float32)
    unit = 2.0 * math.pi / GRID
    squares = (
        (k * unit)[:, None, None, None] ** 2
        + (ky * unit)[None, :, :, None] ** 2
        + (k * unit)[None, None, None, :] ** 2
    )
    guarded = jnp.where(squares > 0, squares, 1.0)
    table = jnp.where(
        squares > 0, (1.0 - jnp.exp(-guarded / (4.0 * SCREEN * SCREEN))) / guarded, 0.0
    )
    table = table * jnp.asarray(weight, jnp.float32)[None, :, None, None]
    return table.reshape(GRID, GRID * GRID)


def rotate(c, s, cos, sin):
    return cos * c - sin * s, sin * c + cos * s


def forward(x):
    n = len(x)
    if n == 2:
        return [x[0] + x[1], x[0] - x[1]], {}
    ce, se = forward(x[0::2])
    co, so = forward(x[1::2])
    half, quarter = n // 2, n // 4
    c, s = [None] * (half + 1), {}
    c[0], c[half] = ce[0] + co[0], ce[0] - co[0]
    c[quarter], s[quarter] = ce[quarter], co[quarter]
    for q in range(1, quarter):
        if 8 * q == n:
            r = math.sqrt(0.5)
            a, b = (co[q] - so[q]) * r, (co[q] + so[q]) * r
        else:
            a, b = rotate(co[q], so[q], math.cos(2 * math.pi * q / n), math.sin(2 * math.pi * q / n))
        c[q], c[half - q] = ce[q] + a, ce[q] - a
        s[q], s[half - q] = b + se[q], b - se[q]
    return c, s


def backward(c, s):
    n = 2 * (len(c) - 1)
    if n == 2:
        return [c[0] + c[1], c[0] - c[1]]
    half, quarter = n // 2, n // 4
    ce, co, se, so = [None] * (quarter + 1), [None] * (quarter + 1), {}, {}
    ce[0], co[0] = c[0] + c[half], c[0] - c[half]
    ce[quarter], co[quarter] = c[quarter], s[quarter]
    for q in range(1, quarter):
        ce[q], a = c[q] + c[half - q], c[q] - c[half - q]
        b, se[q] = s[q] + s[half - q], s[q] - s[half - q]
        if 8 * q == n:
            r = math.sqrt(0.5)
            co[q], so[q] = (a + b) * r, (b - a) * r
        else:
            co[q], so[q] = rotate(a, b, math.cos(2 * math.pi * q / n), -math.sin(2 * math.pi * q / n))
    out = [None] * n
    out[0::2], out[1::2] = backward(ce, se), backward(co, so)
    return out


def twiddles(shape, q):
    odd = lax.broadcasted_iota(jnp.int32, shape, 1) >= shape[1] // 2
    angle = 2 * math.pi * q / GRID
    return jnp.where(odd, math.cos(angle), 1.0), jnp.where(odd, math.sin(angle), 0.0)


def halves(value):
    high = value.astype(jnp.bfloat16)
    return high, (value - high.astype(jnp.float32)).astype(jnp.bfloat16)


def along_z(tiles, double):
    high, rest = halves(jnp.concatenate(tiles, 0))
    out = jnp.dot(jnp.concatenate([high, rest], 1), double, preferred_element_type=jnp.float32)
    out = out[:, :LANES] + out[:, LANES:]
    step = tiles[0].shape[0]
    return [out[i * step : (i + 1) * step] for i in range(len(tiles))]


def along_x(value, double):
    length = value.shape[0]
    out = jnp.dot(double, jnp.concatenate(halves(value), 0), preferred_element_type=jnp.float32)
    return out[:length] + out[length:]


LANES = 128
PART = 4096
TABLE_PART = 512


def into_modes(densities):
    count = len(densities)
    quarter = count // 2
    c, s = forward(densities)
    for q in range(1, quarter):
        cos, sin = twiddles(densities[0].shape, q)
        c[q], s[q] = rotate(c[q], s[q], cos, sin)
    return c + [s[q] for q in range(1, quarter)]


def out_of_modes(values):
    quarter = len(values) // 2
    c, s = values[: quarter + 1], dict(enumerate(values[quarter + 1 :], 1))
    for q in range(1, quarter):
        cos, sin = twiddles(values[0].shape, q)
        c[q], s[q] = rotate(c[q], s[q], cos, -sin)
    return backward(c, s)


def filtered(tiles, table, z_forward, z_backward, x_forward, x_backward):
    value = along_x(jnp.concatenate(along_z(tiles, z_forward), 1), x_forward)
    value = along_x(value * table, x_backward)
    return along_z([value[:, i : i + LANES] for i in range(0, value.shape[1], LANES)], z_backward)


def columns(i):
    return slice(i * LANES, (i + 1) * LANES)


def exchange_kernel(orbital_ref, source_ref, filter_ref, *rest):
    constants, out_ref, work = rest
    length, cells = work.shape
    count = cells // LANES

    @pl.loop(0, length // 8)
    def _(block):
        rows = pl.ds(pl.multiple_of(block * 8, 8), 8)
        values = [
            orbital_ref[rows, columns(i)] * source_ref[0, rows, columns(i)] for i in range(count)
        ]
        for i, value in enumerate(into_modes(values)):
            work[rows, columns(i)] = value

    @pl.loop(0, cells // PART)
    def _(part):
        lanes = [pl.ds(pl.multiple_of(part * PART + i, LANES), LANES) for i in range(0, PART, LANES)]
        table = filter_ref[:, pl.ds(pl.multiple_of(part * PART, PART), PART)]
        tiles = filtered([work[:, lane] for lane in lanes], table, *unpack(constants))
        for lane, tile in zip(lanes, tiles):
            work[:, lane] = tile

    first = pl.program_id(0) == 0

    @pl.loop(0, length // 8)
    def _(block):
        rows = pl.ds(pl.multiple_of(block * 8, 8), 8)
        values = out_of_modes([work[rows, columns(i)] for i in range(count)])
        for i, value in enumerate(values):
            term = value * source_ref[0, rows, columns(i)] * -EXX_FRACTION
            out_ref[rows, columns(i)] = jnp.where(first, 0.0, out_ref[rows, columns(i)]) + term


def apply_exchange(orbital, sources):
    count, length, cells = sources.shape
    constants = jnp.asarray(matrices())
    whole = lambda shape: pl.BlockSpec(shape, lambda j: (0, 0))
    return pl.pallas_call(
        exchange_kernel,
        grid=(count,),
        out_shape=jax.ShapeDtypeStruct((length, cells), jnp.float32),
        in_specs=[
            whole((length, cells)),
            pl.BlockSpec((1, length, cells), lambda j: (j, 0, 0)),
            whole((length, cells)),
            whole(constants.shape),
        ],
        out_specs=whole((length, cells)),
        scratch_shapes=[pltpu.VMEM((length, cells), jnp.float32)],
        compiler_params=pltpu.CompilerParams(vmem_limit_bytes=32 * MIB),
        name="exchange",
    )(orbital, sources, filter_table(), constants)


GROUP = 8
COLUMNS = 4
LAG = 2
TABLE_PART = 512


def filter_part(part, length):
    shape = (length, TABLE_PART)
    half, quarter = length // 2, length // 4
    lane = lax.broadcasted_iota(jnp.int32, shape, 1) + part * TABLE_PART

    def mode(index):
        return jnp.where(index > half, index - half, index)

    row = lane >> 7
    q = jnp.where(row > quarter, row - quarter, row)
    ky = jnp.where((lane & half * 2) == 0, q, half - q)
    edge = jnp.logical_or(q == 0, q == quarter)
    squares = jnp.zeros(shape, jnp.float32)
    for k in (mode(lax.broadcasted_iota(jnp.int32, shape, 0)), ky, mode(lane & (length - 1))):
        squares = squares + (k.astype(jnp.float32) * (2.0 * math.pi / length)) ** 2
    guarded = jnp.where(squares > 0, squares, 1.0)
    table = (1.0 - jnp.exp(-guarded / (4.0 * SCREEN * SCREEN))) / guarded
    scale = -EXX_FRACTION / half
    return jnp.where(squares > 0, table, 0.0) * jnp.where(edge, scale, 2.0 * scale)


def fused_kernel(chips, row, x_ref, matrix_ref, out_ref, *rest):
    (constants, source, orbital, table, work, total, partial, copy_sem, swap_send, swap_recv, beside_send,
     beside_recv, local_sem, scatter_send, up_send, far_send, y_send, x_send, own_recv, y_recv, x_recv, d_recv,
     part_send, part_recv, back_send, back_recv, done_send, done_recv) = rest
    band, half = lax.axis_index("band"), lax.axis_index("fft")
    chip, core = band // 2, band % 2
    side, layer = chip % row, chip // row
    owned, planes, cells = x_ref.shape
    length = 2 * planes
    other = 1 - half
    groups, width = planes // GROUP, cells // COLUMNS
    share = groups // 2
    per_orbital = 2 * groups
    pieces = owned * per_orbital
    root, has_up, bottom = chip == 0, layer % 2 == 0, layer == 0
    across_band, beside_band = band + 2 - 4 * side, band + 1 - 2 * core
    to_y = {"band": band, "fft": other}
    to_core = {"band": beside_band, "fft": half}
    to_cross = {"band": beside_band, "fft": other}
    to_x = {"band": across_band, "fft": half}
    to_diagonal = {"band": across_band, "fft": other}
    to_up = {"band": band + 2 * row, "fft": half}
    to_far = {"band": band + 4 * row, "fft": half}
    to_down = {"band": band - 2 * row * jnp.where(layer == 2, 2, 1), "fft": half}
    own = 2 * side + half
    over_y, over_x, over_both = own + 1 - 2 * half, own + 2 - 4 * side, 3 - own

    barrier = pltpu.get_barrier_semaphore()

    def greet(target):
        pl.semaphore_signal(barrier, inc=1, device_id=target, device_id_type=MESH)

    greet(to_y)
    greet(to_core)
    greet(to_cross)
    greet(to_x)

    @pl.when(has_up)
    def _():
        greet(to_up)

    @pl.when(jnp.logical_not(bottom))
    def _():
        greet(to_down)

    @pl.when(bottom)
    def _():
        greet(to_diagonal)
        greet(to_far)

    pl.semaphore_wait(barrier, 5 + has_up.astype(jnp.int32) + bottom.astype(jnp.int32))

    def remote(src, dst, send, recv, target):
        return pltpu.make_async_remote_copy(
            src_ref=src, dst_ref=dst, send_sem=send, recv_sem=recv, device_id=target, device_id_type=MESH
        )

    def send(block, send_sem, recv_sem, target):
        remote(block, block, send_sem, recv_sem, target).start()

    def arrived(block, recv):
        remote(block, block, swap_send, recv, to_y).wait_recv()

    def sent(block, send_sem):
        remote(block, block, send_sem, swap_recv, to_y).wait_send()

    def group_rows(group):
        return pl.ds(pl.multiple_of(group * GROUP, GROUP), GROUP)

    def place(q, column):
        rows = group_rows((q % per_orbital) // 2)
        return q // per_orbital, q % 2, rows, pl.ds(pl.multiple_of(column * width, width), width)

    def piece(q, column):
        return source.at[place(q, column)]

    def outer(q, column):
        o, _, rows, lanes = place(q, column)
        return x_ref.at[o, rows, lanes]

    def local(q):
        return pltpu.make_async_copy(outer(q, own), piece(q, own), local_sem.at[q])

    def swap(k):
        rows, lanes = group_rows(k // 2), pl.ds(pl.multiple_of(k % 2 * (cells // 2), cells // 2), cells // 2)
        return remote(
            x_ref.at[other, rows, lanes], orbital.at[core, half, rows, lanes], swap_send, swap_recv, to_y
        )

    @pl.when(root)
    def _():
        @pl.loop(0, pieces)
        def _(q):
            @pl.when(q % 2 == half)
            def _():
                for i, (column, target) in enumerate(
                    ((over_x, to_x), (over_both, to_diagonal), (over_y, to_y))
                ):
                    remote(
                        outer(q, column), piece(q, column), scatter_send.at[i], own_recv.at[q], target
                    ).start()
                local(q).start()

    remote(x_ref.at[half], orbital.at[core, half], beside_send.at[0], beside_recv.at[0], to_core).start()
    keep = pltpu.make_async_copy(x_ref.at[half], orbital.at[core, half], copy_sem.at[0])
    keep.start()
    fetch = pltpu.make_async_copy(matrix_ref, constants, copy_sem.at[1])
    fetch.start()

    def within(q):
        return jnp.logical_and(q >= 0, q < pieces)

    def event(k):
        @pl.when(k < pieces)
        def _():
            block = piece(k, own)
            at_home = jnp.logical_and(root, k % 2 == half)

            @pl.when(at_home)
            def _():
                local(k).wait()

            @pl.when(jnp.logical_not(at_home))
            def _():
                arrived(block, own_recv.at[k])

            @pl.when(bottom)
            def _():
                send(block, far_send, own_recv.at[k], to_far)

            @pl.when(has_up)
            def _():
                send(block, up_send, own_recv.at[k], to_up)

            send(block, y_send, y_recv.at[k], to_y)
            send(block, x_send, x_recv.at[k], to_x)

        @pl.when(k < per_orbital)
        def _():
            swap(k).start()

        q = k - LAG

        @pl.when(within(q))
        def _():
            block = piece(q, over_y)
            arrived(block, y_recv.at[q])
            send(block, x_send, d_recv.at[q], to_x)
            arrived(piece(q, over_x), x_recv.at[q])

        r = k - 2 * LAG

        @pl.when(within(r))
        def _():
            arrived(piece(r, over_both), d_recv.at[r])

    count = cells // LANES
    ahead = per_orbital + 2 * LAG

    @pl.loop(0, ahead)
    def _(k):
        event(k)

        @pl.when(k < cells // TABLE_PART)
        def _():
            lanes = pl.ds(pl.multiple_of(k * TABLE_PART, TABLE_PART), TABLE_PART)
            table[:, lanes] = filter_part(k, length)

        @pl.when(k == ahead - 2)
        def _():
            arrived(orbital.at[core, other], swap_recv)
            send(orbital.at[core, other], beside_send.at[1], beside_recv.at[1], to_core)

    keep.wait()
    arrived(orbital.at[1 - core, half], beside_recv.at[0])
    arrived(orbital.at[1 - core, other], beside_recv.at[1])
    fetch.wait()

    def slot(index, number):
        @pl.when(index == 0)
        def _():
            event(ahead + number)

    @pl.loop(0, 2 * owned)
    def _(index):
        which, o = index % 2, index // 2

        @pl.when(which == 0)
        def _():
            @pl.loop(0, per_orbital)
            def _(block):
                @pl.when(block % 2 == 0)
                def _():
                    slot(index, block // 2)

                h, rows, to = block // groups, group_rows(block % groups), group_rows(block)

                @pl.loop(0, 2)
                def _(field):
                    values = [
                        orbital[field, h, rows, columns(i)] * source[o, h, rows, columns(i)]
                        for i in range(count)
                    ]
                    for i, value in enumerate(into_modes(values)):
                        work[2 * o + field, to, columns(i)] = value

        for part in range(cells // PART):
            slot(index, 4)
            slot(index, 5)
            lanes = [slice(part * PART + i, part * PART + i + LANES) for i in range(0, PART, LANES)]
            whole = table[:, part * PART : (part + 1) * PART]
            tiles = filtered([work[index, :, lane] for lane in lanes], whole, *unpack(constants))
            for lane, tile in zip(lanes, tiles):
                work[index, :, lane] = tile

        @pl.loop(0, per_orbital)
        def _(step):
            @pl.when(step % 4 == 0)
            def _():
                slot(index, 6 + step // 4)

            mine = step // groups
            n = step % groups
            h = jnp.where(n < share, other, half)
            holder = jnp.where(mine == 1, core, 1 - core)
            group = holder * share + n % share
            rows, to = group_rows(group), group_rows(h * groups + group)
            values = out_of_modes([work[index, to, columns(i)] for i in range(count)])
            for i, value in enumerate(values):
                term = value * source[o, h, rows, columns(i)]
                earlier = jnp.where(o == 0, 0.0, total[which, h, rows, columns(i)])
                total[which, h, rows, columns(i)] = earlier + term

            block = total.at[which, h, rows]
            last = o == owned - 1

            @pl.when(jnp.logical_and(last, mine == 0))
            def _():
                remote(block, partial.at[which, n], part_send, part_recv.at[which, n], to_core).start()

            @pl.when(jnp.logical_and(last, mine == 1))
            def _():
                arrived(partial.at[which, n], part_recv.at[which, n])
                for i in range(count):
                    total[which, h, rows, columns(i)] += partial[which, n, :, columns(i)]
                goal = out_ref.at[half, rows]

                @pl.when(n < share)
                def _():
                    remote(
                        block, goal, back_send, back_recv.at[core], {"band": 2 * chip + which, "fft": other}
                    ).start()

                @pl.when(jnp.logical_and(n >= share, which == core))
                def _():
                    pltpu.make_async_copy(block, goal, copy_sem.at[2]).start()

                @pl.when(jnp.logical_and(n >= share, which != core))
                def _():
                    remote(block, goal, done_send, done_recv, to_core).start()

    @pl.when(has_up)
    def _():
        sent(orbital.at[0, 0], up_send)

    @pl.when(bottom)
    def _():
        sent(orbital.at[0, 0], far_send)

    @pl.when(root)
    def _():
        for i in range(3):
            sent(orbital.at[0, 0, : planes // 2], scatter_send.at[i])

    sent(orbital.at[0, 0], y_send)
    sent(orbital.at[0], x_send)
    sent(orbital.at[0, 0], beside_send.at[0])
    sent(orbital.at[0, 0], beside_send.at[1])
    sent(orbital.at[0, 0], swap_send)
    sent(total.at[0], part_send)
    sent(total.at[0, 0], back_send)
    first, second = out_ref.at[other, : planes // 2], out_ref.at[other, planes // 2 :]
    sent(total.at[0, 0, : planes // 2], done_send)
    arrived(first, done_recv)
    pltpu.make_async_copy(total.at[0, 0, : planes // 2], first, copy_sem.at[2]).wait()
    arrived(first, back_recv.at[0])
    arrived(second, back_recv.at[1])


def two_halves(bands, row, orbitals):
    owned, planes, cells = orbitals.shape
    groups = planes // GROUP
    count = owned * 2 * groups
    dma = pltpu.SemaphoreType.DMA
    constants = jnp.asarray(matrices())
    grid = lambda *lead: pltpu.VMEM((*lead, planes, cells), jnp.float32)
    return pl.pallas_call(
        functools.partial(fused_kernel, bands // 2, row),
        out_shape=jax.ShapeDtypeStruct(orbitals.shape, jnp.float32),
        in_specs=[pl.BlockSpec(memory_space=pl.ANY)] * 2,
        out_specs=pl.BlockSpec(memory_space=pl.ANY),
        scratch_shapes=[
            pltpu.VMEM(constants.shape, jnp.bfloat16),
            grid(owned, 2),
            grid(2, 2),
            pltpu.VMEM((2 * planes, cells), jnp.float32),
            pltpu.VMEM((2 * owned, 2 * planes, cells), jnp.float32),
            grid(2, 2),
            pltpu.VMEM((2, groups, GROUP, cells), jnp.float32),
        ]
        + [dma((3,)), dma, dma, dma((2,)), dma((2,)), dma((count,)), dma((3,))]
        + [dma] * 4
        + [dma((count,))] * 4
        + [dma, dma((2, groups)), dma, dma((2,)), dma, dma],
        compiler_params=pltpu.CompilerParams(
            collective_id=0, has_side_effects=True, vmem_limit_bytes=60 * MIB
        ),
        name="exchange",
    )(orbitals, constants)


def many_parts(parts, orbitals):
    owned = orbitals.shape[0]
    place, band = lax.axis_index("fft"), lax.axis_index("band")
    fields = lax.all_gather(orbitals, "fft", axis=1, tiled=True)
    held = jnp.concatenate([jnp.where(band == r, fields, 0.0) for r in range(ROUNDS)], 0)
    sources = lax.psum(held, "band")
    groups = max(parts // owned, 1)
    share = sources.shape[0] // groups
    mine = lax.dynamic_slice_in_dim(sources, (place // owned) * share, share, 0)
    which = place % owned
    result = apply_exchange(lax.dynamic_index_in_dim(fields, which, 0, False), mine)
    placed = jnp.where(jnp.arange(owned)[:, None, None] == which, result[None], 0.0)
    return lax.psum_scatter(placed, "fft", scatter_dimension=1, tiled=True)


def solution(mesh):
    parts = mesh.shape["fft"]
    if parts == 2 and mesh.shape["band"] == 16:
        body = functools.partial(two_halves, mesh.shape["band"], 2)
    else:
        body = functools.partial(many_parts, parts)
    return jax.shard_map(
        body, mesh=mesh, in_specs=(P("band", "fft", None),), out_specs=P("band", "fft", None), check_vma=False
    )
```

```python
import functools
import math

import jax
import jax.numpy as jnp
import numpy as np
from jax import lax
from jax.experimental import pallas as pl
from jax.experimental.pallas import tpu as pltpu
from jax.sharding import PartitionSpec as P

GRID = 64
ROUNDS = 2
EXX_FRACTION = 0.25
SCREEN = 0.05
MESH = pl.DeviceIdType.MESH
MIB = 1024 * 1024


def real_modes(length):
    n = np.arange(length)
    rows = [np.cos(2 * np.pi * q * n / length) for q in range(length // 2 + 1)]
    rows += [np.sin(2 * np.pi * q * n / length) for q in range(1, length // 2)]
    matrix = np.array(rows)
    return matrix / np.sqrt((matrix**2).sum(1, keepdims=True))


def split(matrix):
    high = matrix.astype(jnp.bfloat16)
    return high, (matrix - high.astype(np.float64)).astype(jnp.bfloat16)


def matrices():
    modes = real_modes(GRID)
    z_forward = np.kron(np.array([[1.0, 1.0], [1.0, -1.0]]) / np.sqrt(2.0), modes.T)
    out = []
    for matrix in (z_forward, z_forward.T):
        high, low = split(matrix)
        out += [np.concatenate([high, high], 0), np.concatenate([low, np.zeros_like(low)], 0)]
    for matrix in (modes, modes.T):
        high, low = split(matrix)
        out.append(
            np.concatenate(
                [np.concatenate([high, high], 1), np.concatenate([low, np.zeros_like(low)], 1)], 0
            )
        )
    return np.concatenate(out, 0)


def unpack(ref):
    sides = [ref[i * 256 : (i + 1) * 256, :] for i in range(4)]
    across = [ref[1024 + i * 128 : 1152 + i * 128, :] for i in range(2)]
    return [jnp.concatenate(sides[:2], 1), jnp.concatenate(sides[2:], 1)] + across


def mode_numbers():
    half = GRID // 2
    return np.concatenate([np.arange(half + 1), np.arange(1, half)])


def filter_table():
    k = jnp.asarray(mode_numbers(), jnp.float32)
    quarter = GRID // 4
    q = np.concatenate([np.arange(quarter + 1), np.arange(1, quarter)])
    weight = np.where((q == 0) | (q == quarter), 1.0, 2.0) / (GRID // 2)
    ky = jnp.asarray(np.stack([q, GRID // 2 - q], 1), jnp.float32)
    unit = 2.0 * math.pi / GRID
    squares = (
        (k * unit)[:, None, None, None] ** 2
        + (ky * unit)[None, :, :, None] ** 2
        + (k * unit)[None, None, None, :] ** 2
    )
    guarded = jnp.where(squares > 0, squares, 1.0)
    table = jnp.where(
        squares > 0, (1.0 - jnp.exp(-guarded / (4.0 * SCREEN * SCREEN))) / guarded, 0.0
    )
    table = table * jnp.asarray(weight, jnp.float32)[None, :, None, None]
    return table.reshape(GRID, GRID * GRID)


def rotate(c, s, cos, sin):
    return cos * c - sin * s, sin * c + cos * s


def forward(x):
    n = len(x)
    if n == 2:
        return [x[0] + x[1], x[0] - x[1]], {}
    ce, se = forward(x[0::2])
    co, so = forward(x[1::2])
    half, quarter = n // 2, n // 4
    c, s = [None] * (half + 1), {}
    c[0], c[half] = ce[0] + co[0], ce[0] - co[0]
    c[quarter], s[quarter] = ce[quarter], co[quarter]
    for q in range(1, quarter):
        if 8 * q == n:
            r = math.sqrt(0.5)
            a, b = (co[q] - so[q]) * r, (co[q] + so[q]) * r
        else:
            a, b = rotate(co[q], so[q], math.cos(2 * math.pi * q / n), math.sin(2 * math.pi * q / n))
        c[q], c[half - q] = ce[q] + a, ce[q] - a
        s[q], s[half - q] = b + se[q], b - se[q]
    return c, s


def backward(c, s):
    n = 2 * (len(c) - 1)
    if n == 2:
        return [c[0] + c[1], c[0] - c[1]]
    half, quarter = n // 2, n // 4
    ce, co, se, so = [None] * (quarter + 1), [None] * (quarter + 1), {}, {}
    ce[0], co[0] = c[0] + c[half], c[0] - c[half]
    ce[quarter], co[quarter] = c[quarter], s[quarter]
    for q in range(1, quarter):
        ce[q], a = c[q] + c[half - q], c[q] - c[half - q]
        b, se[q] = s[q] + s[half - q], s[q] - s[half - q]
        if 8 * q == n:
            r = math.sqrt(0.5)
            co[q], so[q] = (a + b) * r, (b - a) * r
        else:
            co[q], so[q] = rotate(a, b, math.cos(2 * math.pi * q / n), -math.sin(2 * math.pi * q / n))
    out = [None] * n
    out[0::2], out[1::2] = backward(ce, se), backward(co, so)
    return out


def twiddles(shape, q):
    odd = lax.broadcasted_iota(jnp.int32, shape, 1) >= shape[1] // 2
    angle = 2 * math.pi * q / GRID
    return jnp.where(odd, math.cos(angle), 1.0), jnp.where(odd, math.sin(angle), 0.0)


def halves(value):
    high = value.astype(jnp.bfloat16)
    return high, (value - high.astype(jnp.float32)).astype(jnp.bfloat16)


def along_z(tiles, double):
    high, rest = halves(jnp.concatenate(tiles, 0))
    out = jnp.dot(jnp.concatenate([high, rest], 1), double, preferred_element_type=jnp.float32)
    out = out[:, :LANES] + out[:, LANES:]
    step = tiles[0].shape[0]
    return [out[i * step : (i + 1) * step] for i in range(len(tiles))]


def along_x(value, double):
    length = value.shape[0]
    out = jnp.dot(double, jnp.concatenate(halves(value), 0), preferred_element_type=jnp.float32)
    return out[:length] + out[length:]


LANES = 128
PART = 4096
TABLE_PART = 512


def into_modes(densities):
    count = len(densities)
    quarter = count // 2
    c, s = forward(densities)
    for q in range(1, quarter):
        cos, sin = twiddles(densities[0].shape, q)
        c[q], s[q] = rotate(c[q], s[q], cos, sin)
    return c + [s[q] for q in range(1, quarter)]


def out_of_modes(values):
    quarter = len(values) // 2
    c, s = values[: quarter + 1], dict(enumerate(values[quarter + 1 :], 1))
    for q in range(1, quarter):
        cos, sin = twiddles(values[0].shape, q)
        c[q], s[q] = rotate(c[q], s[q], cos, -sin)
    return backward(c, s)


def filtered(tiles, table, z_forward, z_backward, x_forward, x_backward):
    value = along_x(jnp.concatenate(along_z(tiles, z_forward), 1), x_forward)
    value = along_x(value * table, x_backward)
    return along_z([value[:, i : i + LANES] for i in range(0, value.shape[1], LANES)], z_backward)


def columns(i):
    return slice(i * LANES, (i + 1) * LANES)


def exchange_kernel(orbital_ref, source_ref, filter_ref, *rest):
    constants, out_ref, work = rest
    length, cells = work.shape
    count = cells // LANES

    @pl.loop(0, length // 8)
    def _(block):
        rows = pl.ds(pl.multiple_of(block * 8, 8), 8)
        values = [
            orbital_ref[rows, columns(i)] * source_ref[0, rows, columns(i)] for i in range(count)
        ]
        for i, value in enumerate(into_modes(values)):
            work[rows, columns(i)] = value

    @pl.loop(0, cells // PART)
    def _(part):
        lanes = [pl.ds(pl.multiple_of(part * PART + i, LANES), LANES) for i in range(0, PART, LANES)]
        table = filter_ref[:, pl.ds(pl.multiple_of(part * PART, PART), PART)]
        tiles = filtered([work[:, lane] for lane in lanes], table, *unpack(constants))
        for lane, tile in zip(lanes, tiles):
            work[:, lane] = tile

    first = pl.program_id(0) == 0

    @pl.loop(0, length // 8)
    def _(block):
        rows = pl.ds(pl.multiple_of(block * 8, 8), 8)
        values = out_of_modes([work[rows, columns(i)] for i in range(count)])
        for i, value in enumerate(values):
            term = value * source_ref[0, rows, columns(i)] * -EXX_FRACTION
            out_ref[rows, columns(i)] = jnp.where(first, 0.0, out_ref[rows, columns(i)]) + term


def apply_exchange(orbital, sources):
    count, length, cells = sources.shape
    constants = jnp.asarray(matrices())
    whole = lambda shape: pl.BlockSpec(shape, lambda j: (0, 0))
    return pl.pallas_call(
        exchange_kernel,
        grid=(count,),
        out_shape=jax.ShapeDtypeStruct((length, cells), jnp.float32),
        in_specs=[
            whole((length, cells)),
            pl.BlockSpec((1, length, cells), lambda j: (j, 0, 0)),
            whole((length, cells)),
            whole(constants.shape),
        ],
        out_specs=whole((length, cells)),
        scratch_shapes=[pltpu.VMEM((length, cells), jnp.float32)],
        compiler_params=pltpu.CompilerParams(vmem_limit_bytes=32 * MIB),
        name="exchange",
    )(orbital, sources, filter_table(), constants)


GROUP = 8
COLUMNS = 4
LAG = 3
TABLE_PART = 512


def filter_part(part, length):
    shape = (length, TABLE_PART)
    half, quarter = length // 2, length // 4
    lane = lax.broadcasted_iota(jnp.int32, shape, 1) + part * TABLE_PART

    def mode(index):
        return jnp.where(index > half, index - half, index)

    row = lane >> 7
    q = jnp.where(row > quarter, row - quarter, row)
    ky = jnp.where((lane & half * 2) == 0, q, half - q)
    edge = jnp.logical_or(q == 0, q == quarter)
    squares = jnp.zeros(shape, jnp.float32)
    for k in (mode(lax.broadcasted_iota(jnp.int32, shape, 0)), ky, mode(lane & (length - 1))):
        squares = squares + (k.astype(jnp.float32) * (2.0 * math.pi / length)) ** 2
    guarded = jnp.where(squares > 0, squares, 1.0)
    table = (1.0 - jnp.exp(-guarded / (4.0 * SCREEN * SCREEN))) / guarded
    scale = 1.0 / half
    return jnp.where(squares > 0, table, 0.0) * jnp.where(edge, scale, 2.0 * scale)


def fused_kernel(chips, row, x_ref, matrix_ref, out_ref, *rest):
    (constants, source, orbital, table, work, total, partial, copy_sem, swap_send, swap_recv, beside_send,
     beside_recv, local_sem, scatter_send, up_send, far_send, y_send, x_send, own_recv, y_recv, x_recv, d_recv,
     part_send, part_recv, back_send, back_recv, done_send, done_recv) = rest
    band, half = lax.axis_index("band"), lax.axis_index("fft")
    chip, core = band // 2, band % 2
    side, layer = chip % row, chip // row
    owned, planes, cells = x_ref.shape
    length = 2 * planes
    other = 1 - half
    groups, width = planes // GROUP, cells // COLUMNS
    share = groups // 2
    per_orbital = 2 * groups
    pieces = owned * per_orbital
    root, has_up, bottom = chip == 0, layer % 2 == 0, layer == 0
    across_band, beside_band = band + 2 - 4 * side, band + 1 - 2 * core
    to_y = {"band": band, "fft": other}
    to_core = {"band": beside_band, "fft": half}
    to_cross = {"band": beside_band, "fft": other}
    to_x = {"band": across_band, "fft": half}
    to_diagonal = {"band": across_band, "fft": other}
    to_up = {"band": band + 2 * row, "fft": half}
    to_far = {"band": band + 4 * row, "fft": half}
    to_down = {"band": band - 2 * row * jnp.where(layer == 2, 2, 1), "fft": half}
    own = 2 * side + half
    over_y, over_x, over_both = own + 1 - 2 * half, own + 2 - 4 * side, 3 - own

    barrier = pltpu.get_barrier_semaphore()

    def greet(target):
        pl.semaphore_signal(barrier, inc=1, device_id=target, device_id_type=MESH)

    greet(to_y)
    greet(to_core)
    greet(to_cross)
    greet(to_x)

    @pl.when(has_up)
    def _():
        greet(to_up)

    @pl.when(jnp.logical_not(bottom))
    def _():
        greet(to_down)

    @pl.when(bottom)
    def _():
        greet(to_diagonal)
        greet(to_far)

    pl.semaphore_wait(barrier, 5 + has_up.astype(jnp.int32) + bottom.astype(jnp.int32))

    def remote(src, dst, send, recv, target):
        return pltpu.make_async_remote_copy(
            src_ref=src, dst_ref=dst, send_sem=send, recv_sem=recv, device_id=target, device_id_type=MESH
        )

    def send(block, send_sem, recv_sem, target):
        remote(block, block, send_sem, recv_sem, target).start()

    def arrived(block, recv):
        remote(block, block, swap_send, recv, to_y).wait_recv()

    def sent(block, send_sem):
        remote(block, block, send_sem, swap_recv, to_y).wait_send()

    def group_rows(group):
        return pl.ds(pl.multiple_of(group * GROUP, GROUP), GROUP)

    def place(q, column):
        rows = group_rows((q % per_orbital) // 2)
        return q // per_orbital, q % 2, rows, pl.ds(pl.multiple_of(column * width, width), width)

    def piece(q, column):
        return source.at[place(q, column)]

    def outer(q, column):
        o, _, rows, lanes = place(q, column)
        return x_ref.at[o, rows, lanes]

    def local(q):
        return pltpu.make_async_copy(outer(q, own), piece(q, own), local_sem.at[q])

    def swap(k):
        rows, lanes = group_rows(k // 2), pl.ds(pl.multiple_of(k % 2 * (cells // 2), cells // 2), cells // 2)
        return remote(
            x_ref.at[other, rows, lanes], orbital.at[core, half, rows, lanes], swap_send, swap_recv, to_y
        )

    @pl.when(root)
    def _():
        @pl.loop(0, pieces)
        def _(q):
            @pl.when(q % 2 == half)
            def _():
                for i, (column, target) in enumerate(
                    ((over_x, to_x), (over_both, to_diagonal), (over_y, to_y))
                ):
                    remote(
                        outer(q, column), piece(q, column), scatter_send.at[i], own_recv.at[q], target
                    ).start()
                local(q).start()

    remote(x_ref.at[half], orbital.at[core, half], beside_send.at[0], beside_recv.at[0], to_core).start()
    keep = pltpu.make_async_copy(x_ref.at[half], orbital.at[core, half], copy_sem.at[0])
    keep.start()
    fetch = pltpu.make_async_copy(matrix_ref, constants, copy_sem.at[1])
    fetch.start()

    def within(q):
        return jnp.logical_and(q >= 0, q < pieces)

    def event(k):
        @pl.when(k < pieces)
        def _():
            block = piece(k, own)
            at_home = jnp.logical_and(root, k % 2 == half)

            @pl.when(at_home)
            def _():
                local(k).wait()

            @pl.when(jnp.logical_not(at_home))
            def _():
                arrived(block, own_recv.at[k])

            @pl.when(bottom)
            def _():
                send(block, far_send, own_recv.at[k], to_far)

            @pl.when(has_up)
            def _():
                send(block, up_send, own_recv.at[k], to_up)

            send(block, y_send, y_recv.at[k], to_y)
            send(block, x_send, x_recv.at[k], to_x)

        @pl.when(k < per_orbital)
        def _():
            swap(k).start()

        q = k - LAG

        @pl.when(within(q))
        def _():
            block = piece(q, over_y)
            arrived(block, y_recv.at[q])
            send(block, x_send, d_recv.at[q], to_x)
            arrived(piece(q, over_x), x_recv.at[q])

        r = k - 2 * LAG

        @pl.when(within(r))
        def _():
            arrived(piece(r, over_both), d_recv.at[r])

    count = cells // LANES
    ahead = per_orbital + 2 * LAG

    @pl.loop(0, ahead)
    def _(k):
        event(k)

        @pl.when(k < cells // TABLE_PART)
        def _():
            lanes = pl.ds(pl.multiple_of(k * TABLE_PART, TABLE_PART), TABLE_PART)
            table[:, lanes] = filter_part(k, length)

        @pl.when(k == ahead - 2)
        def _():
            arrived(orbital.at[core, other], swap_recv)
            send(orbital.at[core, other], beside_send.at[1], beside_recv.at[1], to_core)

    keep.wait()
    arrived(orbital.at[1 - core, half], beside_recv.at[0])
    arrived(orbital.at[1 - core, other], beside_recv.at[1])
    fetch.wait()

    def slot(index, number):
        @pl.when(index == 0)
        def _():
            event(ahead + number)

    @pl.loop(0, 2 * owned)
    def _(index):
        which, o = index % 2, index // 2

        @pl.when(which == 0)
        def _():
            @pl.loop(0, per_orbital)
            def _(block):
                @pl.when(block % 2 == 0)
                def _():
                    slot(index, block // 2)

                h, rows, to = block // groups, group_rows(block % groups), group_rows(block)

                @pl.loop(0, 2)
                def _(field):
                    values = [
                        orbital[field, h, rows, columns(i)] * source[o, h, rows, columns(i)]
                        for i in range(count)
                    ]
                    for i, value in enumerate(into_modes(values)):
                        work[2 * o + field, to, columns(i)] = value

        for part in range(cells // PART):
            slot(index, 4)
            slot(index, 5)
            lanes = [slice(part * PART + i, part * PART + i + LANES) for i in range(0, PART, LANES)]
            whole = table[:, part * PART : (part + 1) * PART]
            tiles = filtered([work[index, :, lane] for lane in lanes], whole, *unpack(constants))
            for lane, tile in zip(lanes, tiles):
                work[index, :, lane] = tile

        @pl.loop(0, per_orbital)
        def _(step):
            @pl.when(step % 4 == 0)
            def _():
                slot(index, 6 + step // 4)

            mine = step // groups
            n = step % groups
            h = jnp.where(n < share, other, half)
            holder = jnp.where(mine == 1, core, 1 - core)
            group = holder * share + n % share
            rows, to = group_rows(group), group_rows(h * groups + group)
            values = out_of_modes([work[index, to, columns(i)] for i in range(count)])
            for i, value in enumerate(values):
                term = value * source[o, h, rows, columns(i)]
                earlier = jnp.where(o == 0, 0.0, total[which, h, rows, columns(i)])
                total[which, h, rows, columns(i)] = earlier + term

            block = total.at[which, h, rows]
            last = o == owned - 1

            @pl.when(jnp.logical_and(last, mine == 0))
            def _():
                remote(block, partial.at[which, n], part_send, part_recv.at[which, n], to_core).start()

            @pl.when(jnp.logical_and(last, mine == 1))
            def _():
                arrived(partial.at[which, n], part_recv.at[which, n])
                for i in range(count):
                    total[which, h, rows, columns(i)] += partial[which, n, :, columns(i)]
                goal = out_ref.at[half, rows]

                @pl.when(n < share)
                def _():
                    remote(
                        block, goal, back_send, back_recv.at[core], {"band": 2 * chip + which, "fft": other}
                    ).start()

                @pl.when(jnp.logical_and(n >= share, which == core))
                def _():
                    pltpu.make_async_copy(block, goal, copy_sem.at[2]).start()

                @pl.when(jnp.logical_and(n >= share, which != core))
                def _():
                    remote(block, goal, done_send, done_recv, to_core).start()

    @pl.when(has_up)
    def _():
        sent(orbital.at[0, 0], up_send)

    @pl.when(bottom)
    def _():
        sent(orbital.at[0, 0], far_send)

    @pl.when(root)
    def _():
        for i in range(3):
            sent(orbital.at[0, 0, : planes // 2], scatter_send.at[i])

    sent(orbital.at[0, 0], y_send)
    sent(orbital.at[0], x_send)
    sent(orbital.at[0, 0], beside_send.at[0])
    sent(orbital.at[0, 0], beside_send.at[1])
    sent(orbital.at[0, 0], swap_send)
    sent(total.at[0], part_send)
    sent(total.at[0, 0], back_send)
    first, second = out_ref.at[other, : planes // 2], out_ref.at[other, planes // 2 :]
    sent(total.at[0, 0, : planes // 2], done_send)
    arrived(first, done_recv)
    pltpu.make_async_copy(total.at[0, 0, : planes // 2], first, copy_sem.at[2]).wait()
    arrived(first, back_recv.at[0])
    arrived(second, back_recv.at[1])


def two_halves(bands, row, orbitals):
    owned, planes, cells = orbitals.shape
    groups = planes // GROUP
    count = owned * 2 * groups
    dma = pltpu.SemaphoreType.DMA
    constants = jnp.asarray(matrices())
    grid = lambda *lead: pltpu.VMEM((*lead, planes, cells), jnp.float32)
    exchange = pl.pallas_call(
        functools.partial(fused_kernel, bands // 2, row),
        out_shape=jax.ShapeDtypeStruct(orbitals.shape, jnp.float32),
        in_specs=[pl.BlockSpec(memory_space=pl.ANY)] * 2,
        out_specs=pl.BlockSpec(memory_space=pl.ANY),
        scratch_shapes=[
            pltpu.VMEM(constants.shape, jnp.bfloat16),
            grid(owned, 2),
            grid(2, 2),
            pltpu.VMEM((2 * planes, cells), jnp.float32),
            pltpu.VMEM((2 * owned, 2 * planes, cells), jnp.float32),
            grid(2, 2),
            pltpu.VMEM((2, groups, GROUP, cells), jnp.float32),
        ]
        + [dma((3,)), dma, dma, dma((2,)), dma((2,)), dma((count,)), dma((3,))]
        + [dma] * 4
        + [dma((count,))] * 4
        + [dma, dma((2, groups)), dma, dma((2,)), dma, dma],
        compiler_params=pltpu.CompilerParams(
            collective_id=0, has_side_effects=True, vmem_limit_bytes=60 * MIB
        ),
        name="exchange",
    )(orbitals, constants)
    return -EXX_FRACTION * exchange


def many_parts(parts, orbitals):
    owned = orbitals.shape[0]
    place, band = lax.axis_index("fft"), lax.axis_index("band")
    fields = lax.all_gather(orbitals, "fft", axis=1, tiled=True)
    held = jnp.concatenate([jnp.where(band == r, fields, 0.0) for r in range(ROUNDS)], 0)
    sources = lax.psum(held, "band")
    groups = max(parts // owned, 1)
    share = sources.shape[0] // groups
    mine = lax.dynamic_slice_in_dim(sources, (place // owned) * share, share, 0)
    which = place % owned
    result = apply_exchange(lax.dynamic_index_in_dim(fields, which, 0, False), mine)
    placed = jnp.where(jnp.arange(owned)[:, None, None] == which, result[None], 0.0)
    return lax.psum_scatter(placed, "fft", scatter_dimension=1, tiled=True)


def solution(mesh):
    parts = mesh.shape["fft"]
    if parts == 2 and mesh.shape["band"] == 16:
        body = functools.partial(two_halves, mesh.shape["band"], 2)
    else:
        body = functools.partial(many_parts, parts)
    return jax.shard_map(
        body, mesh=mesh, in_specs=(P("band", "fft", None),), out_specs=P("band", "fft", None), check_vma=False
    )
```

```python
import functools
import math

import jax
import jax.numpy as jnp
import numpy as np
from jax import lax
from jax.experimental import pallas as pl
from jax.experimental.pallas import tpu as pltpu
from jax.sharding import PartitionSpec as P

GRID = 64
ROUNDS = 2
EXX_FRACTION = 0.25
SCREEN = 0.05
MESH = pl.DeviceIdType.MESH
MIB = 1024 * 1024


def real_modes(length):
    n = np.arange(length)
    rows = [np.cos(2 * np.pi * q * n / length) for q in range(length // 2 + 1)]
    rows += [np.sin(2 * np.pi * q * n / length) for q in range(1, length // 2)]
    matrix = np.array(rows)
    return matrix / np.sqrt((matrix**2).sum(1, keepdims=True))


def split(matrix):
    high = matrix.astype(jnp.bfloat16)
    return high, (matrix - high.astype(np.float64)).astype(jnp.bfloat16)


def matrices():
    modes = real_modes(GRID)
    z_forward = np.kron(np.array([[1.0, 1.0], [1.0, -1.0]]) / np.sqrt(2.0), modes.T)
    out = []
    for matrix in (z_forward, z_forward.T):
        high, low = split(matrix)
        out += [np.concatenate([high, high], 0), np.concatenate([low, np.zeros_like(low)], 0)]
    for matrix in (modes, modes.T):
        high, low = split(matrix)
        out.append(
            np.concatenate(
                [np.concatenate([high, high], 1), np.concatenate([low, np.zeros_like(low)], 1)], 0
            )
        )
    return np.concatenate(out, 0)


def unpack(ref):
    sides = [ref[i * 256 : (i + 1) * 256, :] for i in range(4)]
    across = [ref[1024 + i * 128 : 1152 + i * 128, :] for i in range(2)]
    return [jnp.concatenate(sides[:2], 1), jnp.concatenate(sides[2:], 1)] + across


def mode_numbers():
    half = GRID // 2
    return np.concatenate([np.arange(half + 1), np.arange(1, half)])


def filter_table():
    k = jnp.asarray(mode_numbers(), jnp.float32)
    quarter = GRID // 4
    q = np.concatenate([np.arange(quarter + 1), np.arange(1, quarter)])
    weight = np.where((q == 0) | (q == quarter), 1.0, 2.0) / (GRID // 2)
    ky = jnp.asarray(np.stack([q, GRID // 2 - q], 1), jnp.float32)
    unit = 2.0 * math.pi / GRID
    squares = (
        (k * unit)[:, None, None, None] ** 2
        + (ky * unit)[None, :, :, None] ** 2
        + (k * unit)[None, None, None, :] ** 2
    )
    guarded = jnp.where(squares > 0, squares, 1.0)
    table = jnp.where(
        squares > 0, (1.0 - jnp.exp(-guarded / (4.0 * SCREEN * SCREEN))) / guarded, 0.0
    )
    table = table * jnp.asarray(weight, jnp.float32)[None, :, None, None]
    return table.reshape(GRID, GRID * GRID)


def rotate(c, s, cos, sin):
    return cos * c - sin * s, sin * c + cos * s


def forward(x):
    n = len(x)
    if n == 2:
        return [x[0] + x[1], x[0] - x[1]], {}
    ce, se = forward(x[0::2])
    co, so = forward(x[1::2])
    half, quarter = n // 2, n // 4
    c, s = [None] * (half + 1), {}
    c[0], c[half] = ce[0] + co[0], ce[0] - co[0]
    c[quarter], s[quarter] = ce[quarter], co[quarter]
    for q in range(1, quarter):
        if 8 * q == n:
            r = math.sqrt(0.5)
            a, b = (co[q] - so[q]) * r, (co[q] + so[q]) * r
        else:
            a, b = rotate(co[q], so[q], math.cos(2 * math.pi * q / n), math.sin(2 * math.pi * q / n))
        c[q], c[half - q] = ce[q] + a, ce[q] - a
        s[q], s[half - q] = b + se[q], b - se[q]
    return c, s


def backward(c, s):
    n = 2 * (len(c) - 1)
    if n == 2:
        return [c[0] + c[1], c[0] - c[1]]
    half, quarter = n // 2, n // 4
    ce, co, se, so = [None] * (quarter + 1), [None] * (quarter + 1), {}, {}
    ce[0], co[0] = c[0] + c[half], c[0] - c[half]
    ce[quarter], co[quarter] = c[quarter], s[quarter]
    for q in range(1, quarter):
        ce[q], a = c[q] + c[half - q], c[q] - c[half - q]
        b, se[q] = s[q] + s[half - q], s[q] - s[half - q]
        if 8 * q == n:
            r = math.sqrt(0.5)
            co[q], so[q] = (a + b) * r, (b - a) * r
        else:
            co[q], so[q] = rotate(a, b, math.cos(2 * math.pi * q / n), -math.sin(2 * math.pi * q / n))
    out = [None] * n
    out[0::2], out[1::2] = backward(ce, se), backward(co, so)
    return out


def twiddles(shape, q):
    odd = lax.broadcasted_iota(jnp.int32, shape, 1) >= shape[1] // 2
    angle = 2 * math.pi * q / GRID
    return jnp.where(odd, math.cos(angle), 1.0), jnp.where(odd, math.sin(angle), 0.0)


def halves(value):
    high = value.astype(jnp.bfloat16)
    return high, (value - high.astype(jnp.float32)).astype(jnp.bfloat16)


def along_z(tiles, double):
    high, rest = halves(jnp.concatenate(tiles, 0))
    out = jnp.dot(jnp.concatenate([high, rest], 1), double, preferred_element_type=jnp.float32)
    out = out[:, :LANES] + out[:, LANES:]
    step = tiles[0].shape[0]
    return [out[i * step : (i + 1) * step] for i in range(len(tiles))]


def along_x(value, double):
    length = value.shape[0]
    out = jnp.dot(double, jnp.concatenate(halves(value), 0), preferred_element_type=jnp.float32)
    return out[:length] + out[length:]


LANES = 128
PART = 4096
TABLE_PART = 512


def into_modes(densities):
    count = len(densities)
    quarter = count // 2
    c, s = forward(densities)
    for q in range(1, quarter):
        cos, sin = twiddles(densities[0].shape, q)
        c[q], s[q] = rotate(c[q], s[q], cos, sin)
    return c + [s[q] for q in range(1, quarter)]


def out_of_modes(values):
    quarter = len(values) // 2
    c, s = values[: quarter + 1], dict(enumerate(values[quarter + 1 :], 1))
    for q in range(1, quarter):
        cos, sin = twiddles(values[0].shape, q)
        c[q], s[q] = rotate(c[q], s[q], cos, -sin)
    return backward(c, s)


def filtered(tiles, table, z_forward, z_backward, x_forward, x_backward):
    value = along_x(jnp.concatenate(along_z(tiles, z_forward), 1), x_forward)
    value = along_x(value * table, x_backward)
    return along_z([value[:, i : i + LANES] for i in range(0, value.shape[1], LANES)], z_backward)


def columns(i):
    return slice(i * LANES, (i + 1) * LANES)


def exchange_kernel(orbital_ref, source_ref, filter_ref, *rest):
    constants, out_ref, work = rest
    length, cells = work.shape
    count = cells // LANES

    @pl.loop(0, length // 8)
    def _(block):
        rows = pl.ds(pl.multiple_of(block * 8, 8), 8)
        values = [
            orbital_ref[rows, columns(i)] * source_ref[0, rows, columns(i)] for i in range(count)
        ]
        for i, value in enumerate(into_modes(values)):
            work[rows, columns(i)] = value

    @pl.loop(0, cells // PART)
    def _(part):
        lanes = [pl.ds(pl.multiple_of(part * PART + i, LANES), LANES) for i in range(0, PART, LANES)]
        table = filter_ref[:, pl.ds(pl.multiple_of(part * PART, PART), PART)]
        tiles = filtered([work[:, lane] for lane in lanes], table, *unpack(constants))
        for lane, tile in zip(lanes, tiles):
            work[:, lane] = tile

    first = pl.program_id(0) == 0

    @pl.loop(0, length // 8)
    def _(block):
        rows = pl.ds(pl.multiple_of(block * 8, 8), 8)
        values = out_of_modes([work[rows, columns(i)] for i in range(count)])
        for i, value in enumerate(values):
            term = value * source_ref[0, rows, columns(i)] * -EXX_FRACTION
            out_ref[rows, columns(i)] = jnp.where(first, 0.0, out_ref[rows, columns(i)]) + term


def apply_exchange(orbital, sources):
    count, length, cells = sources.shape
    constants = jnp.asarray(matrices())
    whole = lambda shape: pl.BlockSpec(shape, lambda j: (0, 0))
    return pl.pallas_call(
        exchange_kernel,
        grid=(count,),
        out_shape=jax.ShapeDtypeStruct((length, cells), jnp.float32),
        in_specs=[
            whole((length, cells)),
            pl.BlockSpec((1, length, cells), lambda j: (j, 0, 0)),
            whole((length, cells)),
            whole(constants.shape),
        ],
        out_specs=whole((length, cells)),
        scratch_shapes=[pltpu.VMEM((length, cells), jnp.float32)],
        compiler_params=pltpu.CompilerParams(vmem_limit_bytes=32 * MIB),
        name="exchange",
    )(orbital, sources, filter_table(), constants)


GROUP = 8
COLUMNS = 4
LAG = 3
AHEAD = 4
TABLE_PART = 512


def filter_part(part, length):
    shape = (length, TABLE_PART)
    half, quarter = length // 2, length // 4
    lane = lax.broadcasted_iota(jnp.int32, shape, 1) + part * TABLE_PART

    def mode(index):
        return jnp.where(index > half, index - half, index)

    row = lane >> 7
    q = jnp.where(row > quarter, row - quarter, row)
    ky = jnp.where((lane & half * 2) == 0, q, half - q)
    edge = jnp.logical_or(q == 0, q == quarter)
    squares = jnp.zeros(shape, jnp.float32)
    for k in (mode(lax.broadcasted_iota(jnp.int32, shape, 0)), ky, mode(lane & (length - 1))):
        squares = squares + (k.astype(jnp.float32) * (2.0 * math.pi / length)) ** 2
    guarded = jnp.where(squares > 0, squares, 1.0)
    table = (1.0 - jnp.exp(-guarded / (4.0 * SCREEN * SCREEN))) / guarded
    scale = 1.0 / half
    return jnp.where(squares > 0, table, 0.0) * jnp.where(edge, scale, 2.0 * scale)


def fused_kernel(chips, row, x_ref, matrix_ref, out_ref, *rest):
    (constants, source, orbital, table, work, total, partial, copy_sem, swap_send, swap_recv, beside_send,
     beside_recv, local_sem, scatter_send, up_send, far_send, y_send, x_send, own_recv, y_recv, x_recv, d_recv,
     part_send, part_recv, back_send, back_recv, done_send, done_recv) = rest
    band, half = lax.axis_index("band"), lax.axis_index("fft")
    chip, core = band // 2, band % 2
    side, layer = chip % row, chip // row
    owned, planes, cells = x_ref.shape
    length = 2 * planes
    other = 1 - half
    groups, width = planes // GROUP, cells // COLUMNS
    share = groups // 2
    per_orbital = 2 * groups
    pieces = owned * per_orbital
    root, has_up, bottom = chip == 0, layer % 2 == 0, layer == 0
    across_band, beside_band = band + 2 - 4 * side, band + 1 - 2 * core
    to_y = {"band": band, "fft": other}
    to_core = {"band": beside_band, "fft": half}
    to_cross = {"band": beside_band, "fft": other}
    to_x = {"band": across_band, "fft": half}
    to_diagonal = {"band": across_band, "fft": other}
    to_up = {"band": band + 2 * row, "fft": half}
    to_far = {"band": band + 4 * row, "fft": half}
    to_down = {"band": band - 2 * row * jnp.where(layer == 2, 2, 1), "fft": half}
    own = 2 * side + half
    over_y, over_x, over_both = own + 1 - 2 * half, own + 2 - 4 * side, 3 - own

    barrier = pltpu.get_barrier_semaphore()

    def greet(target):
        pl.semaphore_signal(barrier, inc=1, device_id=target, device_id_type=MESH)

    greet(to_y)
    greet(to_core)
    greet(to_cross)
    greet(to_x)

    @pl.when(has_up)
    def _():
        greet(to_up)

    @pl.when(jnp.logical_not(bottom))
    def _():
        greet(to_down)

    @pl.when(bottom)
    def _():
        greet(to_diagonal)
        greet(to_far)

    pl.semaphore_wait(barrier, 5 + has_up.astype(jnp.int32) + bottom.astype(jnp.int32))

    def remote(src, dst, send, recv, target):
        return pltpu.make_async_remote_copy(
            src_ref=src, dst_ref=dst, send_sem=send, recv_sem=recv, device_id=target, device_id_type=MESH
        )

    def send(block, send_sem, recv_sem, target):
        remote(block, block, send_sem, recv_sem, target).start()

    def arrived(block, recv):
        remote(block, block, swap_send, recv, to_y).wait_recv()

    def sent(block, send_sem):
        remote(block, block, send_sem, swap_recv, to_y).wait_send()

    def group_rows(group):
        return pl.ds(pl.multiple_of(group * GROUP, GROUP), GROUP)

    def place(q, column):
        rows = group_rows((q % per_orbital) // 2)
        return q // per_orbital, q % 2, rows, pl.ds(pl.multiple_of(column * width, width), width)

    def piece(q, column):
        return source.at[place(q, column)]

    def outer(q, column):
        o, _, rows, lanes = place(q, column)
        return x_ref.at[o, rows, lanes]

    def local(q):
        return pltpu.make_async_copy(outer(q, own), piece(q, own), local_sem.at[q])

    def swap(k):
        rows, lanes = group_rows(k // 2), pl.ds(pl.multiple_of(k % 2 * (cells // 2), cells // 2), cells // 2)
        return remote(
            x_ref.at[other, rows, lanes], orbital.at[core, half, rows, lanes], swap_send, swap_recv, to_y
        )

    def scatter(q):
        @pl.when(jnp.logical_and(root, jnp.logical_and(q < pieces, q % 2 == half)))
        def _():
            for i, (column, target) in enumerate(
                ((over_x, to_x), (over_both, to_diagonal), (over_y, to_y))
            ):
                remote(
                    outer(q, column), piece(q, column), scatter_send.at[i], own_recv.at[q], target
                ).start()
            local(q).start()

    @pl.loop(0, AHEAD)
    def _(q):
        scatter(q)

    remote(x_ref.at[half], orbital.at[core, half], beside_send.at[0], beside_recv.at[0], to_core).start()
    keep = pltpu.make_async_copy(x_ref.at[half], orbital.at[core, half], copy_sem.at[0])
    keep.start()
    fetch = pltpu.make_async_copy(matrix_ref, constants, copy_sem.at[1])
    fetch.start()

    def within(q):
        return jnp.logical_and(q >= 0, q < pieces)

    def event(k):
        @pl.when(k < pieces)
        def _():
            block = piece(k, own)
            at_home = jnp.logical_and(root, k % 2 == half)

            @pl.when(at_home)
            def _():
                local(k).wait()

            @pl.when(jnp.logical_not(at_home))
            def _():
                arrived(block, own_recv.at[k])

            @pl.when(bottom)
            def _():
                send(block, far_send, own_recv.at[k], to_far)

            @pl.when(has_up)
            def _():
                send(block, up_send, own_recv.at[k], to_up)

            send(block, y_send, y_recv.at[k], to_y)
            send(block, x_send, x_recv.at[k], to_x)

        scatter(k + AHEAD)

        @pl.when(k < per_orbital)
        def _():
            swap(k).start()

        q = k - LAG

        @pl.when(within(q))
        def _():
            block = piece(q, over_y)
            arrived(block, y_recv.at[q])
            send(block, x_send, d_recv.at[q], to_x)
            arrived(piece(q, over_x), x_recv.at[q])

        r = k - 2 * LAG

        @pl.when(within(r))
        def _():
            arrived(piece(r, over_both), d_recv.at[r])

    count = cells // LANES
    ahead = per_orbital + 2 * LAG

    @pl.loop(0, ahead)
    def _(k):
        event(k)

        @pl.when(k < cells // TABLE_PART)
        def _():
            lanes = pl.ds(pl.multiple_of(k * TABLE_PART, TABLE_PART), TABLE_PART)
            table[:, lanes] = filter_part(k, length)

        @pl.when(k == ahead - 2)
        def _():
            arrived(orbital.at[core, other], swap_recv)
            send(orbital.at[core, other], beside_send.at[1], beside_recv.at[1], to_core)

    keep.wait()
    arrived(orbital.at[1 - core, half], beside_recv.at[0])
    arrived(orbital.at[1 - core, other], beside_recv.at[1])
    fetch.wait()

    def slot(index, number):
        @pl.when(index == 0)
        def _():
            event(ahead + number)

    @pl.loop(0, 2 * owned)
    def _(index):
        which, o = index % 2, index // 2

        @pl.when(which == 0)
        def _():
            @pl.loop(0, per_orbital)
            def _(block):
                @pl.when(block % 2 == 0)
                def _():
                    slot(index, block // 2)

                h, rows, to = block // groups, group_rows(block % groups), group_rows(block)

                @pl.loop(0, 2)
                def _(field):
                    values = [
                        orbital[field, h, rows, columns(i)] * source[o, h, rows, columns(i)]
                        for i in range(count)
                    ]
                    for i, value in enumerate(into_modes(values)):
                        work[2 * o + field, to, columns(i)] = value

        for part in range(cells // PART):
            slot(index, 4)
            slot(index, 5)
            lanes = [slice(part * PART + i, part * PART + i + LANES) for i in range(0, PART, LANES)]
            whole = table[:, part * PART : (part + 1) * PART]
            tiles = filtered([work[index, :, lane] for lane in lanes], whole, *unpack(constants))
            for lane, tile in zip(lanes, tiles):
                work[index, :, lane] = tile

        @pl.loop(0, per_orbital)
        def _(step):
            @pl.when(step % 4 == 0)
            def _():
                slot(index, 6 + step // 4)

            mine = step // groups
            n = step % groups
            h = jnp.where(n < share, other, half)
            holder = jnp.where(mine == 1, core, 1 - core)
            group = holder * share + n % share
            rows, to = group_rows(group), group_rows(h * groups + group)
            values = out_of_modes([work[index, to, columns(i)] for i in range(count)])
            for i, value in enumerate(values):
                term = value * source[o, h, rows, columns(i)]
                earlier = jnp.where(o == 0, 0.0, total[which, h, rows, columns(i)])
                total[which, h, rows, columns(i)] = earlier + term

            block = total.at[which, h, rows]
            last = o == owned - 1

            @pl.when(jnp.logical_and(last, mine == 0))
            def _():
                remote(block, partial.at[which, n], part_send, part_recv.at[which, n], to_core).start()

            @pl.when(jnp.logical_and(last, mine == 1))
            def _():
                arrived(partial.at[which, n], part_recv.at[which, n])
                for i in range(count):
                    total[which, h, rows, columns(i)] += partial[which, n, :, columns(i)]
                goal = out_ref.at[half, rows]

                @pl.when(n < share)
                def _():
                    remote(
                        block, goal, back_send, back_recv.at[core], {"band": 2 * chip + which, "fft": other}
                    ).start()

                @pl.when(jnp.logical_and(n >= share, which == core))
                def _():
                    pltpu.make_async_copy(block, goal, copy_sem.at[2]).start()

                @pl.when(jnp.logical_and(n >= share, which != core))
                def _():
                    remote(block, goal, done_send, done_recv, to_core).start()

    @pl.when(has_up)
    def _():
        sent(orbital.at[0, 0], up_send)

    @pl.when(bottom)
    def _():
        sent(orbital.at[0, 0], far_send)

    @pl.when(root)
    def _():
        for i in range(3):
            sent(orbital.at[0, 0, : planes // 2], scatter_send.at[i])

    sent(orbital.at[0, 0], y_send)
    sent(orbital.at[0], x_send)
    sent(orbital.at[0, 0], beside_send.at[0])
    sent(orbital.at[0, 0], beside_send.at[1])
    sent(orbital.at[0, 0], swap_send)
    sent(total.at[0], part_send)
    sent(total.at[0, 0], back_send)
    first, second = out_ref.at[other, : planes // 2], out_ref.at[other, planes // 2 :]
    sent(total.at[0, 0, : planes // 2], done_send)
    arrived(first, done_recv)
    pltpu.make_async_copy(total.at[0, 0, : planes // 2], first, copy_sem.at[2]).wait()
    arrived(first, back_recv.at[0])
    arrived(second, back_recv.at[1])


def two_halves(bands, row, orbitals):
    owned, planes, cells = orbitals.shape
    groups = planes // GROUP
    count = owned * 2 * groups
    dma = pltpu.SemaphoreType.DMA
    constants = jnp.asarray(matrices())
    grid = lambda *lead: pltpu.VMEM((*lead, planes, cells), jnp.float32)
    exchange = pl.pallas_call(
        functools.partial(fused_kernel, bands // 2, row),
        out_shape=jax.ShapeDtypeStruct(orbitals.shape, jnp.float32),
        in_specs=[pl.BlockSpec(memory_space=pl.ANY)] * 2,
        out_specs=pl.BlockSpec(memory_space=pl.ANY),
        scratch_shapes=[
            pltpu.VMEM(constants.shape, jnp.bfloat16),
            grid(owned, 2),
            grid(2, 2),
            pltpu.VMEM((2 * planes, cells), jnp.float32),
            pltpu.VMEM((2 * owned, 2 * planes, cells), jnp.float32),
            grid(2, 2),
            pltpu.VMEM((2, groups, GROUP, cells), jnp.float32),
        ]
        + [dma((3,)), dma, dma, dma((2,)), dma((2,)), dma((count,)), dma((3,))]
        + [dma] * 4
        + [dma((count,))] * 4
        + [dma, dma((2, groups)), dma, dma((2,)), dma, dma],
        compiler_params=pltpu.CompilerParams(
            collective_id=0, has_side_effects=True, vmem_limit_bytes=60 * MIB
        ),
        name="exchange",
    )(orbitals, constants)
    return -EXX_FRACTION * exchange


def many_parts(parts, orbitals):
    owned = orbitals.shape[0]
    place, band = lax.axis_index("fft"), lax.axis_index("band")
    fields = lax.all_gather(orbitals, "fft", axis=1, tiled=True)
    held = jnp.concatenate([jnp.where(band == r, fields, 0.0) for r in range(ROUNDS)], 0)
    sources = lax.psum(held, "band")
    groups = max(parts // owned, 1)
    share = sources.shape[0] // groups
    mine = lax.dynamic_slice_in_dim(sources, (place // owned) * share, share, 0)
    which = place % owned
    result = apply_exchange(lax.dynamic_index_in_dim(fields, which, 0, False), mine)
    placed = jnp.where(jnp.arange(owned)[:, None, None] == which, result[None], 0.0)
    return lax.psum_scatter(placed, "fft", scatter_dimension=1, tiled=True)


def solution(mesh):
    parts = mesh.shape["fft"]
    if parts == 2 and mesh.shape["band"] == 16:
        body = functools.partial(two_halves, mesh.shape["band"], 2)
    else:
        body = functools.partial(many_parts, parts)
    return jax.shard_map(
        body, mesh=mesh, in_specs=(P("band", "fft", None),), out_specs=P("band", "fft", None), check_vma=False
    )
```

```python
import functools
import math

import jax
import jax.numpy as jnp
import numpy as np
from jax import lax
from jax.experimental import pallas as pl
from jax.experimental.pallas import tpu as pltpu
from jax.sharding import PartitionSpec as P

GRID = 64
ROUNDS = 2
EXX_FRACTION = 0.25
SCREEN = 0.05
MESH = pl.DeviceIdType.MESH
MIB = 1024 * 1024


def real_modes(length):
    n = np.arange(length)
    rows = [np.cos(2 * np.pi * q * n / length) for q in range(length // 2 + 1)]
    rows += [np.sin(2 * np.pi * q * n / length) for q in range(1, length // 2)]
    matrix = np.array(rows)
    return matrix / np.sqrt((matrix**2).sum(1, keepdims=True))


def split(matrix):
    high = matrix.astype(jnp.bfloat16)
    return high, (matrix - high.astype(np.float64)).astype(jnp.bfloat16)


def matrices():
    modes = real_modes(GRID)
    z_forward = np.kron(np.array([[1.0, 1.0], [1.0, -1.0]]) / np.sqrt(2.0), modes.T)
    out = []
    for matrix in (z_forward, z_forward.T):
        high, low = split(matrix)
        out += [np.concatenate([high, high], 0), np.concatenate([low, np.zeros_like(low)], 0)]
    for matrix in (modes, modes.T):
        high, low = split(matrix)
        out.append(
            np.concatenate(
                [np.concatenate([high, high], 1), np.concatenate([low, np.zeros_like(low)], 1)], 0
            )
        )
    return np.concatenate(out, 0)


def unpack(ref):
    sides = [ref[i * 256 : (i + 1) * 256, :] for i in range(4)]
    across = [ref[1024 + i * 128 : 1152 + i * 128, :] for i in range(2)]
    return [jnp.concatenate(sides[:2], 1), jnp.concatenate(sides[2:], 1)] + across


def mode_numbers():
    half = GRID // 2
    return np.concatenate([np.arange(half + 1), np.arange(1, half)])


def filter_table():
    k = jnp.asarray(mode_numbers(), jnp.float32)
    quarter = GRID // 4
    q = np.concatenate([np.arange(quarter + 1), np.arange(1, quarter)])
    weight = np.where((q == 0) | (q == quarter), 1.0, 2.0) / (GRID // 2)
    ky = jnp.asarray(np.stack([q, GRID // 2 - q], 1), jnp.float32)
    unit = 2.0 * math.pi / GRID
    squares = (
        (k * unit)[:, None, None, None] ** 2
        + (ky * unit)[None, :, :, None] ** 2
        + (k * unit)[None, None, None, :] ** 2
    )
    guarded = jnp.where(squares > 0, squares, 1.0)
    table = jnp.where(
        squares > 0, (1.0 - jnp.exp(-guarded / (4.0 * SCREEN * SCREEN))) / guarded, 0.0
    )
    table = table * jnp.asarray(weight, jnp.float32)[None, :, None, None]
    return table.reshape(GRID, GRID * GRID)


def rotate(c, s, cos, sin):
    return cos * c - sin * s, sin * c + cos * s


def forward(x):
    n = len(x)
    if n == 2:
        return [x[0] + x[1], x[0] - x[1]], {}
    ce, se = forward(x[0::2])
    co, so = forward(x[1::2])
    half, quarter = n // 2, n // 4
    c, s = [None] * (half + 1), {}
    c[0], c[half] = ce[0] + co[0], ce[0] - co[0]
    c[quarter], s[quarter] = ce[quarter], co[quarter]
    for q in range(1, quarter):
        if 8 * q == n:
            r = math.sqrt(0.5)
            a, b = (co[q] - so[q]) * r, (co[q] + so[q]) * r
        else:
            a, b = rotate(co[q], so[q], math.cos(2 * math.pi * q / n), math.sin(2 * math.pi * q / n))
        c[q], c[half - q] = ce[q] + a, ce[q] - a
        s[q], s[half - q] = b + se[q], b - se[q]
    return c, s


def backward(c, s):
    n = 2 * (len(c) - 1)
    if n == 2:
        return [c[0] + c[1], c[0] - c[1]]
    half, quarter = n // 2, n // 4
    ce, co, se, so = [None] * (quarter + 1), [None] * (quarter + 1), {}, {}
    ce[0], co[0] = c[0] + c[half], c[0] - c[half]
    ce[quarter], co[quarter] = c[quarter], s[quarter]
    for q in range(1, quarter):
        ce[q], a = c[q] + c[half - q], c[q] - c[half - q]
        b, se[q] = s[q] + s[half - q], s[q] - s[half - q]
        if 8 * q == n:
            r = math.sqrt(0.5)
            co[q], so[q] = (a + b) * r, (b - a) * r
        else:
            co[q], so[q] = rotate(a, b, math.cos(2 * math.pi * q / n), -math.sin(2 * math.pi * q / n))
    out = [None] * n
    out[0::2], out[1::2] = backward(ce, se), backward(co, so)
    return out


def twiddles(shape, q):
    odd = lax.broadcasted_iota(jnp.int32, shape, 1) >= shape[1] // 2
    angle = 2 * math.pi * q / GRID
    return jnp.where(odd, math.cos(angle), 1.0), jnp.where(odd, math.sin(angle), 0.0)


def halves(value):
    high = value.astype(jnp.bfloat16)
    return high, (value - high.astype(jnp.float32)).astype(jnp.bfloat16)


def along_z(tiles, double):
    high, rest = halves(jnp.concatenate(tiles, 0))
    out = jnp.dot(jnp.concatenate([high, rest], 1), double, preferred_element_type=jnp.float32)
    out = out[:, :LANES] + out[:, LANES:]
    step = tiles[0].shape[0]
    return [out[i * step : (i + 1) * step] for i in range(len(tiles))]


def along_x(value, double):
    length = value.shape[0]
    out = jnp.dot(double, jnp.concatenate(halves(value), 0), preferred_element_type=jnp.float32)
    return out[:length] + out[length:]


LANES = 128
PART = 4096
TABLE_PART = 512


def into_modes(densities):
    count = len(densities)
    quarter = count // 2
    c, s = forward(densities)
    for q in range(1, quarter):
        cos, sin = twiddles(densities[0].shape, q)
        c[q], s[q] = rotate(c[q], s[q], cos, sin)
    return c + [s[q] for q in range(1, quarter)]


def out_of_modes(values):
    quarter = len(values) // 2
    c, s = values[: quarter + 1], dict(enumerate(values[quarter + 1 :], 1))
    for q in range(1, quarter):
        cos, sin = twiddles(values[0].shape, q)
        c[q], s[q] = rotate(c[q], s[q], cos, -sin)
    return backward(c, s)


def filtered(tiles, table, z_forward, z_backward, x_forward, x_backward):
    value = along_x(jnp.concatenate(along_z(tiles, z_forward), 1), x_forward)
    value = along_x(value * table, x_backward)
    return along_z([value[:, i : i + LANES] for i in range(0, value.shape[1], LANES)], z_backward)


def columns(i):
    return slice(i * LANES, (i + 1) * LANES)


def exchange_kernel(orbital_ref, source_ref, filter_ref, *rest):
    constants, out_ref, work = rest
    length, cells = work.shape
    count = cells // LANES

    @pl.loop(0, length // 8)
    def _(block):
        rows = pl.ds(pl.multiple_of(block * 8, 8), 8)
        values = [
            orbital_ref[rows, columns(i)] * source_ref[0, rows, columns(i)] for i in range(count)
        ]
        for i, value in enumerate(into_modes(values)):
            work[rows, columns(i)] = value

    @pl.loop(0, cells // PART)
    def _(part):
        lanes = [pl.ds(pl.multiple_of(part * PART + i, LANES), LANES) for i in range(0, PART, LANES)]
        table = filter_ref[:, pl.ds(pl.multiple_of(part * PART, PART), PART)]
        tiles = filtered([work[:, lane] for lane in lanes], table, *unpack(constants))
        for lane, tile in zip(lanes, tiles):
            work[:, lane] = tile

    first = pl.program_id(0) == 0

    @pl.loop(0, length // 8)
    def _(block):
        rows = pl.ds(pl.multiple_of(block * 8, 8), 8)
        values = out_of_modes([work[rows, columns(i)] for i in range(count)])
        for i, value in enumerate(values):
            term = value * source_ref[0, rows, columns(i)] * -EXX_FRACTION
            out_ref[rows, columns(i)] = jnp.where(first, 0.0, out_ref[rows, columns(i)]) + term


def apply_exchange(orbital, sources):
    count, length, cells = sources.shape
    constants = jnp.asarray(matrices())
    whole = lambda shape: pl.BlockSpec(shape, lambda j: (0, 0))
    return pl.pallas_call(
        exchange_kernel,
        grid=(count,),
        out_shape=jax.ShapeDtypeStruct((length, cells), jnp.float32),
        in_specs=[
            whole((length, cells)),
            pl.BlockSpec((1, length, cells), lambda j: (j, 0, 0)),
            whole((length, cells)),
            whole(constants.shape),
        ],
        out_specs=whole((length, cells)),
        scratch_shapes=[pltpu.VMEM((length, cells), jnp.float32)],
        compiler_params=pltpu.CompilerParams(vmem_limit_bytes=32 * MIB),
        name="exchange",
    )(orbital, sources, filter_table(), constants)


GROUP = 8
COLUMNS = 4
LAG = 4
AHEAD = 4
TABLE_PART = 512


def filter_part(part, length):
    shape = (length, TABLE_PART)
    half, quarter = length // 2, length // 4
    lane = lax.broadcasted_iota(jnp.int32, shape, 1) + part * TABLE_PART

    def mode(index):
        return jnp.where(index > half, index - half, index)

    row = lane >> 7
    q = jnp.where(row > quarter, row - quarter, row)
    ky = jnp.where((lane & half * 2) == 0, q, half - q)
    edge = jnp.logical_or(q == 0, q == quarter)
    squares = jnp.zeros(shape, jnp.float32)
    for k in (mode(lax.broadcasted_iota(jnp.int32, shape, 0)), ky, mode(lane & (length - 1))):
        squares = squares + (k.astype(jnp.float32) * (2.0 * math.pi / length)) ** 2
    guarded = jnp.where(squares > 0, squares, 1.0)
    table = (1.0 - jnp.exp(-guarded / (4.0 * SCREEN * SCREEN))) / guarded
    scale = 1.0 / half
    return jnp.where(squares > 0, table, 0.0) * jnp.where(edge, scale, 2.0 * scale)


def fused_kernel(chips, row, x_ref, matrix_ref, out_ref, *rest):
    (constants, source, orbital, table, work, total, partial, copy_sem, swap_send, swap_recv, beside_send,
     beside_recv, local_sem, scatter_send, up_send, far_send, y_send, x_send, own_recv, y_recv, x_recv, d_recv,
     part_send, part_recv, back_send, back_recv, done_send, done_recv) = rest
    band, half = lax.axis_index("band"), lax.axis_index("fft")
    chip, core = band // 2, band % 2
    side, layer = chip % row, chip // row
    owned, planes, cells = x_ref.shape
    length = 2 * planes
    other = 1 - half
    groups, width = planes // GROUP, cells // COLUMNS
    share = groups // 2
    per_orbital = 2 * groups
    pieces = owned * per_orbital
    root, has_up, bottom = chip == 0, layer % 2 == 0, layer == 0
    across_band, beside_band = band + 2 - 4 * side, band + 1 - 2 * core
    to_y = {"band": band, "fft": other}
    to_core = {"band": beside_band, "fft": half}
    to_cross = {"band": beside_band, "fft": other}
    to_x = {"band": across_band, "fft": half}
    to_diagonal = {"band": across_band, "fft": other}
    to_up = {"band": band + 2 * row, "fft": half}
    to_far = {"band": band + 4 * row, "fft": half}
    to_down = {"band": band - 2 * row * jnp.where(layer == 2, 2, 1), "fft": half}
    own = 2 * side + half
    over_y, over_x, over_both = own + 1 - 2 * half, own + 2 - 4 * side, 3 - own

    barrier = pltpu.get_barrier_semaphore()

    def greet(target):
        pl.semaphore_signal(barrier, inc=1, device_id=target, device_id_type=MESH)

    greet(to_y)
    greet(to_core)
    greet(to_cross)
    greet(to_x)

    @pl.when(has_up)
    def _():
        greet(to_up)

    @pl.when(jnp.logical_not(bottom))
    def _():
        greet(to_down)

    @pl.when(bottom)
    def _():
        greet(to_diagonal)
        greet(to_far)

    pl.semaphore_wait(barrier, 5 + has_up.astype(jnp.int32) + bottom.astype(jnp.int32))

    def remote(src, dst, send, recv, target):
        return pltpu.make_async_remote_copy(
            src_ref=src, dst_ref=dst, send_sem=send, recv_sem=recv, device_id=target, device_id_type=MESH
        )

    def send(block, send_sem, recv_sem, target):
        remote(block, block, send_sem, recv_sem, target).start()

    def arrived(block, recv):
        remote(block, block, swap_send, recv, to_y).wait_recv()

    def sent(block, send_sem):
        remote(block, block, send_sem, swap_recv, to_y).wait_send()

    def group_rows(group):
        return pl.ds(pl.multiple_of(group * GROUP, GROUP), GROUP)

    def place(q, column):
        rows = group_rows((q % per_orbital) // 2)
        return q // per_orbital, q % 2, rows, pl.ds(pl.multiple_of(column * width, width), width)

    def piece(q, column):
        return source.at[place(q, column)]

    def outer(q, column):
        o, _, rows, lanes = place(q, column)
        return x_ref.at[o, rows, lanes]

    def local(q):
        return pltpu.make_async_copy(outer(q, own), piece(q, own), local_sem.at[q])

    def swap(k):
        rows, lanes = group_rows(k // 2), pl.ds(pl.multiple_of(k % 2 * (cells // 2), cells // 2), cells // 2)
        return remote(
            x_ref.at[other, rows, lanes], orbital.at[core, half, rows, lanes], swap_send, swap_recv, to_y
        )

    def scatter(q):
        @pl.when(jnp.logical_and(root, jnp.logical_and(q < pieces, q % 2 == half)))
        def _():
            for i, (column, target) in enumerate(
                ((over_x, to_x), (over_both, to_diagonal), (over_y, to_y))
            ):
                remote(
                    outer(q, column), piece(q, column), scatter_send.at[i], own_recv.at[q], target
                ).start()
            local(q).start()

    @pl.loop(0, AHEAD)
    def _(q):
        scatter(q)

    remote(x_ref.at[half], orbital.at[core, half], beside_send.at[0], beside_recv.at[0], to_core).start()
    keep = pltpu.make_async_copy(x_ref.at[half], orbital.at[core, half], copy_sem.at[0])
    keep.start()
    fetch = pltpu.make_async_copy(matrix_ref, constants, copy_sem.at[1])
    fetch.start()

    def within(q):
        return jnp.logical_and(q >= 0, q < pieces)

    def event(k):
        @pl.when(k < pieces)
        def _():
            block = piece(k, own)
            at_home = jnp.logical_and(root, k % 2 == half)

            @pl.when(at_home)
            def _():
                local(k).wait()

            @pl.when(jnp.logical_not(at_home))
            def _():
                arrived(block, own_recv.at[k])

            @pl.when(bottom)
            def _():
                send(block, far_send, own_recv.at[k], to_far)

            @pl.when(has_up)
            def _():
                send(block, up_send, own_recv.at[k], to_up)

            send(block, y_send, y_recv.at[k], to_y)
            send(block, x_send, x_recv.at[k], to_x)

        scatter(k + AHEAD)

        @pl.when(k < per_orbital)
        def _():
            swap(k).start()

        q = k - LAG

        @pl.when(within(q))
        def _():
            block = piece(q, over_y)
            arrived(block, y_recv.at[q])
            send(block, x_send, d_recv.at[q], to_x)
            arrived(piece(q, over_x), x_recv.at[q])

        r = k - 2 * LAG

        @pl.when(within(r))
        def _():
            arrived(piece(r, over_both), d_recv.at[r])

    count = cells // LANES
    ahead = per_orbital + 2 * LAG

    @pl.loop(0, ahead)
    def _(k):
        event(k)

        @pl.when(k < cells // TABLE_PART)
        def _():
            lanes = pl.ds(pl.multiple_of(k * TABLE_PART, TABLE_PART), TABLE_PART)
            table[:, lanes] = filter_part(k, length)

        @pl.when(k == ahead - 2)
        def _():
            arrived(orbital.at[core, other], swap_recv)
            send(orbital.at[core, other], beside_send.at[1], beside_recv.at[1], to_core)

    keep.wait()
    arrived(orbital.at[1 - core, half], beside_recv.at[0])
    arrived(orbital.at[1 - core, other], beside_recv.at[1])
    fetch.wait()

    def slot(index, number):
        @pl.when(index == 0)
        def _():
            event(ahead + number)

    @pl.loop(0, 2 * owned)
    def _(index):
        which, o = index % 2, index // 2

        @pl.when(which == 0)
        def _():
            @pl.loop(0, per_orbital)
            def _(block):
                @pl.when(block % 2 == 0)
                def _():
                    slot(index, block // 2)

                h, rows, to = block // groups, group_rows(block % groups), group_rows(block)

                @pl.loop(0, 2)
                def _(field):
                    values = [
                        orbital[field, h, rows, columns(i)] * source[o, h, rows, columns(i)]
                        for i in range(count)
                    ]
                    for i, value in enumerate(into_modes(values)):
                        work[2 * o + field, to, columns(i)] = value

        for part in range(cells // PART):
            slot(index, 4)
            slot(index, 5)
            lanes = [slice(part * PART + i, part * PART + i + LANES) for i in range(0, PART, LANES)]
            whole = table[:, part * PART : (part + 1) * PART]
            tiles = filtered([work[index, :, lane] for lane in lanes], whole, *unpack(constants))
            for lane, tile in zip(lanes, tiles):
                work[index, :, lane] = tile

        @pl.loop(0, per_orbital)
        def _(step):
            @pl.when(step % 4 == 0)
            def _():
                slot(index, 6 + step // 4)

            mine = step // groups
            n = step % groups
            h = jnp.where(n < share, other, half)
            holder = jnp.where(mine == 1, core, 1 - core)
            group = holder * share + n % share
            rows, to = group_rows(group), group_rows(h * groups + group)
            values = out_of_modes([work[index, to, columns(i)] for i in range(count)])
            for i, value in enumerate(values):
                term = value * source[o, h, rows, columns(i)]
                earlier = jnp.where(o == 0, 0.0, total[which, h, rows, columns(i)])
                total[which, h, rows, columns(i)] = earlier + term

            block = total.at[which, h, rows]
            last = o == owned - 1

            @pl.when(jnp.logical_and(last, mine == 0))
            def _():
                remote(block, partial.at[which, n], part_send, part_recv.at[which, n], to_core).start()

            @pl.when(jnp.logical_and(last, mine == 1))
            def _():
                arrived(partial.at[which, n], part_recv.at[which, n])
                for i in range(count):
                    total[which, h, rows, columns(i)] += partial[which, n, :, columns(i)]
                goal = out_ref.at[half, rows]

                @pl.when(n < share)
                def _():
                    remote(
                        block, goal, back_send, back_recv.at[core], {"band": 2 * chip + which, "fft": other}
                    ).start()

                @pl.when(jnp.logical_and(n >= share, which == core))
                def _():
                    pltpu.make_async_copy(block, goal, copy_sem.at[2]).start()

                @pl.when(jnp.logical_and(n >= share, which != core))
                def _():
                    remote(block, goal, done_send, done_recv, to_core).start()

    @pl.when(has_up)
    def _():
        sent(orbital.at[0, 0], up_send)

    @pl.when(bottom)
    def _():
        sent(orbital.at[0, 0], far_send)

    @pl.when(root)
    def _():
        for i in range(3):
            sent(orbital.at[0, 0, : planes // 2], scatter_send.at[i])

    sent(orbital.at[0, 0], y_send)
    sent(orbital.at[0], x_send)
    sent(orbital.at[0, 0], beside_send.at[0])
    sent(orbital.at[0, 0], beside_send.at[1])
    sent(orbital.at[0, 0], swap_send)
    sent(total.at[0], part_send)
    sent(total.at[0, 0], back_send)
    first, second = out_ref.at[other, : planes // 2], out_ref.at[other, planes // 2 :]
    sent(total.at[0, 0, : planes // 2], done_send)
    arrived(first, done_recv)
    pltpu.make_async_copy(total.at[0, 0, : planes // 2], first, copy_sem.at[2]).wait()
    arrived(first, back_recv.at[0])
    arrived(second, back_recv.at[1])


def two_halves(bands, row, orbitals):
    owned, planes, cells = orbitals.shape
    groups = planes // GROUP
    count = owned * 2 * groups
    dma = pltpu.SemaphoreType.DMA
    constants = jnp.asarray(matrices())
    grid = lambda *lead: pltpu.VMEM((*lead, planes, cells), jnp.float32)
    exchange = pl.pallas_call(
        functools.partial(fused_kernel, bands // 2, row),
        out_shape=jax.ShapeDtypeStruct(orbitals.shape, jnp.float32),
        in_specs=[pl.BlockSpec(memory_space=pl.ANY)] * 2,
        out_specs=pl.BlockSpec(memory_space=pl.ANY),
        scratch_shapes=[
            pltpu.VMEM(constants.shape, jnp.bfloat16),
            grid(owned, 2),
            grid(2, 2),
            pltpu.VMEM((2 * planes, cells), jnp.float32),
            pltpu.VMEM((2 * owned, 2 * planes, cells), jnp.float32),
            grid(2, 2),
            pltpu.VMEM((2, groups, GROUP, cells), jnp.float32),
        ]
        + [dma((3,)), dma, dma, dma((2,)), dma((2,)), dma((count,)), dma((3,))]
        + [dma] * 4
        + [dma((count,))] * 4
        + [dma, dma((2, groups)), dma, dma((2,)), dma, dma],
        compiler_params=pltpu.CompilerParams(
            collective_id=0, has_side_effects=True, vmem_limit_bytes=60 * MIB
        ),
        name="exchange",
    )(orbitals, constants)
    return -EXX_FRACTION * exchange


def many_parts(parts, orbitals):
    owned = orbitals.shape[0]
    place, band = lax.axis_index("fft"), lax.axis_index("band")
    fields = lax.all_gather(orbitals, "fft", axis=1, tiled=True)
    held = jnp.concatenate([jnp.where(band == r, fields, 0.0) for r in range(ROUNDS)], 0)
    sources = lax.psum(held, "band")
    groups = max(parts // owned, 1)
    share = sources.shape[0] // groups
    mine = lax.dynamic_slice_in_dim(sources, (place // owned) * share, share, 0)
    which = place % owned
    result = apply_exchange(lax.dynamic_index_in_dim(fields, which, 0, False), mine)
    placed = jnp.where(jnp.arange(owned)[:, None, None] == which, result[None], 0.0)
    return lax.psum_scatter(placed, "fft", scatter_dimension=1, tiled=True)


def solution(mesh):
    parts = mesh.shape["fft"]
    if parts == 2 and mesh.shape["band"] == 16:
        body = functools.partial(two_halves, mesh.shape["band"], 2)
    else:
        body = functools.partial(many_parts, parts)
    return jax.shard_map(
        body, mesh=mesh, in_specs=(P("band", "fft", None),), out_specs=P("band", "fft", None), check_vma=False
    )
```
